32 devices in a mesh: wide: 8 (over z, x), narrow: 4 (over y, core).
Axes of the slice: x: 2, y: 2, z: 4, core: 2. Of those that a mesh axis runs over, the one named last changes fastest.
Arguments:
- expression: bfloat16 [32768, 7000], P(('wide', 'narrow')), may hold values from -8 to 8
- epsilon: bfloat16 [32768, 100], P(('wide', 'narrow')), may hold values from -5 to 5
- params: bfloat16 [12734464], P(('wide', 'narrow')), as said below
- panels: int32 [4, 7000], replicated, may hold values 0 or 1
- labels: int32 [32768], P(('wide', 'narrow')), may hold values from 0 to 3, as said below
Outputs:
- rebuilt: bfloat16 [32768, 7000], P(('wide', 'narrow'))
- offset: float32 [4, 100], P(None, 'narrow')
- total_loss: float32 [], replicated
- grad_cells: bfloat16 [32768, 7000], P(('wide', 'narrow'))
- grad_params: float32 [12734464], P(('wide', 'narrow'))
- divergence: float32 [], replicated
The draws below stay inside these ranges and needn't reach their ends.
Inputs may be any that keep to these rules, and one draw needn't show every extreme that they name: labels of the first 4 cells are 0, 1, ... in order, so every condition has a cell; the others are even over conditions. `params`: packed as described; gains near 1.
All inputs are finite; a program needn't handle non-finite values.
Results may differ from the reference program's by a relative error of at most 0.0065.
Values may be sent and summed in bfloat16 or wider, within the bound.
A program may use at most 384 MiB of HBM per device.

```python
import math
import jax
import jax.numpy as jnp
from jax import lax

G = 7000
H = 800
L = 100
NC = 4
CELLS = 32768
FLAT = 12734464


def draw_params(key, part):
    position = jnp.arange(FLAT)
    values = jax.random.normal(key, (FLAT,), jnp.float32)
    segments = [(G * H, 0.0, G ** (-0.5)), (H, 1.0, 0.1), (H, 0.0, 0.1), (H * H, 0.0, H ** (-0.5)), (H, 1.0, 0.1), (H, 0.0, 0.1), (H * 2 * L, 0.0, H ** (-0.5)), (2 * L, 0.0, 0.2), (L * H, 0.0, L ** (-0.5)), (H, 1.0, 0.1), (H, 0.0, 0.1), (H * H, 0.0, H ** (-0.5)), (H, 1.0, 0.1), (H, 0.0, 0.1), (H * G, 0.0, H ** (-0.5)), (G, 0.0, 0.5)]
    scales = jnp.full((FLAT,), 0.1, jnp.float32)
    bases = jnp.zeros((FLAT,), jnp.float32)
    cursor = 0
    for length, base_value, scale_value in segments:
        inside = (position >= cursor) & (position < cursor + length)
        scales = jnp.where(inside, scale_value, scales)
        bases = jnp.where(inside, base_value, bases)
        cursor = cursor + length
    return (bases + scales * values).astype(jnp.bfloat16)


def cell_conditions(key):
    drawn = jax.random.randint(jax.random.fold_in(key, 17), (CELLS,), 0, NC, jnp.int32)
    position = jnp.arange(CELLS, dtype=jnp.int32)
    return jnp.where(position < NC, position, drawn).astype(jnp.int32)


def draw_labels(key, part):
    return cell_conditions(key)


def draw_expression(key, part):
    conditions = cell_conditions(key)
    fraction = jnp.arange(CELLS, dtype=jnp.float32) / CELLS
    own_part = jax.random.normal(jax.random.fold_in(key, 29), (CELLS, G), jnp.float32)
    study_part = jax.random.normal(jax.random.fold_in(key, 31), (NC, G), jnp.float32)
    row_scale = 0.5 * jnp.exp(1.0986123 * fraction)
    values = row_scale[:, None] * (own_part + jnp.take(study_part, conditions, axis=0))
    return jnp.clip(values, -8.0, 8.0).astype(jnp.bfloat16)


def with_ends(result, stream_key, least, largest):
    dims = result.shape
    spot = [jax.random.randint(jax.random.fold_in(stream_key, axis), (), 0, dims[axis]) for axis in range(len(dims))]
    result = result.at[tuple(spot)].set(least)
    longest = dims.index(max(dims))
    spot[longest] = (spot[longest] + 1) % dims[longest]
    return result.at[tuple(spot)].set(largest)


def block_levels(stream_key, shape, cuts, low, largest):
    gain, own = 1.0, jax.random.fold_in(stream_key, 6)
    for dim, shards_of in cuts:
        heights = jnp.exp(jax.random.uniform(jax.random.fold_in(own, dim), (shards_of,), jnp.float32, low / len(cuts), largest / len(cuts)))
        gain = gain * jnp.repeat(heights, shape[dim] // shards_of).reshape([-1 if axis == dim else 1 for axis in range(len(shape))])
    return gain


def gaussian(rng, dims, width, bound, shards=(), kind=jnp.bfloat16):
    entries = width * jax.random.normal(rng, dims, jnp.float32)
    if shards:
        entries = entries * block_levels(rng, dims, shards, -0.22, 0.18)
    return jnp.clip(entries, -bound, bound).astype(kind)


def setup_inputs(seed: int = 0) -> dict:
    splits = jax.random.split(jax.random.key(seed), 6)
    expression = draw_expression(jax.random.fold_in(splits[5], 71), 0)
    epsilon = gaussian(splits[1], (CELLS, L), 1.0, 5.0, ((0, 32),))
    params = draw_params(jax.random.fold_in(splits[5], 71), 0)
    panels = with_ends((jax.random.randint(splits[3], (NC, G), 0, 4) < 3).astype(jnp.int32), jax.random.fold_in(splits[3], 1), 0, 1)
    labels = draw_labels(jax.random.fold_in(splits[5], 71), 0)
    return {"expression": expression, "epsilon": epsilon, "params": params, "panels": panels, "labels": labels}


EPSILON_NORM = 1e-05
KL_WEIGHT = 5e-05

@jax.custom_vjp
def low(v):
    return lax.optimization_barrier(v.astype(jnp.bfloat16)).astype(jnp.float32)

@jax.custom_vjp
def low_back(v):
    return v

def low_keep(v):
    return (low(v), None)

def low_pass(kept, grad):
    return (grad,)

def back_keep(v):
    return (v, None)

def back_low(kept, grad):
    return (low(grad),)
low.defvjp(low_keep, low_pass)
low_back.defvjp(back_keep, back_low)

def layer_shapes():
    return [(G, H), (H,), (H,), (H, H), (H,), (H,), (H, 2 * L), (2 * L,), (L, H), (H,), (H,), (H, H), (H,), (H,), (H, G), (G,)]

def unpack(packed):
    pieces = []
    cursor = 0
    for layer_shape in layer_shapes():
        length = math.prod(layer_shape)
        pieces.append(packed[cursor:cursor + length].reshape(layer_shape))
        cursor = cursor + length
    return pieces

def matmul(left, right):
    return jnp.dot(left, right, precision=lax.Precision.HIGHEST, preferred_element_type=jnp.float32)

def batch_norm(values, gain_vec, shift_vec):
    centre = lax.optimization_barrier(jnp.mean(values, axis=0))
    spread = lax.optimization_barrier(jnp.mean(values * values, axis=0)) - centre * centre
    return gain_vec * ((values - centre) * lax.rsqrt(spread + EPSILON_NORM)) + shift_vec

def objective(packed, inputs, jitter, onehot, gene_mask):
    weights = unpack(packed)
    linear_one = low_back(matmul(inputs, weights[0]))
    active_one = low(jax.nn.silu(batch_norm(linear_one, weights[1], weights[2])))
    linear_two = low_back(matmul(active_one, weights[3]))
    active_two = low(jax.nn.silu(batch_norm(linear_two, weights[4], weights[5])))
    head_out = low_back(low(matmul(active_two, weights[6]) + weights[7]))
    latent_mean = head_out[:, :L]
    logvar = head_out[:, L:]
    counts = lax.optimization_barrier(jnp.sum(onehot, axis=0))
    offset = matmul(onehot.T, latent_mean) / counts[:, None] - lax.optimization_barrier(jnp.sum(latent_mean, axis=0)) / CELLS
    latent = low_back(low(latent_mean + jnp.exp(0.5 * logvar) * jitter - matmul(onehot, offset)))
    linear_three = low_back(matmul(latent, weights[8]))
    active_three = low(jax.nn.silu(batch_norm(linear_three, weights[9], weights[10])))
    linear_four = low_back(matmul(active_three, weights[11]))
    active_four = low(jax.nn.silu(batch_norm(linear_four, weights[12], weights[13])))
    output = low_back(matmul(active_four, weights[14]) + weights[15])
    rebuilt = jax.nn.softplus(output)
    residue = rebuilt - inputs
    masked_mean = jnp.sum(gene_mask * residue * residue) / jnp.sum(gene_mask)
    diverge = -0.5 * jnp.sum(1.0 + logvar - latent_mean * latent_mean - jnp.exp(logvar)) / CELLS
    total_loss = masked_mean + KL_WEIGHT * diverge
    return (total_loss, (rebuilt, offset, diverge))

def reference(expression, epsilon, params, panels, labels):
    inputs = expression.astype(jnp.float32)
    jitter = epsilon.astype(jnp.float32)
    onehot = (labels[:, None] == jnp.arange(NC, dtype=jnp.int32)[None, :]).astype(jnp.float32)
    gene_mask = matmul(onehot, panels.astype(jnp.float32))

    def wrapped(packed, cells_in):
        return objective(packed, cells_in, jitter, onehot, gene_mask)
    total_loss, pullback, extras = jax.vjp(wrapped, params.astype(jnp.float32), inputs, has_aux=True)
    grad_params, grad_cells = pullback(jnp.ones((), jnp.float32))
    rebuilt, offset, diverge = extras
    return (rebuilt.astype(jnp.bfloat16), offset, total_loss, grad_cells.astype(jnp.bfloat16), grad_params, diverge)
```

```python
import functools

import jax
import jax.numpy as jnp
from jax import lax
from jax.experimental import pallas as pl
from jax.experimental.pallas import tpu as pltpu
from jax.sharding import PartitionSpec as P

G, H, L, NC = 7000, 800, 100, 4
EPSILON_NORM = 1e-05
KL_WEIGHT = 5e-05
F32, BF16 = jnp.float32, jnp.bfloat16
TN = ((0,), (0,))
NN = ((1,), (0,))
NT = ((1,), (1,))
HX = 816


def mm(left, right, dims):
    return lax.dot_general(left, right, (dims, ((), ())), preferred_element_type=F32)


def params_of(limit=56):
    return pltpu.CompilerParams(dimension_semantics=("arbitrary",), vmem_limit_bytes=limit * 2**20)


def output_kernel(part, block, scale, d_ref, a_ref, x_ref, p_ref, h_ref, reb, direct, dg, g_ref, sq, dscr):
    i = pl.program_id(0)
    cells = a_ref.shape[1]

    @pl.when(i == 0)
    def _():
        g_ref[...] = jnp.zeros_like(g_ref)
        sq[...] = jnp.zeros_like(sq)

    lim = G - i * block
    for j in range(block // part):
        r = slice(j * part, (j + 1) * part)
        inside = lax.broadcasted_iota(jnp.int32, (part, 1), 0) + j * part < lim
        w = d_ref[:, r]
        out = mm(w, a_ref[...], TN)
        mask = jnp.where(inside, mm(p_ref[:, r], h_ref[...], TN), 0.0)
        t = jnp.exp(-jnp.abs(out))
        one = 1.0 + t
        soft = jnp.maximum(out, 0.0) + jnp.where(t < 1e-3, t - 0.5 * t * t, jnp.log(one))
        reb[r, :] = soft.astype(BF16)
        res = jnp.where(mask > 0.0, soft - x_ref[r, :].astype(F32), 0.0)
        sq[...] += jnp.sum((res * res).reshape(part // 8, 8, cells), axis=0)
        dr = scale[0] * res
        direct[r, :] = dr.astype(BF16)
        d = (dr * (jnp.where(out >= 0.0, 1.0, t) / one)).astype(BF16)
        lane = lax.broadcasted_iota(jnp.int32, (1, part), 1) + j * part < lim
        dscr[r, :] = d
    lane = lax.broadcasted_iota(jnp.int32, (1, block), 1) < lim
    dg[...] = mm(a_ref[...], dscr[...], NT).astype(BF16)
    g_ref[...] += mm(jnp.where(lane, d_ref[...], jnp.zeros((), BF16)), dscr[...], NN)


def output_layer(D, act, x, panels, hot, scale, block=1024, part=256):
    cells = x.shape[1]
    n = pl.cdiv(G, block)
    rows = lambda: pl.BlockSpec((block, cells), lambda i: (i, 0))
    whole = lambda r, c: pl.BlockSpec((r, c), lambda i: (0, 0))
    return pl.pallas_call(
        functools.partial(output_kernel, part, block),
        grid=(n,),
        out_shape=(jax.ShapeDtypeStruct((G, cells), BF16), jax.ShapeDtypeStruct((G, cells), BF16),
                   jax.ShapeDtypeStruct((HX, G), BF16), jax.ShapeDtypeStruct((HX, cells), F32),
                   jax.ShapeDtypeStruct((8, cells), F32)),
        in_specs=[pl.BlockSpec(memory_space=pltpu.SMEM), pl.BlockSpec((HX, block), lambda i: (0, i)), whole(HX, cells),
                  rows(), pl.BlockSpec((NC, block), lambda i: (0, i)), whole(NC, cells)],
        out_specs=[rows(), rows(), pl.BlockSpec((HX, block), lambda i: (0, i)), whole(HX, cells), whole(8, cells)],
        scratch_shapes=[pltpu.VMEM((block, cells), BF16)],
        compiler_params=params_of(),
        cost_estimate=pl.CostEstimate(flops=6 * G * H * cells, bytes_accessed=70_000_000, transcendentals=3 * G * cells),
        name="output_layer",
    )(scale.reshape(1), D, act, x, panels, hot)


def first_rows_kernel(block, w_ref, x_ref, o_ref):
    i = pl.program_id(0)

    @pl.when(i == 0)
    def _():
        o_ref[...] = jnp.zeros_like(o_ref)

    inside = lax.broadcasted_iota(jnp.int32, (block, 1), 0) < G - i * block
    zero = jnp.zeros((), BF16)

    @pl.when((i + 1) * block <= G)
    def _():
        o_ref[...] += mm(w_ref[...], x_ref[...], TN)

    @pl.when((i + 1) * block > G)
    def _():
        o_ref[...] += mm(jnp.where(inside, w_ref[...], zero), jnp.where(inside, x_ref[...], zero), TN)


def first_linear(F, x, block=1024):
    cells = x.shape[1]
    return pl.pallas_call(
        functools.partial(first_rows_kernel, block),
        grid=(pl.cdiv(G, block),),
        out_shape=jax.ShapeDtypeStruct((H, cells), F32),
        in_specs=[pl.BlockSpec((block, H), lambda i: (i, 0)), pl.BlockSpec((block, cells), lambda i: (i, 0))],
        out_specs=pl.BlockSpec((H, cells), lambda i: (0, 0)),
        compiler_params=params_of(),
        cost_estimate=pl.CostEstimate(flops=2 * G * H * cells, bytes_accessed=30_000_000, transcendentals=0),
        name="first_linear",
    )(F, x)


def last_kernel(x_ref, w_ref, d_ref, t_ref, fg, gc):
    fg[...] = mm(x_ref[...], d_ref[...], NT).astype(BF16)
    gc[...] = (mm(w_ref[...], d_ref[...], NN) - t_ref[...].astype(F32)).astype(BF16)


def last_layer(x, F, d1, direct, frows, block=512):
    cells = x.shape[1]
    rows = lambda c: pl.BlockSpec((block, c), lambda i: (i, 0))
    return pl.pallas_call(
        last_kernel,
        grid=(pl.cdiv(G, block),),
        out_shape=(jax.ShapeDtypeStruct((frows, H), BF16), jax.ShapeDtypeStruct((G, cells), BF16)),
        in_specs=[rows(cells), rows(H), pl.BlockSpec((H, cells), lambda i: (0, 0)), rows(cells)],
        out_specs=[rows(H), rows(cells)],
        compiler_params=params_of(),
        cost_estimate=pl.CostEstimate(flops=4 * G * H * cells, bytes_accessed=70_000_000, transcendentals=0),
        name="last_layer",
    )(x, F, d1, direct)


MESH = pl.DeviceIdType.MESH
FROWS, DROWS = 496, 64
NF = 18
SHARD = 397952
FLATF = 7126600
ALL = (0, 1, 2)


def d_unit(s):
    v = (s * SHARD - FLATF + 111999) // 112000
    return jnp.where(s == NF, 0, jnp.where(s > 31, 51, v))


def place():
    w, n = lax.axis_index("wide"), lax.axis_index("narrow")
    return w // 2, w % 2, n // 2, n % 2


def dev(z, x, y, c):
    return (z * 2 + x, y * 2 + c)


def index(z, x, y, c):
    return (z * 2 + x) * 4 + y * 2 + c


def grd(cond, guard, fn):
    pl.when(cond if guard is None else jnp.logical_and(cond, guard))(fn)


def four(s):
    return jnp.logical_and(s >= NF, (d_unit(s + 1) - d_unit(s)) == 4)


def greet(z, x, y, c, extra=()):
    bar = pltpu.get_barrier_semaphore()
    sig = lambda d: pl.semaphore_signal(bar, inc=1, device_id=d, device_id_type=MESH)
    for d in extra:
        sig(d)
    sig(dev(z, 1 - x, y, c))
    sig(dev(z, x, 1 - y, c))
    sig(dev(z, x, y, 1 - c))

    @pl.when(z > 0)
    def _():
        sig(dev(z - 1, x, y, c))

    @pl.when(z < 3)
    def _():
        sig(dev(z + 1, x, y, c))
    pl.semaphore_wait(bar, len(extra) + 3 + (z > 0).astype(jnp.int32) + (z < 3).astype(jnp.int32))


class Spread:
    def __init__(self, kind, own, buf, send, recv, base=0):
        self.kind, self.own, self.buf, self.send, self.recv = kind, own, buf, send, recv
        self.place = z, x, y, c = place()
        self.sems, self.base, self.started = {}, base, []
        self.XP, self.YP, self.CP = (z, 1 - x, y, c), (z, x, 1 - y, c), (z, x, y, 1 - c)
        self.UP, self.DN = (z + 1, x, y, c), (z - 1, x, y, c)
        self.tags = {0: (0, z, None)}
        for t in (1, 2, 3):
            self.tags[2 * t] = (2 * t, z - t, z >= t)
            self.tags[2 * t + 1] = (2 * t + 1, z + t, z + t <= 3)

    def pieces(self, s, p):
        if self.kind == "F":
            return [] if p == 2 else [(s < NF, FROWS * s, (0, 240)[p], (240, 256)[p])]
        return [(four(s) if p == 2 else s >= NF, 16 * d_unit(s), (0, 32, 48)[p], (32, 16, 16)[p])]

    def rows(self, s, p):
        for cond, base, off, n in self.pieces(s, p):
            yield cond, self.buf.at[pl.ds(pl.multiple_of(base + off, 16), n)], self.own.at[pl.ds(off, n)]

    def copies(self, s, p, key, target, local):
        if not self.pieces(s, p):
            return []
        k = self.base + self.sems.setdefault((key, p), len(self.sems))
        return [(cond, pltpu.make_async_remote_copy(
            src_ref=own if local else dst, dst_ref=dst, send_sem=self.send.at[k], recv_sem=self.recv.at[k],
            device_id=dev(*target), device_id_type=MESH)) for cond, dst, own in self.rows(s, p)]

    def send_to(self, s, parts, key, target, guard=None, local=False):
        for p in parts:
            for cond, cp in self.copies(s, p, key, target, local):
                grd(cond, guard, cp.start)
        self.started.append((s, parts, key, target, guard, local))

    def wait_from(self, s, parts, key, target, guard=None):
        for p in parts:
            for cond, cp in self.copies(s, p, key, target, False):
                grd(cond, guard, cp.wait_recv)

    def begin(self, loc, planes=True, names="ud"):
        z, x, y, c = self.place
        me = index(*self.place)
        self.from_own(names)
        if planes:
            self.spread(0, True)
        self.kept = [(cond, pltpu.make_async_copy(own, dst, loc.at[p])) for p in ALL for cond, dst, own in self.rows(me, p)]
        for cond, cp in self.kept:
            pl.when(cond)(cp.start)

    def from_own(self, names):
        z, x, y, c = self.place
        for p in ALL:
            for name in names:
                to, more = (self.UP, z < 3) if name == "u" else (self.DN, z > 0)
                self.send_to(index(*self.place), (p,), (name, 1), to, more, True)

    def own_in_place(self):
        for cond, cp in self.kept:
            pl.when(cond)(cp.wait)

    def spread(self, tag, local=False):
        _, zz, guard = self.tags[tag]
        z, x, y, c = self.place
        s = index(zz, x, y, c)
        for p in ALL:
            self.send_to(s, (p,), ("x", tag), self.XP, guard, local)
            self.send_to(s, (p,), ("y", tag), self.YP, guard, local)
        self.send_to(s, ALL, ("c0", tag), self.CP, guard, local)

    def along_z(self, t, names="ud", planes=True):
        z, x, y, c = self.place
        for p in ALL:
            for name in names:
                if name == "u":
                    s, ok, frm, to, more = index(z - t, x, y, c), z >= t, self.DN, self.UP, z < 3
                else:
                    s, ok, frm, to, more = index(z + t, x, y, c), z + t <= 3, self.UP, self.DN, z > 0
                self.wait_from(s, (p,), (name, t), frm, ok)
                if t < 3:
                    self.send_to(s, (p,), (name, t + 1), to, jnp.logical_and(ok, more))
        for name in names if planes else "":
            self.spread(2 * t + (name == "d"))

    def flat_parts(self, tag):
        _, zz, guard = self.tags[tag]
        if tag == 0:
            return (guard, guard)
        even = lax.rem(zz + 4, 2) == 0
        return jnp.logical_and(guard, even), jnp.logical_and(guard, jnp.logical_not(even))

    def cross(self, tag):
        _, zz, guard = self.tags[tag]
        z, x, y, c = self.place
        sx, sy = index(zz, 1 - x, y, c), index(zz, x, 1 - y, c)
        second, half = self.flat_parts(tag)
        self.wait_from(sx, ALL, ("x", tag), self.XP, guard)
        self.send_to(sx, (1, 2), ("xy", tag), self.YP, second)
        self.wait_from(sy, ALL, ("y", tag), self.YP, guard)
        self.send_to(sy, (0,), ("yx", tag), self.XP, half)
        self.send_to(sx, ALL, ("c1", tag), self.CP, guard)
        self.send_to(sy, ALL, ("c2", tag), self.CP, guard)

    def diag(self, tag):
        _, zz, guard = self.tags[tag]
        z, x, y, c = self.place
        sd = index(zz, 1 - x, 1 - y, c)
        second, half = self.flat_parts(tag)
        t, name = tag // 2, "ud"[tag % 2]
        both = jnp.logical_and
        if tag:
            frm, to, more = (self.DN, self.UP, z < 3) if name == "u" else (self.UP, self.DN, z > 0)
            self.wait_from(sd, (0,), ("g" + name, t), frm, second)
            self.wait_from(sd, (1, 2), ("g" + name, t), frm, half)
            if t < 3:
                self.send_to(sd, (0,), ("g" + name, t + 1), to, both(second, more))
                self.send_to(sd, (1, 2), ("g" + name, t + 1), to, both(half, more))
        self.wait_from(sd, (1, 2), ("xy", tag), self.YP, second)
        self.wait_from(sd, (0,), ("yx", tag), self.XP, half)
        if tag == 0:
            even = lax.rem(z, 2) == 0
            odd = jnp.logical_not(even)
            for name, to, more in (("u", self.UP, z < 3), ("d", self.DN, z > 0)):
                self.send_to(sd, (0,), ("g" + name, 1), to, both(even, more))
                self.send_to(sd, (1, 2), ("g" + name, 1), to, both(odd, more))
        self.send_to(sd, ALL, ("c3", tag), self.CP, guard)

    def core(self, tag, i):
        _, zz, guard = self.tags[tag]
        z, x, y, c = self.place
        xx, yy = ((x, y), (1 - x, y), (x, 1 - y), (1 - x, 1 - y))[i]
        self.wait_from(index(zz, xx, yy, 1 - c), ALL, ("c%d" % i, tag), self.CP, guard)

    def end(self):
        for s, parts, key, target, guard, local in self.started:
            for p in parts:
                for cond, cp in self.copies(s, p, key, target, local):
                    grd(cond, guard, cp.wait_send)


def first_kernel(fs, x_hbm, ds, F, D, lin, fv, xv, send, recv, loc, fsem, xsem, dsend, drecv, dloc):
    z, x, y, c = place()
    xcopy = pltpu.make_async_copy(x_hbm, xv, xsem)
    xcopy.start()
    net = Spread("F", fs, fv, send, recv)
    late = Spread("D", ds, D, dsend, drecv)
    greet(z, x, y, c)
    net.begin(loc)
    late.begin(dloc)
    lin[...] = jnp.zeros_like(lin)
    out = []

    def store(s, k, guard):
        r = pl.ds(pl.multiple_of(FROWS * s, 16), FROWS)
        cp = pltpu.make_async_copy(fv.at[r], F.at[r], fsem.at[k])
        grd(s < NF, guard, cp.start)
        out.append((s < NF, guard, cp))

    def times(tag, i):
        _, zz, guard = net.tags[tag]
        xx, yy = ((x, y), (1 - x, y), (x, 1 - y), (1 - x, 1 - y))[i]
        m = (zz * 2 + xx) * 2 + yy

        def whole():
            r = pl.ds(pl.multiple_of(2 * FROWS * m, 16), 2 * FROWS)
            lin[...] += mm(fv[r, :], xv[r, :], TN)

        def rest():
            r = pl.ds(14 * FROWS, G - 14 * FROWS)
            lin[...] += mm(fv[r, :], xv[r, :], TN)
        grd(m < 7, guard, whole)
        grd(m == 7, guard, rest)
        k = 8 * tag + 2 * i
        store(2 * m, k, guard)
        store(2 * m + 1, k + 1, guard)

    def finish(tag, cols):
        for i in cols:
            net.core(tag, i)
            times(tag, i)

    def both(name, *tags):
        for n in (net, late):
            for tag in tags:
                getattr(n, name)(tag)

    def settle(tag, cols):
        for i in cols:
            late.core(tag, i)

    both("along_z", 1)
    both("cross", 0)
    both("along_z", 2)
    both("diag", 0)
    both("cross", 2, 3)
    net.own_in_place()
    late.own_in_place()
    xcopy.wait()
    finish(0, (0, 1, 2, 3))
    both("along_z", 3)
    both("diag", 2, 3)
    both("cross", 4, 5)
    finish(2, (0, 1, 2))
    finish(3, (0, 1, 2))
    both("diag", 4, 5)
    both("cross", 6, 7)
    finish(2, (3,))
    finish(3, (3,))
    finish(4, (0, 1, 2))
    finish(5, (0, 1, 2))
    both("diag", 6, 7)
    for tag in (4, 5):
        finish(tag, (3,))
    for tag in (6, 7):
        finish(tag, (0, 1, 2, 3))
    for tag in (0, 2, 3, 4, 5, 6, 7):
        settle(tag, (0, 1, 2, 3))
    net.end()
    late.end()
    for cond, guard, cp in out:
        grd(cond, guard, cp.wait)


def spread_and_first(fslot, dslot, x, cid=1):
    cells = x.shape[1]
    V = pltpu.VMEM
    return pl.pallas_call(
        first_kernel,
        out_shape=(jax.ShapeDtypeStruct((FROWS * NF, H), BF16), jax.ShapeDtypeStruct((HX, G), BF16), jax.ShapeDtypeStruct((H, cells), F32)),
        in_specs=[pl.BlockSpec(memory_space=pl.ANY)] * 3,
        out_specs=[pl.BlockSpec(memory_space=pl.ANY)] * 2 + [pl.BlockSpec(memory_space=V)],
        scratch_shapes=[V((FROWS * NF, H), BF16), V((G, cells), BF16), pltpu.SemaphoreType.DMA((128,)), pltpu.SemaphoreType.DMA((128,)),
                        pltpu.SemaphoreType.DMA((3,)), pltpu.SemaphoreType.DMA((64,)), pltpu.SemaphoreType.DMA,
                        pltpu.SemaphoreType.DMA((192,)), pltpu.SemaphoreType.DMA((192,)), pltpu.SemaphoreType.DMA((3,))],
        compiler_params=pltpu.CompilerParams(collective_id=cid, has_side_effects=True, vmem_limit_bytes=58 * 2**20),
        name="spread_and_first",
    )(fslot, x, dslot)


def slots(p):
    n = 32
    me = lax.axis_index("wide") * 4 + lax.axis_index("narrow")
    ax = ("wide", "narrow")
    head = lax.ppermute(p[-36864:], ax, [(i, i + 1) for i in range(n - 1)])
    tail = lax.ppermute(p[:112000], ax, [(i + 1, i) for i in range(n - 1)])
    ext = jnp.concatenate([head, p, tail, jnp.zeros((112000,), p.dtype)])
    f = lax.dynamic_slice(ext, (jnp.maximum(36864 - 1152 * me, 0),), (FROWS * 800,)).reshape(FROWS, 800)
    off = 36864 + FLATF + 112000 * d_unit(me) - SHARD * me
    d = lax.dynamic_slice(ext, (jnp.clip(off, 0, ext.shape[0] - DROWS * 7000),), (DROWS * 7000,)).reshape(DROWS, 7000)
    return f, d

LP = 128
STEP, UNROLL = 32, 5


def rows_loop(n, fn, step=STEP, unroll=UNROLL):
    def body(i, _):
        for j in range(unroll):
            fn(pl.ds(pl.multiple_of((i * unroll + j) * step, step), step))
        return 0
    lax.fori_loop(0, n // (step * unroll), body, 0)


def silu(u):
    return u * (0.5 + 0.5 * jnp.tanh(0.5 * u))


def by_lanes(v):
    return sum(v[:, 128 * i:128 * i + 128] for i in range(v.shape[1] // 128))


def over_rows(buf):
    return jnp.sum(jnp.transpose(buf), axis=0, keepdims=True)


def along_rows(row):
    return jnp.transpose(jnp.broadcast_to(row, (128, 896)))


def wide(col, cells):
    return jnp.concatenate([col] * (cells // 128), axis=1)


class Sums:
    def __init__(self, bufs, sems):
        self.bufs, self.sems, self.turn = bufs, sems, 0
        self.place = z, x, y, c = place()
        self.spot = x * 4 + y * 2 + c
        self.inside = [(k, lax.bitwise_xor(self.spot, k)) for k in range(1, 8)]
        self.planes = [(k, lax.bitwise_xor(z, k)) for k in range(1, 4)]

    def near_dev(self, q):
        return dev(self.place[0], q // 4, (q // 2) % 2, q % 2)

    def far_dev(self, q):
        return dev(q, *self.place[1:])

    def others(self):
        return [self.near_dev(q) for k, q in self.inside] + [self.far_dev(q) for k, q in self.planes]

    def __call__(self, kind, value, between=None, after=None):
        near, far = self.bufs[kind]
        i, t = self.turn, self.sems
        self.turn += 1
        j = self.count[kind] = self.count.get(kind, -1) + 1 if hasattr(self, "count") else self.first(kind)
        s, f = near.at[j], far.at[j]
        s[self.spot] = value
        cps = [pltpu.make_async_remote_copy(src_ref=s.at[self.spot], dst_ref=s.at[self.spot], send_sem=t[0].at[i, k], recv_sem=t[1].at[i, k],
                                            device_id=self.near_dev(q), device_id_type=MESH) for k, q in self.inside]
        for cp in cps:
            cp.start()
        if between:
            between()
        for cp in cps:
            cp.wait_recv()
        z = self.place[0]
        f[z] = jnp.sum(s[...], axis=0)
        cpz = [pltpu.make_async_remote_copy(src_ref=f.at[z], dst_ref=f.at[z], send_sem=t[2].at[i, k], recv_sem=t[3].at[i, k],
                                            device_id=self.far_dev(q), device_id_type=MESH) for k, q in self.planes]
        for cp in cpz:
            cp.start()
        for cp in cps:
            cp.wait_send()
        if after:
            after()
        for cp in cpz:
            cp.wait()
        return jnp.sum(f[...], axis=0)

    def first(self, kind):
        self.count = {}
        return 0


def sums_scratch(stats, tables):
    V = pltpu.VMEM
    n = stats + tables
    dma = pltpu.SemaphoreType.DMA
    return [V((stats, 8, 2, 896), F32), V((stats, 4, 2, 896), F32), V((max(tables, 1), 8, 8, 128), F32), V((max(tables, 1), 4, 8, 128), F32),
            dma((n, 8)), dma((n, 8)), dma((n, 4)), dma((n, 4))]


def forward_kernel(total, lin1, w2, wh, wd1, wd2, grows, bh, hot, eps,
                   act1o, act2o, act3o, ends, heads, latent, lin2o, lin3o, lin4, stat, table,
                   act1, act2, act3, lin2, lin3, osem, bufs, square, n1, f1, n2, f2, a1, a2, a3, a4):
    z, x, y, c = place()
    sums = Sums({"stat": (n1, f1), "table": (n2, f2)}, (a1, a2, a3, a4))
    cells = lin1.shape[1]
    for i in range(2):
        bufs[i, pl.ds(H, 96), :] = jnp.zeros((96, 128), F32)
    square[...] = jnp.zeros_like(square)
    greet_all(sums.others())

    def stats(lin):
        def one(r):
            v = lin[r, :]
            bufs[0, r, :] = by_lanes(v)
            bufs[1, r, :] = by_lanes(v * v)
        rows_loop(H, one)
        return jnp.concatenate([over_rows(bufs[0]), over_rows(bufs[1])])

    def norm(k, lin, out, between=None, after=None):
        t = sums("stat", stats(lin), between, after)
        centre = t[0:1, :] / total
        inverse = lax.rsqrt(t[1:2, :] / total - centre * centre + EPSILON_NORM)
        stat[pl.ds(2 * k, 1), :] = centre
        stat[pl.ds(2 * k + 1, 1), :] = inverse
        scale = inverse * grows[2 * k:2 * k + 1, :]
        bufs[0] = along_rows(scale)
        bufs[1] = along_rows(grows[2 * k + 1:2 * k + 2, :] - centre * scale)

        def one(r):
            out[r, :] = silu(lin[r, :] * wide(bufs[0, r, :], cells) + wide(bufs[1, r, :], cells)).astype(BF16)
        rows_loop(H, one)

    leaving = []

    def leave(src, dst):
        cp = pltpu.make_async_copy(src, dst, osem.at[len(leaving)])
        cp.start()
        leaving.append(cp)

    norm(0, lin1, act1)
    lin2[...] = mm(w2[...], act1[...], TN)
    leave(act1, act1o)
    leave(lin2, lin2o)
    norm(1, lin2, act2)
    leave(act2, act2o)
    h = (mm(wh[...], act2[...], TN) + bh[...]).astype(BF16)
    heads[...] = h
    mu, lv = h[:LP].astype(F32), h[LP:].astype(F32)
    part = mm(hot[...], h[:LP], NT)
    hf = hot[...].astype(F32)
    lane = lax.broadcasted_iota(jnp.int32, (NC, LP), 1)
    top = jnp.where(lane == LP - 1, jnp.sum(hf, axis=1, keepdims=True), part)
    kl = jnp.sum(jnp.sum(1.0 + lv - mu * mu - jnp.exp(lv), axis=0, keepdims=True), axis=1, keepdims=True)
    low = jnp.where(lax.broadcasted_iota(jnp.int32, (4, LP), 0) == 0, kl, 0.0)

    t = sums("table", jnp.concatenate([top, low]))
    table[...] = t
    cond = t[0:NC, :]
    counts = cond[:, LP - 1:LP]
    cond = jnp.where(lane == LP - 1, 0.0, cond)
    off = cond / counts - jnp.sum(cond, axis=0, keepdims=True) / total
    square[pl.ds(0, NC), :] = off
    offc = jnp.transpose(square[...])
    chosen = sum(offc[:, i:i + 1] * hf[i:i + 1, :] for i in range(NC))
    lat = (mu + jnp.exp(0.5 * lv) * eps[...].astype(F32) - chosen).astype(BF16)
    latent[...] = lat
    lin3[...] = mm(wd1[...], latent[...], TN)
    leave(lin3, lin3o)
    norm(2, lin3, act3)
    leave(act3, act3o)
    lin4[...] = mm(wd2[...], act3[...], TN)

    norm(3, lin4, ends)
    ends[pl.ds(H, 16), :] = jnp.where(lax.broadcasted_iota(jnp.int32, (16, ends.shape[1]), 0) == 0, 1.0, 0.0).astype(BF16)
    for cp in leaving:
        cp.wait()


def greet_all(devices):
    bar = pltpu.get_barrier_semaphore()
    for d in devices:
        pl.semaphore_signal(bar, inc=1, device_id=d, device_id_type=MESH)
    pl.semaphore_wait(bar, len(devices))


def hidden_layers(total, lin1, w2, wh, wd1, wd2, grows, bh, hot, eps, cid=2):
    cells = lin1.shape[1]
    V = pltpu.VMEM
    vm = pl.BlockSpec(memory_space=V)
    hbm = pl.BlockSpec(memory_space=pl.ANY)
    S = jax.ShapeDtypeStruct
    return pl.pallas_call(
        functools.partial(forward_kernel, total),
        out_shape=(S((H, cells), BF16), S((H, cells), BF16), S((H, cells), BF16), S((HX, cells), BF16), S((2 * LP, cells), BF16),
                   S((LP, cells), BF16), S((H, cells), F32), S((H, cells), F32), S((H, cells), F32), S((8, 896), F32),
                   S((8, LP), F32)),
        in_specs=[vm] * 9,
        out_specs=[hbm] * 3 + [vm] * 3 + [hbm] * 2 + [vm] * 3,
        scratch_shapes=[*[V((H, cells), BF16)] * 3, *[V((H, cells), F32)] * 2, pltpu.SemaphoreType.DMA((8,)), V((2, 896, 128), F32), V((LP, LP), F32), *sums_scratch(4, 1)],
        compiler_params=pltpu.CompilerParams(collective_id=cid, has_side_effects=True, vmem_limit_bytes=58 * 2**20),
        name="hidden_layers",
    )(lin1, w2, wh, wd1, wd2, grows, bh, hot, eps)


def backward_kernel(total, g4, lin4, w2, wh, wd1, wd2, grows, stat, latent, heads, hot, eps, table, squares, act1i, act2i, act3i, lin1i, lin2i, lin3i,
                    d1, gw2, gwh, gwd1, gwd2, gbh, gnorm, sums2,
                    act1, act2, act3, lin1, lin2, lin3, isem, pbuf, dbuf, hbuf, bufs, part, square, n1, f1, n2, f2, a1, a2, a3, a4):
    cells = lin4.shape[1]
    sums = Sums({"stat": (n1, f1), "table": (n2, f2)}, (a1, a2, a3, a4))
    comes = {}
    for i, (name, src, dst) in enumerate((("lin3", lin3i, lin3), ("act3", act3i, act3), ("lin2", lin2i, lin2), ("act2", act2i, act2),
                                          ("lin1", lin1i, lin1), ("act1", act1i, act1))):
        comes[name] = pltpu.make_async_copy(src, dst, isem.at[i])
        comes[name].start()
    for i in range(2):
        part[i, pl.ds(H, 96), :] = jnp.zeros((96, 128), F32)
    square[...] = jnp.zeros_like(square)
    greet_all(sums.others())

    def norm(k, g, lin, out, between=None):
        centre, inverse = stat[2 * k:2 * k + 1, :], stat[2 * k + 1:2 * k + 2, :]
        gain, shift = grows[2 * k:2 * k + 1, :], grows[2 * k + 1:2 * k + 2, :]
        bufs[0] = along_rows(inverse)
        bufs[1] = along_rows(-centre * inverse)
        bufs[2] = along_rows(gain)
        bufs[3] = along_rows(shift)

        def one(r):
            n = lin[r, :] * wide(bufs[0, r, :], cells) + wide(bufs[1, r, :], cells)
            u = n * wide(bufs[2, r, :], cells) + wide(bufs[3, r, :], cells)
            s = 0.5 + 0.5 * jnp.tanh(0.5 * u)
            p = g[r, :] * s * (1.0 + u * (1.0 - s))
            pbuf[r, :] = p
            part[0, r, :] = by_lanes(p)
            part[1, r, :] = by_lanes(p * n)
        rows_loop(H, one)
        local = jnp.concatenate([over_rows(part[0]), over_rows(part[1])])
        gnorm[pl.ds(2 * k, 2), :] = local
        t = sums("stat", local, between)
        a = gain * inverse
        b = -a * t[1:2, :] / total
        bufs[0] = along_rows(a)
        bufs[1] = along_rows(b * inverse)
        bufs[2] = along_rows(-b * centre * inverse - a * t[0:1, :] / total)

        def two(r):
            out[r, :] = (pbuf[r, :] * wide(bufs[0, r, :], cells) + lin[r, :] * wide(bufs[1, r, :], cells)
                         + wide(bufs[2, r, :], cells)).astype(BF16)
        rows_loop(H, two)

    norm(3, g4, lin4, dbuf)
    pbuf[...] = mm(wd2[...], dbuf[...], NN)
    comes["lin3"].wait()
    comes["act3"].wait()

    def grads4():
        gwd2[...] = mm(act3[...], dbuf[...], NT).astype(BF16)
    norm(2, pbuf, lin3, hbuf, grads4)
    dl = mm(wd1[...], hbuf[...], NN).astype(BF16)
    cond = mm(hot[...], dl, NT)
    sq = jnp.sum(jnp.sum(squares[...], axis=0, keepdims=True), axis=1, keepdims=True)
    low = jnp.where(lax.broadcasted_iota(jnp.int32, (4, LP), 0) == 0, sq, 0.0)

    def grads3():
        gwd1[...] = mm(latent[...], hbuf[...], NT).astype(BF16)
    t = sums("table", jnp.concatenate([cond, low]), grads3)
    sums2[...] = t
    cond = t[0:NC, :]
    counts = table[0:NC, LP - 1:LP]
    square[pl.ds(0, NC), :] = jnp.sum(cond, axis=0, keepdims=True) / total - cond / counts
    take = jnp.transpose(square[...])
    hf = hot[...].astype(F32)
    change = sum(take[:, i:i + 1] * hf[i:i + 1, :] for i in range(NC))
    mu, lv = heads[pl.ds(0, LP), :].astype(F32), heads[pl.ds(LP, LP), :].astype(F32)
    dl = dl.astype(F32)
    dh = jnp.concatenate([
        dl + change + (KL_WEIGHT / total) * mu,
        0.5 * dl * jnp.exp(0.5 * lv) * eps[...].astype(F32) + (0.5 * KL_WEIGHT / total) * (jnp.exp(lv) - 1.0)]).astype(BF16)
    dbuf[pl.ds(0, 2 * LP), :] = dh
    gbh[...] = mm(jnp.ones((8, cells), BF16), dh, NT)
    pbuf[...] = mm(wh[...], dh, NN)
    comes["lin2"].wait()
    comes["act2"].wait()

    def grads2():
        gwh[...] = mm(act2[...], dbuf[pl.ds(0, 2 * LP), :], NT).astype(BF16)
    norm(1, pbuf, lin2, hbuf, grads2)
    pbuf[...] = mm(w2[...], hbuf[...], NN)
    comes["lin1"].wait()
    comes["act1"].wait()

    def grads1():
        gw2[...] = mm(act1[...], hbuf[...], NT).astype(BF16)
    norm(0, pbuf, lin1, d1, grads1)


def hidden_backward(total, g4, lin4, w2, wh, wd1, wd2, grows, stat, latent, heads, hot, eps, table, squares, acts, lins, cid=3):
    cells = lin4.shape[1]
    V = pltpu.VMEM
    vm = pl.BlockSpec(memory_space=V)
    hbm = pl.BlockSpec(memory_space=pl.ANY)
    S = jax.ShapeDtypeStruct
    return pl.pallas_call(
        functools.partial(backward_kernel, total),
        out_shape=(S((H, cells), BF16), S((H, H), BF16), S((H, 2 * LP), BF16), S((LP, H), BF16), S((H, H), BF16),
                   S((8, 2 * LP), F32), S((8, 896), F32), S((8, LP), F32)),
        in_specs=[vm] * 14 + [hbm] * 6,
        out_specs=[vm] * 8,
        scratch_shapes=[*[V((H, cells), BF16)] * 3, *[V((H, cells), F32)] * 3, pltpu.SemaphoreType.DMA((6,)),
                        V((H, cells), F32), V((H, cells), BF16), V((H, cells), BF16),
                        V((4, 896, 128), F32), V((2, 896, 128), F32), V((LP, LP), F32), *sums_scratch(4, 1)],
        compiler_params=pltpu.CompilerParams(collective_id=cid, has_side_effects=True, vmem_limit_bytes=58 * 2**20),
        name="hidden_backward",
    )(g4, lin4, w2, wh, wd1, wd2, grows, stat, latent, heads, hot, eps, table, squares, *acts, *lins)


ZF, ZD = (0, 1, 2), (2, 3)

def reduce_kernel(FG, DG, fo, do, tF, tD, cF, cD, rF, rD, aF, aD, bF, bD, uF, uD, vF, vD, send, recv, loc):
    z, x, y, c = place()
    bar = pltpu.get_barrier_semaphore()
    sig = lambda d: pl.semaphore_signal(bar, inc=1, device_id=d, device_id_type=MESH)
    XP, YP, CP = (z, 1 - x, y, c), (z, x, 1 - y, c), (z, x, y, 1 - c)
    UP, DN = (z + 1, x, y, c), (z - 1, x, y, c)
    for d in (XP, YP, CP):
        sig(dev(*d))
    @pl.when(z > 0)
    def _(): sig(dev(*DN))
    @pl.when(z < 3)
    def _(): sig(dev(*UP))
    pl.semaphore_wait(bar, 3 + (z > 0).astype(jnp.int32) + (z < 3).astype(jnp.int32))

    sems = {}
    def sem_index(key):
        return sems.setdefault(key, len(sems))
    started = []

    def cases(s, part):
        e = d_unit(s)
        four = jnp.logical_and(s >= NF, (d_unit(s + 1) - e) == 4)
        f, d = s < NF, s >= NF
        if part == "all":
            return [(f, "F", 0, 496, 0), (d, "D", 0, 48, 0), (four, "D", 48, 16, 1)]
        if part == "a":
            return [(f, "F", 0, 240, 0), (d, "D", 0, 32, 0)]
        return [(f, "F", 240, 256, 0), (d, "D", 32, 16, 0), (four, "D", 48, 16, 1)]

    def land(pair, zz, b, col=None):
        buf = pair[0 if b == "F" else 1]
        zi = zz if b == "F" else zz - 2
        return buf.at[zi] if col is None else buf.at[col, zi]

    def grd(cond, guard, fn):
        pl.when(cond if guard is None else jnp.logical_and(cond, guard))(fn)

    def clampz(zz, b):
        return jnp.clip(zz, 0, 2) if b == "F" else jnp.clip(zz, 2, 3)

    def make(s, zz, part, key, target, src_of, dst_of):
        out = []
        for cond, b, off, rows, q in cases(s, part):
            k = sem_index((key, q))
            zc = clampz(zz, b)
            ref, base = src_of(b, zc)
            out.append((cond, pltpu.make_async_remote_copy(
                src_ref=ref.at[pl.ds(off if isinstance(base, int) else pl.multiple_of(base + off, 16), rows)],
                dst_ref=dst_of(b, zc)[0].at[pl.ds(off, rows)],
                send_sem=send.at[k], recv_sem=recv.at[k], device_id=dev(*target), device_id_type=MESH)))
        return out

    def go(guard, *a):
        for cond, cp in make(*a):
            grd(cond, guard, cp.start)
        started.append((guard, a))

    def got(guard, *a):
        for cond, cp in make(*a):
            grd(cond, guard, cp.wait_recv)

    def each(rows, off, fn):
        def body(i, _):
            fn(pl.ds(pl.multiple_of(off + 16 * i, 16), 16))
            return 0
        lax.fori_loop(0, rows // 16, body, 0)

    def total(s, guard, part, zz, dst, terms, out=None):
        for cond, b, off, rows, q in cases(s, part):
            zc = clampz(zz, b)
            def fn(b=b, off=off, rows=rows, zc=zc):
                refs = [t(b, zc)[0] for t in terms]
                def step(r):
                    v = refs[0][r, :].astype(jnp.float32)
                    for ref in refs[1:]:
                        v = v + ref[r, :].astype(jnp.float32)
                    if out is None:
                        dst(b, zc)[0][r, :] = v.astype(jnp.bfloat16)
                    else:
                        out[0 if b == "F" else 1][r, :] = v
                each(rows, off, step)
            grd(cond, guard, fn)

    C, R, A, B, U, V = (cF, cD), (rF, rD), (aF, aD), (bF, bD), (uF, uD), (vF, vD)
    cols = ((x, y), (1 - x, y), (x, 1 - y), (1 - x, 1 - y))
    tags = [(7, z - 3, z >= 3), (6, z + 3, z <= 0), (5, z - 2, z >= 2), (4, z + 2, z <= 1),
            (3, z - 1, z >= 1), (2, z + 1, z <= 2), (0, z, None)]

    def own_rows(s):
        return lambda b, zc: (FG, FROWS * s) if b == "F" else (DG, 16 * d_unit(s))
    on = lambda pair, col=None: (lambda b, zc: (land(pair, zc, b, col), 0))

    for tag, zz, guard in tags:
        for col in (3, 1, 2, 0):
            s = index(zz, *cols[col], 1 - c)
            go(guard, s, zz, "all", ("c", tag, col), CP, own_rows(s), on(C, col))

    order = [(tg, col) for tg in tags for col in (3, 1, 2, 0)]

    def load(k, what):
        (tag, zz, guard), col = order[k]
        s = index(zz, *cols[col], c)
        e = d_unit(s)
        for cond, b, off, rows, q in cases(s, "all"):
            src = FG.at[pl.ds(pl.multiple_of(FROWS * s + off, 16), rows)] if b == "F" else DG.at[pl.ds(pl.multiple_of(16 * e + off, 16), rows)]
            dst = (tF if b == "F" else tD).at[k % 2, pl.ds(off, rows)]
            cp = pltpu.make_async_copy(src, dst, loc.at[k % 2, q])
            grd(cond, guard, cp.start if what == "start" else cp.wait)

    def join(k):
        if k + 1 < len(order):
            load(k + 1, "start")
        load(k, "wait")
        (tag, zz, guard), col = order[k]
        s = index(zz, *cols[col], c)
        got(guard, s, zz, "all", ("c", tag, col), CP, own_rows(s), on(C, col))
        mine = lambda b, zc: ((tF if b == "F" else tD).at[k % 2], 0)
        total(s, guard, "all", zz, on(C, col), [on(C, col), mine])

    def first(i):
        tag, zz, guard = tags[i]
        join(4 * i)
        s = index(zz, *cols[3], c)
        go(guard, s, zz, "a", ("xa", tag), XP, on(C, 3), on(R, 1))
        go(guard, s, zz, "b", ("yb", tag), YP, on(C, 3), on(R, 0))
        for k in (1, 2, 3):
            join(4 * i + k)

    def second(i):
        tag, zz, guard = tags[i]
        sx, sy = index(zz, *cols[1], c), index(zz, *cols[2], c)
        got(guard, sx, zz, "b", ("yb", tag), YP, on(C, 3), on(R, 0))
        total(sx, guard, "b", zz, on(C, 1), [on(C, 1), on(R, 0)])
        go(guard, sx, zz, "all", ("X", tag), XP, on(C, 1), on(A))
        got(guard, sy, zz, "a", ("xa", tag), XP, on(C, 3), on(R, 1))
        total(sy, guard, "a", zz, on(C, 2), [on(C, 2), on(R, 1)])
        go(guard, sy, zz, "all", ("Y", tag), YP, on(C, 2), on(B))

    def third(i):
        tag, zz, guard = tags[i]
        s = index(zz, *cols[0], c)
        got(guard, s, zz, "all", ("X", tag), XP, on(C, 1), on(A))
        got(guard, s, zz, "all", ("Y", tag), YP, on(C, 2), on(B))
        t = {7: 3, 6: 3, 5: 2, 4: 2, 3: 1, 2: 1, 0: 0}[tag]
        base = [on(C, 0), on(A), on(B)]
        if t == 0:
            for cond, frm, pair, key in ((z < 3, UP, U, ("zd", 1)), (z > 0, DN, V, ("zu", 1))):
                got(cond, s, zz, "all", key, frm, on(C, 0), on(pair))
            inner = jnp.logical_and(z > 0, z < 3)
            total(s, inner, "all", zz, None, base + [on(U), on(V)], out=(fo, do))
            total(s, z == 0, "all", zz, None, base + [on(U)], out=(fo, do))
            total(s, z == 3, "all", zz, None, base + [on(V)], out=(fo, do))
            return
        down = tag in (7, 5, 3)
        to, frm, pair, name = (DN, UP, U, "zd") if down else (UP, DN, V, "zu")
        more = (z < 3) if down else (z > 0)
        if t < 3:
            got(jnp.logical_and(guard, more), s, zz, "all", (name, t + 1), frm, on(C, 0), on(pair))
            total(s, jnp.logical_and(guard, more), "all", zz, on(C, 0), base + [on(pair)])
            total(s, jnp.logical_and(guard, jnp.logical_not(more)), "all", zz, on(C, 0), base)
        else:
            total(s, guard, "all", zz, on(C, 0), base)
        go(guard, s, zz, "all", (name, t), to, on(C, 0), on(pair))

    me = index(z, x, y, c)
    @pl.when(me >= NF)
    def _(): fo[...] = jnp.zeros_like(fo)
    do[pl.ds(48, 16), :] = jnp.zeros((16, 7000), jnp.float32)
    @pl.when(me < NF)
    def _(): do[pl.ds(0, 48), :] = jnp.zeros((48, 7000), jnp.float32)
    load(0, "start")
    n = len(tags)
    for i in range(n + 2):
        if i < n:
            first(i)
        if 1 <= i <= n:
            second(i - 1)
        if i >= 2:
            third(i - 2)
    for guard, a in started:
        for cond, cp in make(*a):
            grd(cond, guard, cp.wait_send)

def reduce(FG, DG, cid=2):
    B16 = jnp.bfloat16
    V = pltpu.VMEM
    pair = lambda *lead: [V(lead + (3, FROWS, 800), B16), V(lead + (2, DROWS, 7000), B16)]
    return pl.pallas_call(
        reduce_kernel,
        out_shape=(jax.ShapeDtypeStruct((FROWS, 800), jnp.float32), jax.ShapeDtypeStruct((DROWS, 7000), jnp.float32)),
        in_specs=[pl.BlockSpec(memory_space=pl.ANY)] * 2,
        out_specs=[pl.BlockSpec(memory_space=V)] * 2,
        scratch_shapes=[V((2, FROWS, 800), B16), V((2, DROWS, 7000), B16), *pair(4), *pair(2), *pair(), *pair(), *pair(), *pair(),
                        pltpu.SemaphoreType.DMA((192,)), pltpu.SemaphoreType.DMA((192,)), pltpu.SemaphoreType.DMA((2, 2))],
        compiler_params=pltpu.CompilerParams(collective_id=cid, has_side_effects=True, vmem_limit_bytes=60 * 2**20),
        name="sum_gradients",
    )(FG, DG)

def flatten(fo, do):
    n = 32
    me = lax.axis_index("wide") * 4 + lax.axis_index("narrow")
    ax = ("wide", "narrow")
    nextf = lax.ppermute(fo[:26], ax, [(i + 1, i) for i in range(n - 1)]).reshape(-1)
    nextd = lax.ppermute(do[:6], ax, [(18, 17)]).reshape(-1)
    e = d_unit(me)
    last = 16 * jnp.maximum(d_unit(me + 1) - e - 1, 0)
    prevd = lax.ppermute(lax.dynamic_slice(do, (last, 0), (16, 7000)), ax, [(i, i + 1) for i in range(n - 1)]).reshape(-1)
    ff = fo.reshape(-1)
    a = lax.dynamic_slice(jnp.concatenate([ff, nextf]), (1152 * jnp.minimum(me, 16),), (SHARD,))
    b = jnp.concatenate([ff[19584:381000], nextd[:36536]])
    off = 112000 - (112000 * e + 7126600 - SHARD * me)
    c = lax.dynamic_slice(jnp.concatenate([prevd, do.reshape(-1)]), (jnp.clip(off, 0, 560000 - SHARD),), (SHARD,))
    return jnp.where(me < 17, a, jnp.where(me == 17, b, c))


def allsum(arrays):
    return lax.psum(arrays, ("wide", "narrow"))


def norm_forward(values, gain, shift, total):
    sums, squares = allsum([jnp.sum(values, axis=1), jnp.sum(values * values, axis=1)])
    centre = sums / total
    inverse = lax.rsqrt(squares / total - centre * centre + EPSILON_NORM)
    normed = (values - centre[:, None]) * inverse[:, None]
    affine = gain.astype(F32)[:, None] * normed + shift.astype(F32)[:, None]
    return (normed, inverse, affine), jax.nn.silu(affine).astype(BF16)


def norm_backward(g, kept, gain, total):
    normed, inverse, affine = kept
    sigma = jax.nn.sigmoid(affine)
    p = g * sigma * (1.0 + affine * (1.0 - sigma))
    shift_part = jnp.sum(p, axis=1)
    gain_part = jnp.sum(p * normed, axis=1)
    shift_all, gain_all = allsum([shift_part, gain_part])
    d = (gain.astype(F32) * inverse)[:, None] * (p - (shift_all / total)[:, None] - normed * (gain_all / total)[:, None])
    return d.astype(BF16), gain_part, shift_part


def rows_of(params):
    flat = lax.all_gather(params, ("wide", "narrow"), axis=0, tiled=True)
    F = flat[:FROWS * NF * H].reshape(FROWS * NF, H)
    D = flat[FLATF:]
    D = jnp.pad(D, (0, max(0, HX * G - D.shape[0])))[:HX * G].reshape(HX, G)
    return F, D


def scatter_rows(FG, DG, length):
    flat = jnp.concatenate([FG.astype(F32).reshape(-1)[:FLATF], DG.astype(F32).reshape(-1)])
    flat = jnp.pad(flat, (0, max(0, length - flat.shape[0])))[:length]
    return lax.psum_scatter(flat, ("wide", "narrow"), scatter_dimension=0, tiled=True)


def unpack_rows(F):
    tail = jnp.concatenate([F[8004:8908, 200:], F[8005:8909, :200]], axis=1)
    return [None, F[7000], F[7001], F[7002:7802], F[7802], F[7803], F[7804:8004].reshape(H, 2 * L), F[8004, :200],
            tail[:100], tail[100], tail[101], tail[102:902], tail[902], tail[903]]


def pack_rows(g):
    g = [a.astype(BF16) for a in g]
    row = lambda a: a.reshape(1, -1)
    tail = jnp.concatenate([g[7], row(g[8]), row(g[9]), g[10], row(g[11]), row(g[12])])
    bent = jnp.concatenate([jnp.concatenate([row(g[6]), tail[:, 600:]]), jnp.pad(tail[:, :600], ((0, 1), (0, 0)))], axis=1)
    return jnp.concatenate([row(g[0]), row(g[1]), g[2], row(g[3]), row(g[4]), g[5].reshape(200, 800), bent,
                            jnp.zeros((FROWS * NF - 8909, 800), BF16)])


def by_halves(a, axis):
    wide = [(0, 0)] * a.ndim
    wide[axis] = (0, LP - L)
    return jnp.concatenate([jnp.pad(lax.slice_in_dim(a, i, i + L, axis=axis), wide) for i in (0, L)], axis=axis)


def unhalved(a, axis):
    return jnp.concatenate([lax.slice_in_dim(a, i, i + L, axis=axis) for i in (0, LP)], axis=axis)


def one_hot(labels):
    return (labels[None, :] == jnp.arange(NC, dtype=jnp.int32)[:, None]).astype(BF16)


def fast_step(expression, epsilon, params, panels, labels):
    total = float(expression.shape[0] * 32)
    x = expression.T
    hot = one_hot(labels)
    F, D, lin1 = spread_and_first(*slots(params), x)
    w = unpack_rows(F)
    eps = jnp.pad(epsilon.T, ((0, LP - L), (0, 0)))
    wh = by_halves(w[6], 1)
    bh = by_halves(w[7].astype(F32), 0)[:, None]
    wd1 = jnp.pad(w[8], ((0, LP - L), (0, 0)))
    grows = jnp.pad(jnp.stack([w[i].astype(F32) for i in (1, 2, 4, 5, 9, 10, 12, 13)]), ((0, 0), (0, 896 - H)))
    act1, act2, act3, ends, heads, latent, lin2, lin3, lin4, stat, table = hidden_layers(
        total, lin1, w[3], wh, wd1, w[11], grows, bh, hot, eps)
    counts = table[:NC, LP - 1]
    cond_sums = table[:NC, :L]
    offset = cond_sums / counts[:, None] - jnp.sum(cond_sums, axis=0) / total
    mask_total = jnp.sum(counts * jnp.sum(panels.astype(F32), axis=1))
    rebuilt, direct, DG, g4, squares = output_layer(D, ends, x, panels.astype(BF16), hot, 2.0 / mask_total)
    d1, gw2, gwh, gwd1, gwd2, gbh, gnorm, sums2 = hidden_backward(
        total, g4, lin4, w[3], wh, wd1, w[11], grows, stat, latent, heads, hot, eps, table, squares,
        (act1, act2, act3), (lin1, lin2, lin3))
    FG, grad_cells = last_layer(x, F, d1, direct, FROWS * NF)
    gn = gnorm[:, :H]
    tail = pack_rows([gn[1], gn[0], gw2, gn[3], gn[2], unhalved(gwh, 1), unhalved(gbh[0], 0), gwd1[:L], gn[5], gn[4], gwd2, gn[7], gn[6]])
    FG = lax.dynamic_update_slice(FG, tail, (G, 0))
    grad_params = flatten(*reduce(FG, DG, 4))
    divergence = -0.5 * table[NC, 0] / total
    loss = sums2[NC, 0] / mask_total + KL_WEIGHT * divergence
    columns = L // 4
    mine = lax.dynamic_slice(offset, (0, lax.axis_index("narrow") * columns), (NC, columns))
    return rebuilt.T, mine, loss, grad_cells.T, grad_params, divergence


def general_step(expression, epsilon, params, panels, labels):
    total = expression.shape[0] * lax.axis_size("wide") * lax.axis_size("narrow")
    x = expression.T
    noise = epsilon.T.astype(F32)
    F, D = rows_of(params)
    w = unpack_rows(F)
    hot = one_hot(labels)
    panel_sizes = jnp.sum(panels.astype(F32), axis=1)
    kept1, act1 = norm_forward(first_linear(F, x), w[1], w[2], total)
    kept2, act2 = norm_forward(mm(w[3], act1, TN), w[4], w[5], total)
    heads = (mm(w[6], act2, TN) + w[7].astype(F32)[:, None]).astype(BF16)
    mu, logvar = heads[:L].astype(F32), heads[L:].astype(F32)
    deviation = jnp.exp(0.5 * logvar)
    cond_sums, counts, kl = allsum([
        mm(hot, heads[:L], NT), jnp.sum(hot.astype(F32), axis=1),
        jnp.sum(1.0 + logvar - mu * mu - jnp.exp(logvar)).reshape(1)])
    offset = cond_sums / counts[:, None] - jnp.sum(cond_sums, axis=0) / total
    hotf = hot.astype(F32)
    choose = lambda table: sum(table[i][:, None] * hotf[i][None, :] for i in range(NC))
    latent = (mu + deviation * noise - choose(offset)).astype(BF16)
    kept3, act3 = norm_forward(mm(w[8], latent, TN), w[9], w[10], total)
    kept4, act4 = norm_forward(mm(w[11], act3, TN), w[12], w[13], total)
    mask_total = jnp.sum(counts * panel_sizes)
    ends = jnp.concatenate([act4, jnp.ones((1, act4.shape[1]), BF16), jnp.zeros((HX - H - 1, act4.shape[1]), BF16)])
    rebuilt, direct, DG, g4, squares = output_layer(D, ends, x, panels.astype(BF16), hot, 2.0 / mask_total)
    squared_part = jnp.sum(squares)
    d4, gain4, shift4 = norm_backward(g4[:H], kept4, w[12], total)
    grad_wd2 = mm(act3, d4, NT)
    d3, gain3, shift3 = norm_backward(mm(w[11], d4, NN), kept3, w[9], total)
    grad_wd1 = mm(latent, d3, NT)
    d_latent = mm(w[8], d3, NN).astype(BF16)
    cond_grad, squared = allsum([mm(hot, d_latent, NT), squared_part.reshape(1)])
    dl = d_latent.astype(F32)
    total_grad = jnp.sum(cond_grad, axis=0)
    d_mu = dl - choose(cond_grad / counts[:, None]) + (total_grad / total)[:, None] + KL_WEIGHT * mu / total
    d_logvar = 0.5 * dl * deviation * noise + KL_WEIGHT * 0.5 * (jnp.exp(logvar) - 1.0) / total
    d_heads = jnp.concatenate([d_mu, d_logvar]).astype(BF16)
    grad_bh = jnp.sum(d_heads.astype(F32), axis=1)
    grad_wh = mm(act2, d_heads, NT)
    d2, gain2, shift2 = norm_backward(mm(w[6], d_heads, NN), kept2, w[4], total)
    grad_w2 = mm(act1, d2, NT)
    d1, gain1, shift1 = norm_backward(mm(w[3], d2, NN), kept1, w[1], total)
    FG, grad_cells = last_layer(x, F, d1, direct, FROWS * NF)
    tail = pack_rows([gain1, shift1, grad_w2, gain2, shift2, grad_wh, grad_bh, grad_wd1, gain3, shift3, grad_wd2, gain4, shift4])
    FG = lax.dynamic_update_slice(FG, tail, (G, 0))
    grad_params = scatter_rows(FG, DG, params.shape[0] * lax.axis_size("wide") * lax.axis_size("narrow"))
    divergence = -0.5 * kl[0] / total
    loss = squared[0] / mask_total + KL_WEIGHT * divergence
    columns = L // lax.axis_size("narrow")
    mine = lax.dynamic_slice(offset, (0, lax.axis_index("narrow") * columns), (NC, columns))
    return rebuilt.T, mine, loss, grad_cells.T, grad_params, divergence


def solution(mesh):
    cells = P(("wide", "narrow"), None)
    flat = P(("wide", "narrow"))
    step = fast_step if dict(mesh.shape) == {"wide": 8, "narrow": 4} else general_step
    return jax.shard_map(step, mesh=mesh, in_specs=(cells, cells, flat, P(), flat),
                         out_specs=(cells, P(None, "narrow"), P(), cells, flat, P()), check_vma=False)
```

```python
import functools

import jax
import jax.numpy as jnp
from jax import lax
from jax.experimental import pallas as pl
from jax.experimental.pallas import tpu as pltpu
from jax.sharding import PartitionSpec as P

G, H, L, NC = 7000, 800, 100, 4
EPSILON_NORM = 1e-05
KL_WEIGHT = 5e-05
F32, BF16 = jnp.float32, jnp.bfloat16
TN = ((0,), (0,))
NN = ((1,), (0,))
NT = ((1,), (1,))
HX = 816


def mm(left, right, dims):
    return lax.dot_general(left, right, (dims, ((), ())), preferred_element_type=F32)


def params_of(limit=56):
    return pltpu.CompilerParams(dimension_semantics=("arbitrary",), vmem_limit_bytes=limit * 2**20)


def output_kernel(part, block, scale, d_ref, a_ref, x_ref, p_ref, h_ref, reb, direct, dg, g_ref, sq, dscr):
    i = pl.program_id(0)
    cells = a_ref.shape[1]

    @pl.when(i == 0)
    def _():
        g_ref[...] = jnp.zeros_like(g_ref)
        sq[...] = jnp.zeros_like(sq)

    lim = G - i * block
    for j in range(block // part):
        r = slice(j * part, (j + 1) * part)
        inside = lax.broadcasted_iota(jnp.int32, (part, 1), 0) + j * part < lim
        w = d_ref[:, r]
        out = mm(w, a_ref[...], TN)
        mask = jnp.where(inside, mm(p_ref[:, r], h_ref[...], TN), 0.0)
        t = jnp.exp(-jnp.abs(out))
        one = 1.0 + t
        soft = jnp.maximum(out, 0.0) + jnp.where(t < 1e-3, t - 0.5 * t * t, jnp.log(one))
        reb[r, :] = soft.astype(BF16)
        res = jnp.where(mask > 0.0, soft - x_ref[r, :].astype(F32), 0.0)
        sq[...] += jnp.sum((res * res).reshape(part // 8, 8, cells), axis=0)
        dr = scale[0] * res
        direct[r, :] = dr.astype(BF16)
        d = (dr * (jnp.where(out >= 0.0, 1.0, t) / one)).astype(BF16)
        lane = lax.broadcasted_iota(jnp.int32, (1, part), 1) + j * part < lim
        dscr[r, :] = d
    lane = lax.broadcasted_iota(jnp.int32, (1, block), 1) < lim
    dg[...] = mm(a_ref[...], dscr[...], NT).astype(BF16)
    g_ref[...] += mm(jnp.where(lane, d_ref[...], jnp.zeros((), BF16)), dscr[...], NN)


def output_layer(D, act, x, panels, hot, scale, block=1024, part=256):
    cells = x.shape[1]
    n = pl.cdiv(G, block)
    rows = lambda: pl.BlockSpec((block, cells), lambda i: (i, 0))
    whole = lambda r, c: pl.BlockSpec((r, c), lambda i: (0, 0))
    return pl.pallas_call(
        functools.partial(output_kernel, part, block),
        grid=(n,),
        out_shape=(jax.ShapeDtypeStruct((G, cells), BF16), jax.ShapeDtypeStruct((G, cells), BF16),
                   jax.ShapeDtypeStruct((HX, G), BF16), jax.ShapeDtypeStruct((HX, cells), F32),
                   jax.ShapeDtypeStruct((8, cells), F32)),
        in_specs=[pl.BlockSpec(memory_space=pltpu.SMEM), pl.BlockSpec((HX, block), lambda i: (0, i)), whole(HX, cells),
                  rows(), pl.BlockSpec((NC, block), lambda i: (0, i)), whole(NC, cells)],
        out_specs=[rows(), rows(), pl.BlockSpec((HX, block), lambda i: (0, i)), whole(HX, cells), whole(8, cells)],
        scratch_shapes=[pltpu.VMEM((block, cells), BF16)],
        compiler_params=params_of(),
        cost_estimate=pl.CostEstimate(flops=6 * G * H * cells, bytes_accessed=70_000_000, transcendentals=3 * G * cells),
        name="output_layer",
    )(scale.reshape(1), D, act, x, panels, hot)


def first_rows_kernel(block, w_ref, x_ref, o_ref):
    i = pl.program_id(0)

    @pl.when(i == 0)
    def _():
        o_ref[...] = jnp.zeros_like(o_ref)

    inside = lax.broadcasted_iota(jnp.int32, (block, 1), 0) < G - i * block
    zero = jnp.zeros((), BF16)

    @pl.when((i + 1) * block <= G)
    def _():
        o_ref[...] += mm(w_ref[...], x_ref[...], TN)

    @pl.when((i + 1) * block > G)
    def _():
        o_ref[...] += mm(jnp.where(inside, w_ref[...], zero), jnp.where(inside, x_ref[...], zero), TN)


def first_linear(F, x, block=1024):
    cells = x.shape[1]
    return pl.pallas_call(
        functools.partial(first_rows_kernel, block),
        grid=(pl.cdiv(G, block),),
        out_shape=jax.ShapeDtypeStruct((H, cells), F32),
        in_specs=[pl.BlockSpec((block, H), lambda i: (i, 0)), pl.BlockSpec((block, cells), lambda i: (i, 0))],
        out_specs=pl.BlockSpec((H, cells), lambda i: (0, 0)),
        compiler_params=params_of(),
        cost_estimate=pl.CostEstimate(flops=2 * G * H * cells, bytes_accessed=30_000_000, transcendentals=0),
        name="first_linear",
    )(F, x)


def last_kernel(x_ref, w_ref, d_ref, t_ref, fg, gc):
    fg[...] = mm(x_ref[...], d_ref[...], NT).astype(BF16)
    gc[...] = (mm(w_ref[...], d_ref[...], NN) - t_ref[...].astype(F32)).astype(BF16)


def last_layer(x, F, d1, direct, frows, block=512):
    cells = x.shape[1]
    rows = lambda c: pl.BlockSpec((block, c), lambda i: (i, 0))
    return pl.pallas_call(
        last_kernel,
        grid=(pl.cdiv(G, block),),
        out_shape=(jax.ShapeDtypeStruct((frows, H), BF16), jax.ShapeDtypeStruct((G, cells), BF16)),
        in_specs=[rows(cells), rows(H), pl.BlockSpec((H, cells), lambda i: (0, 0)), rows(cells)],
        out_specs=[rows(H), rows(cells)],
        compiler_params=params_of(),
        cost_estimate=pl.CostEstimate(flops=4 * G * H * cells, bytes_accessed=70_000_000, transcendentals=0),
        name="last_layer",
    )(x, F, d1, direct)


MESH = pl.DeviceIdType.MESH
FROWS, DROWS = 496, 64
NF = 18
SHARD = 397952
FLATF = 7126600
ALL = (0, 1, 2)


def d_unit(s):
    v = lax.shift_right_arithmetic(908 * (s - 19) + 1252, 8)
    return jnp.where(s <= NF, 0, v)


def place():
    w, n = lax.axis_index("wide"), lax.axis_index("narrow")
    return w // 2, w % 2, n // 2, n % 2


def dev(z, x, y, c):
    return (z * 2 + x, y * 2 + c)


def index(z, x, y, c):
    return (z * 2 + x) * 4 + y * 2 + c


def grd(cond, guard, fn):
    pl.when(cond if guard is None else jnp.logical_and(cond, guard))(fn)


def four(s):
    return lax.bitwise_and(lax.shift_right_arithmetic(0x355b, jnp.clip(s - NF, 0, 13)), 1) == 1


def greet(z, x, y, c, extra=()):
    bar = pltpu.get_barrier_semaphore()
    sig = lambda d: pl.semaphore_signal(bar, inc=1, device_id=d, device_id_type=MESH)
    for d in extra:
        sig(d)
    sig(dev(z, 1 - x, y, c))
    sig(dev(z, x, 1 - y, c))
    sig(dev(z, x, y, 1 - c))

    @pl.when(z > 0)
    def _():
        sig(dev(z - 1, x, y, c))

    @pl.when(z < 3)
    def _():
        sig(dev(z + 1, x, y, c))
    pl.semaphore_wait(bar, len(extra) + 3 + (z > 0).astype(jnp.int32) + (z < 3).astype(jnp.int32))


class Spread:
    def __init__(self, kind, own, buf, send, recv, base=0):
        self.kind, self.own, self.buf, self.send, self.recv = kind, own, buf, send, recv
        self.place = z, x, y, c = place()
        self.sems, self.base, self.started = {}, base, []
        self.XP, self.YP, self.CP = (z, 1 - x, y, c), (z, x, 1 - y, c), (z, x, y, 1 - c)
        self.UP, self.DN = (z + 1, x, y, c), (z - 1, x, y, c)
        self.tags = {0: (0, z, None)}
        for t in (1, 2, 3):
            self.tags[2 * t] = (2 * t, z - t, z >= t)
            self.tags[2 * t + 1] = (2 * t + 1, z + t, z + t <= 3)

    def pieces(self, s, p):
        if self.kind == "F":
            return [] if p == 2 else [(s < NF, FROWS * s, (0, 240)[p], (240, 256)[p])]
        return [(None, 16 * d_unit(s), (0, 32, 48)[p], (32, 16, 16)[p])]

    def rows(self, s, p):
        for cond, base, off, n in self.pieces(s, p):
            yield cond, self.buf.at[pl.ds(pl.multiple_of(base + off, 16), n)], self.own.at[pl.ds(off, n)]

    def copy(self, s, p, key, target, local=False):
        k = self.base + self.sems.setdefault((key, p), len(self.sems))
        (_, dst, own), = self.rows(s, p)
        return pltpu.make_async_remote_copy(src_ref=own if local else dst, dst_ref=dst, send_sem=self.send.at[k],
                                            recv_sem=self.recv.at[k], device_id=dev(*target), device_id_type=MESH)

    def where(self, s, guard, fn):
        def last():
            fn((2,))

        def both():
            fn((0, 1))
            if self.kind == "D":
                pl.when(four(s))(last)
        grd(s < NF if self.kind == "F" else s >= NF, guard, both)

    def sends(self, s, guard, legs, local=False):
        def start(what, ps):
            for p in ps:
                for parts, key, target, more in legs:
                    if p in parts:
                        fn = getattr(self.copy(s, p, key, target, local), what)
                        fn() if more is None else pl.when(more)(fn)
        self.started.append((s, guard, functools.partial(start, "wait_send")))
        return functools.partial(start, "start")

    def gets(self, s, parts, key, target, more=None):
        def wait(ps):
            for p in ps:
                if p in parts:
                    fn = self.copy(s, p, key, target).wait_recv
                    fn() if more is None else pl.when(more)(fn)
        return wait

    def begin(self, loc, planes=True, names="ud"):
        z, x, y, c = self.place
        me = index(*self.place)
        fs = [self.sends(me, None, [(ALL, (name, 1), *((self.UP, z < 3) if name == "u" else (self.DN, z > 0)))], True) for name in names]
        fs += [self.planes(0, True)] if planes else []
        self.where(me, None, lambda ps: [f(ps) for f in fs])

        def start(what, ps):
            for p in ps:
                (_, dst, own), = self.rows(me, p)
                getattr(pltpu.make_async_copy(own, dst, loc.at[p]), what)()
        self.kept = lambda: self.where(me, None, functools.partial(start, "wait"))
        self.where(me, None, functools.partial(start, "start"))

    def own_in_place(self):
        self.kept()

    def planes(self, tag, local=False):
        _, zz, guard = self.tags[tag]
        z, x, y, c = self.place
        s = index(zz, x, y, c)
        return self.sends(s, guard, [(ALL, ("x", tag), self.XP, None), (ALL, ("y", tag), self.YP, None),
                                     (ALL, ("c0", tag), self.CP, None)], local)

    def along_z(self, t):
        z, x, y, c = self.place
        for name in "ud":
            tag = 2 * t + (name == "d")
            _, zz, ok = self.tags[tag]
            frm, to, more = (self.DN, self.UP, z < 3) if name == "u" else (self.UP, self.DN, z > 0)
            s = index(zz, x, y, c)
            fs = [self.sends(s, ok, [(ALL, (name, t + 1), to, more)])] if t < 3 else []
            fs.append(self.planes(tag))
            get = self.gets(s, ALL, (name, t), frm)

            def fn(ps):
                for p in ps:
                    get((p,))
                    for f in fs:
                        f((p,))
            self.where(s, ok, fn)

    def flat_parts(self, tag):
        _, zz, guard = self.tags[tag]
        if tag == 0:
            return (guard, guard)
        even = lax.rem(zz + 4, 2) == 0
        return jnp.logical_and(guard, even), jnp.logical_and(guard, jnp.logical_not(even))

    def cross(self, tag):
        _, zz, guard = self.tags[tag]
        z, x, y, c = self.place
        second, half = self.flat_parts(tag)
        for s, name, frm, parts, leg, cond, core in (
                (index(zz, 1 - x, y, c), "x", self.XP, (1, 2), ("xy", tag, self.YP), second, "c1"),
                (index(zz, x, 1 - y, c), "y", self.YP, (0,), ("yx", tag, self.XP), half, "c2")):
            get = self.gets(s, ALL, (name, tag), frm)
            send = self.sends(s, guard, [(parts, leg[:2], leg[2], cond), (ALL, (core, tag), self.CP, None)])

            def fn(ps):
                get(ps)
                send(ps)
            self.where(s, guard, fn)

    def diag(self, tag):
        _, zz, guard = self.tags[tag]
        z, x, y, c = self.place
        sd = index(zz, 1 - x, 1 - y, c)
        second, half = self.flat_parts(tag)
        t, name = tag // 2, "ud"[tag % 2]
        both = lambda a, b: b if a is None else jnp.logical_and(a, b)
        gets, legs = [], []
        if tag:
            frm, to, more = (self.DN, self.UP, z < 3) if name == "u" else (self.UP, self.DN, z > 0)
            gets = [self.gets(sd, (0,), ("g" + name, t), frm, second), self.gets(sd, (1, 2), ("g" + name, t), frm, half)]
            if t < 3:
                legs = [((0,), ("g" + name, t + 1), to, both(second, more)), ((1, 2), ("g" + name, t + 1), to, both(half, more))]
        else:
            even = lax.rem(z, 2) == 0
            odd = jnp.logical_not(even)
            for name, to, more in (("u", self.UP, z < 3), ("d", self.DN, z > 0)):
                legs += [((0,), ("g" + name, 1), to, both(even, more)), ((1, 2), ("g" + name, 1), to, both(odd, more))]
        gets += [self.gets(sd, (1, 2), ("xy", tag), self.YP, second), self.gets(sd, (0,), ("yx", tag), self.XP, half)]
        send = self.sends(sd, guard, legs + [(ALL, ("c3", tag), self.CP, None)])

        def fn(ps):
            for get in gets:
                get(ps)
            send(ps)
        self.where(sd, guard, fn)

    def core(self, tag, i):
        _, zz, guard = self.tags[tag]
        z, x, y, c = self.place
        xx, yy = ((x, y), (1 - x, y), (x, 1 - y), (1 - x, 1 - y))[i]
        s = index(zz, xx, yy, 1 - c)
        self.where(s, guard, self.gets(s, ALL, ("c%d" % i, tag), self.CP))

    def end(self):
        for s, guard, fn in self.started:
            self.where(s, guard, fn)


def first_kernel(fs, x_hbm, ds, F, D, lin, fv, xv, send, recv, loc, fsem, xsem, dsend, drecv, dloc):
    z, x, y, c = place()
    xcopy = pltpu.make_async_copy(x_hbm, xv, xsem)
    xcopy.start()
    net = Spread("F", fs, fv, send, recv)
    late = Spread("D", ds, D, dsend, drecv)
    greet(z, x, y, c)
    net.begin(loc)
    late.begin(dloc)
    lin[...] = jnp.zeros_like(lin)
    out = []

    def store(s, k, guard):
        r = pl.ds(pl.multiple_of(FROWS * s, 16), FROWS)
        cp = pltpu.make_async_copy(fv.at[r], F.at[r], fsem.at[k])
        grd(s < NF, guard, cp.start)
        out.append((s < NF, guard, cp))

    def times(tag, i):
        _, zz, guard = net.tags[tag]
        xx, yy = ((x, y), (1 - x, y), (x, 1 - y), (1 - x, 1 - y))[i]
        m = (zz * 2 + xx) * 2 + yy

        def whole():
            r = pl.ds(pl.multiple_of(2 * FROWS * m, 16), 2 * FROWS)
            lin[...] += mm(fv[r, :], xv[r, :], TN)

        def rest():
            r = pl.ds(14 * FROWS, G - 14 * FROWS)
            lin[...] += mm(fv[r, :], xv[r, :], TN)
        grd(m < 7, guard, whole)
        grd(m == 7, guard, rest)
        k = 8 * tag + 2 * i
        store(2 * m, k, guard)
        store(2 * m + 1, k + 1, guard)

    def finish(tag, cols):
        for i in cols:
            net.core(tag, i)
            times(tag, i)

    def both(name, *tags):
        for n in (net, late):
            for tag in tags:
                getattr(n, name)(tag)

    def settle(tag, cols):
        for i in cols:
            late.core(tag, i)

    both("along_z", 1)
    both("cross", 0)
    both("along_z", 2)
    both("diag", 0)
    both("cross", 2, 3)
    net.own_in_place()
    late.own_in_place()
    xcopy.wait()
    finish(0, (0, 1, 2, 3))
    both("along_z", 3)
    both("diag", 2, 3)
    both("cross", 4, 5)
    finish(2, (0, 1, 2))
    finish(3, (0, 1, 2))
    both("diag", 4, 5)
    both("cross", 6, 7)
    finish(2, (3,))
    finish(3, (3,))
    finish(4, (0, 1, 2))
    finish(5, (0, 1, 2))
    both("diag", 6, 7)
    for tag in (4, 5):
        finish(tag, (3,))
    for tag in (6, 7):
        finish(tag, (0, 1, 2, 3))
    for tag in (0, 2, 3, 4, 5, 6, 7):
        settle(tag, (0, 1, 2, 3))
    net.end()
    late.end()
    for cond, guard, cp in out:
        grd(cond, guard, cp.wait)


def spread_and_first(fslot, dslot, x, cid=1):
    cells = x.shape[1]
    V = pltpu.VMEM
    return pl.pallas_call(
        first_kernel,
        out_shape=(jax.ShapeDtypeStruct((FROWS * NF, H), BF16), jax.ShapeDtypeStruct((HX, G), BF16), jax.ShapeDtypeStruct((H, cells), F32)),
        in_specs=[pl.BlockSpec(memory_space=pl.ANY)] * 3,
        out_specs=[pl.BlockSpec(memory_space=pl.ANY)] * 2 + [pl.BlockSpec(memory_space=V)],
        scratch_shapes=[V((FROWS * NF, H), BF16), V((G, cells), BF16), pltpu.SemaphoreType.DMA((128,)), pltpu.SemaphoreType.DMA((128,)),
                        pltpu.SemaphoreType.DMA((3,)), pltpu.SemaphoreType.DMA((64,)), pltpu.SemaphoreType.DMA,
                        pltpu.SemaphoreType.DMA((192,)), pltpu.SemaphoreType.DMA((192,)), pltpu.SemaphoreType.DMA((3,))],
        compiler_params=pltpu.CompilerParams(collective_id=cid, has_side_effects=True, vmem_limit_bytes=58 * 2**20),
        name="spread_and_first",
    )(fslot, x, dslot)


def slots(p):
    n = 32
    me = lax.axis_index("wide") * 4 + lax.axis_index("narrow")
    ax = ("wide", "narrow")
    head = lax.ppermute(p[-36864:], ax, [(i, i + 1) for i in range(n - 1)])
    tail = lax.ppermute(p[:112000], ax, [(i + 1, i) for i in range(n - 1)])
    ext = jnp.concatenate([head, p, tail, jnp.zeros((112000,), p.dtype)])
    f = lax.dynamic_slice(ext, (jnp.maximum(36864 - 1152 * me, 0),), (FROWS * 800,)).reshape(FROWS, 800)
    off = 36864 + FLATF + 112000 * d_unit(me) - SHARD * me
    d = lax.dynamic_slice(ext, (jnp.clip(off, 0, ext.shape[0] - DROWS * 7000),), (DROWS * 7000,)).reshape(DROWS, 7000)
    return f, d

LP = 128
STEP, UNROLL = 32, 5


def rows_loop(n, fn, step=STEP, unroll=UNROLL):
    def body(i, _):
        for j in range(unroll):
            fn(pl.ds(pl.multiple_of((i * unroll + j) * step, step), step))
        return 0
    lax.fori_loop(0, n // (step * unroll), body, 0)


def silu(u):
    return u * (0.5 + 0.5 * jnp.tanh(0.5 * u))


def by_lanes(v):
    return sum(v[:, 128 * i:128 * i + 128] for i in range(v.shape[1] // 128))


def over_rows(buf):
    return jnp.sum(jnp.transpose(buf), axis=0, keepdims=True)


def along_rows(row):
    return jnp.transpose(jnp.broadcast_to(row, (128, 896)))


def wide(col, cells):
    return jnp.concatenate([col] * (cells // 128), axis=1)


class Sums:
    def __init__(self, bufs, sems):
        self.bufs, self.sems, self.turn = bufs, sems, 0
        self.place = z, x, y, c = place()
        self.spot = x * 4 + y * 2 + c
        self.inside = [(k, lax.bitwise_xor(self.spot, k)) for k in range(1, 8)]
        self.planes = [(k, lax.bitwise_xor(z, k)) for k in range(1, 4)]

    def near_dev(self, q):
        return dev(self.place[0], q // 4, (q // 2) % 2, q % 2)

    def far_dev(self, q):
        return dev(q, *self.place[1:])

    def others(self):
        return [self.near_dev(q) for k, q in self.inside] + [self.far_dev(q) for k, q in self.planes]

    def __call__(self, kind, value, between=None, after=None):
        near, far = self.bufs[kind]
        i, t = self.turn, self.sems
        self.turn += 1
        j = self.count[kind] = self.count.get(kind, -1) + 1 if hasattr(self, "count") else self.first(kind)
        s, f = near.at[j], far.at[j]
        s[self.spot] = value
        cps = [pltpu.make_async_remote_copy(src_ref=s.at[self.spot], dst_ref=s.at[self.spot], send_sem=t[0].at[i, k], recv_sem=t[1].at[i, k],
                                            device_id=self.near_dev(q), device_id_type=MESH) for k, q in self.inside]
        for cp in cps:
            cp.start()
        if between:
            between()
        for cp in cps:
            cp.wait_recv()
        z = self.place[0]
        f[z] = jnp.sum(s[...], axis=0)
        cpz = [pltpu.make_async_remote_copy(src_ref=f.at[z], dst_ref=f.at[z], send_sem=t[2].at[i, k], recv_sem=t[3].at[i, k],
                                            device_id=self.far_dev(q), device_id_type=MESH) for k, q in self.planes]
        for cp in cpz:
            cp.start()
        for cp in cps:
            cp.wait_send()
        if after:
            after()
        for cp in cpz:
            cp.wait()
        return jnp.sum(f[...], axis=0)

    def first(self, kind):
        self.count = {}
        return 0


def sums_scratch(stats, tables):
    V = pltpu.VMEM
    n = stats + tables
    dma = pltpu.SemaphoreType.DMA
    return [V((stats, 8, 2, 896), F32), V((stats, 4, 2, 896), F32), V((max(tables, 1), 8, 8, 128), F32), V((max(tables, 1), 4, 8, 128), F32),
            dma((n, 8)), dma((n, 8)), dma((n, 4)), dma((n, 4))]


def forward_kernel(total, lin1, w2, wh, wd1, wd2, grows, bh, hot, eps,
                   act1o, act2o, act3o, ends, heads, latent, lin2o, lin3o, lin4, stat, table,
                   act1, act2, act3, lin2, lin3, osem, bufs, square, n1, f1, n2, f2, a1, a2, a3, a4):
    z, x, y, c = place()
    sums = Sums({"stat": (n1, f1), "table": (n2, f2)}, (a1, a2, a3, a4))
    cells = lin1.shape[1]
    for i in range(2):
        bufs[i, pl.ds(H, 96), :] = jnp.zeros((96, 128), F32)
    square[...] = jnp.zeros_like(square)
    greet_all(sums.others())

    def stats(lin):
        def one(r):
            v = lin[r, :]
            bufs[0, r, :] = by_lanes(v)
            bufs[1, r, :] = by_lanes(v * v)
        rows_loop(H, one)
        return jnp.concatenate([over_rows(bufs[0]), over_rows(bufs[1])])

    def norm(k, lin, out, between=None, after=None):
        t = sums("stat", stats(lin), between, after)
        centre = t[0:1, :] / total
        inverse = lax.rsqrt(t[1:2, :] / total - centre * centre + EPSILON_NORM)
        stat[pl.ds(2 * k, 1), :] = centre
        stat[pl.ds(2 * k + 1, 1), :] = inverse
        scale = inverse * grows[2 * k:2 * k + 1, :]
        bufs[0] = along_rows(scale)
        bufs[1] = along_rows(grows[2 * k + 1:2 * k + 2, :] - centre * scale)

        def one(r):
            out[r, :] = silu(lin[r, :] * wide(bufs[0, r, :], cells) + wide(bufs[1, r, :], cells)).astype(BF16)
        rows_loop(H, one)

    leaving = []

    def leave(src, dst):
        cp = pltpu.make_async_copy(src, dst, osem.at[len(leaving)])
        cp.start()
        leaving.append(cp)

    norm(0, lin1, act1)
    lin2[...] = mm(w2[...], act1[...], TN)
    leave(act1, act1o)
    leave(lin2, lin2o)
    norm(1, lin2, act2)
    leave(act2, act2o)
    h = (mm(wh[...], act2[...], TN) + bh[...]).astype(BF16)
    heads[...] = h
    mu, lv = h[:LP].astype(F32), h[LP:].astype(F32)
    part = mm(hot[...], h[:LP], NT)
    hf = hot[...].astype(F32)
    lane = lax.broadcasted_iota(jnp.int32, (NC, LP), 1)
    top = jnp.where(lane == LP - 1, jnp.sum(hf, axis=1, keepdims=True), part)
    kl = jnp.sum(jnp.sum(1.0 + lv - mu * mu - jnp.exp(lv), axis=0, keepdims=True), axis=1, keepdims=True)
    low = jnp.where(lax.broadcasted_iota(jnp.int32, (4, LP), 0) == 0, kl, 0.0)

    t = sums("table", jnp.concatenate([top, low]))
    table[...] = t
    cond = t[0:NC, :]
    counts = cond[:, LP - 1:LP]
    cond = jnp.where(lane == LP - 1, 0.0, cond)
    off = cond / counts - jnp.sum(cond, axis=0, keepdims=True) / total
    square[pl.ds(0, NC), :] = off
    offc = jnp.transpose(square[...])
    chosen = sum(offc[:, i:i + 1] * hf[i:i + 1, :] for i in range(NC))
    lat = (mu + jnp.exp(0.5 * lv) * eps[...].astype(F32) - chosen).astype(BF16)
    latent[...] = lat
    lin3[...] = mm(wd1[...], latent[...], TN)
    leave(lin3, lin3o)
    norm(2, lin3, act3)
    leave(act3, act3o)
    lin4[...] = mm(wd2[...], act3[...], TN)

    norm(3, lin4, ends)
    ends[pl.ds(H, 16), :] = jnp.where(lax.broadcasted_iota(jnp.int32, (16, ends.shape[1]), 0) == 0, 1.0, 0.0).astype(BF16)
    for cp in leaving:
        cp.wait()


def greet_all(devices):
    bar = pltpu.get_barrier_semaphore()
    for d in devices:
        pl.semaphore_signal(bar, inc=1, device_id=d, device_id_type=MESH)
    pl.semaphore_wait(bar, len(devices))


def hidden_layers(total, lin1, w2, wh, wd1, wd2, grows, bh, hot, eps, cid=2):
    cells = lin1.shape[1]
    V = pltpu.VMEM
    vm = pl.BlockSpec(memory_space=V)
    hbm = pl.BlockSpec(memory_space=pl.ANY)
    S = jax.ShapeDtypeStruct
    return pl.pallas_call(
        functools.partial(forward_kernel, total),
        out_shape=(S((H, cells), BF16), S((H, cells), BF16), S((H, cells), BF16), S((HX, cells), BF16), S((2 * LP, cells), BF16),
                   S((LP, cells), BF16), S((H, cells), F32), S((H, cells), F32), S((H, cells), F32), S((8, 896), F32),
                   S((8, LP), F32)),
        in_specs=[vm] * 9,
        out_specs=[hbm] * 3 + [vm] * 3 + [hbm] * 2 + [vm] * 3,
        scratch_shapes=[*[V((H, cells), BF16)] * 3, *[V((H, cells), F32)] * 2, pltpu.SemaphoreType.DMA((8,)), V((2, 896, 128), F32), V((LP, LP), F32), *sums_scratch(4, 1)],
        compiler_params=pltpu.CompilerParams(collective_id=cid, has_side_effects=True, vmem_limit_bytes=58 * 2**20),
        name="hidden_layers",
    )(lin1, w2, wh, wd1, wd2, grows, bh, hot, eps)


def backward_kernel(total, g4, lin4, w2, wh, wd1, wd2, grows, stat, latent, heads, hot, eps, table, squares, act1i, act2i, act3i, lin1i, lin2i, lin3i,
                    d1, tail, sums2,
                    gnorm, rows, upper, lower, gwh, gwl, act1, act2, act3, lin1, lin2, lin3, isem, pbuf, dbuf, hbuf, bufs, part, square, n1, f1, n2, f2, a1, a2, a3, a4):
    cells = lin4.shape[1]
    sums = Sums({"stat": (n1, f1), "table": (n2, f2)}, (a1, a2, a3, a4))
    comes = {}
    for i, (name, src, dst) in enumerate((("lin3", lin3i, lin3), ("act3", act3i, act3), ("lin2", lin2i, lin2), ("act2", act2i, act2),
                                          ("lin1", lin1i, lin1), ("act1", act1i, act1))):
        comes[name] = pltpu.make_async_copy(src, dst, isem.at[i])
        comes[name].start()
    for i in range(2):
        part[i, pl.ds(H, 96), :] = jnp.zeros((96, 128), F32)
    square[...] = jnp.zeros_like(square)
    for buf in (upper, lower):
        buf[pl.ds(0, 8), :] = jnp.zeros((8, 896), F32)
        buf[pl.ds(904, 8), :] = jnp.zeros((8, 896), F32)
    rows[pl.ds(1904, 32), :] = jnp.zeros((32, 896), F32)
    greet_all(sums.others())

    def keep(r, v):
        upper[pl.ds(r + 4, v.shape[0]), pl.ds(0, H)] = v
        lower[pl.ds(r + 5, v.shape[0]), pl.ds(0, H)] = v

    def turned(v, places):
        lane = lax.broadcasted_iota(jnp.int32, v.shape, 1)
        return sum(jnp.where(jnp.logical_and(lane >= to, lane < to + stop - start), pltpu.roll(v, (to - start) % 896, 1), 0.0)
                   for start, stop, to in places)

    def padded(v):
        return jnp.concatenate([v, jnp.zeros((v.shape[0], 896 - v.shape[1]), F32)], axis=1)

    def pack():
        keep(100, gnorm[5:6, pl.ds(0, H)])
        keep(101, gnorm[4:5, pl.ds(0, H)])
        keep(902, gnorm[7:8, pl.ds(0, H)])
        keep(903, gnorm[6:7, pl.ds(0, H)])

        def bend(r):
            lane = lax.broadcasted_iota(jnp.int32, (16, 896), 1)
            rows[pl.ds(pl.multiple_of(1000 + r.start, 8), 16), :] = jnp.where(
                lane < 200, pltpu.roll(lower[r, :], 296, 1), pltpu.roll(upper[r, :], 200, 1))
        rows_loop(912, bend, 16, 3)
        acc = 0.0
        for i in range(4):
            for j, half in enumerate((gwh, gwl)):
                acc = acc + turned(padded(half[pl.ds(i, 200, stride=4), :]), ((0, L, 200 * i + L * j),))
        rows[pl.ds(804, 200), :] = acc
        rows[pl.ds(802, 1), :] = gnorm[3:4, :]
        rows[pl.ds(803, 1), :] = gnorm[2:3, :]

    def norm(k, g, lin, out, between=None):
        centre, inverse = stat[2 * k:2 * k + 1, :], stat[2 * k + 1:2 * k + 2, :]
        gain, shift = grows[2 * k:2 * k + 1, :], grows[2 * k + 1:2 * k + 2, :]
        bufs[0] = along_rows(inverse)
        bufs[1] = along_rows(-centre * inverse)
        bufs[2] = along_rows(gain)
        bufs[3] = along_rows(shift)

        def one(r):
            n = lin[r, :] * wide(bufs[0, r, :], cells) + wide(bufs[1, r, :], cells)
            u = n * wide(bufs[2, r, :], cells) + wide(bufs[3, r, :], cells)
            s = 0.5 + 0.5 * jnp.tanh(0.5 * u)
            p = g[r, :] * s * (1.0 + u * (1.0 - s))
            pbuf[r, :] = p
            part[0, r, :] = by_lanes(p)
            part[1, r, :] = by_lanes(p * n)
        rows_loop(H, one)
        local = jnp.concatenate([over_rows(part[0]), over_rows(part[1])])
        gnorm[pl.ds(2 * k, 2), :] = local
        t = sums("stat", local, between)
        a = gain * inverse
        b = -a * t[1:2, :] / total
        bufs[0] = along_rows(a)
        bufs[1] = along_rows(b * inverse)
        bufs[2] = along_rows(-b * centre * inverse - a * t[0:1, :] / total)

        def two(r):
            out[r, :] = (pbuf[r, :] * wide(bufs[0, r, :], cells) + lin[r, :] * wide(bufs[1, r, :], cells)
                         + wide(bufs[2, r, :], cells)).astype(BF16)
        rows_loop(H, two)

    norm(3, g4, lin4, dbuf)
    pbuf[...] = mm(wd2[...], dbuf[...], NN)
    comes["lin3"].wait()
    comes["act3"].wait()

    def grads4():
        keep(102, mm(act3[...], dbuf[...], NT))
    norm(2, pbuf, lin3, hbuf, grads4)
    dl = mm(wd1[...], hbuf[...], NN).astype(BF16)
    cond = mm(hot[...], dl, NT)
    sq = jnp.sum(jnp.sum(squares[...], axis=0, keepdims=True), axis=1, keepdims=True)
    low = jnp.where(lax.broadcasted_iota(jnp.int32, (4, LP), 0) == 0, sq, 0.0)

    def grads3():
        keep(0, mm(latent[...], hbuf[...], NT)[:L])
    t = sums("table", jnp.concatenate([cond, low]), grads3)
    sums2[...] = t
    cond = t[0:NC, :]
    counts = table[0:NC, LP - 1:LP]
    square[pl.ds(0, NC), :] = jnp.sum(cond, axis=0, keepdims=True) / total - cond / counts
    take = jnp.transpose(square[...])
    hf = hot[...].astype(F32)
    change = sum(take[:, i:i + 1] * hf[i:i + 1, :] for i in range(NC))
    mu, lv = heads[pl.ds(0, LP), :].astype(F32), heads[pl.ds(LP, LP), :].astype(F32)
    dl = dl.astype(F32)
    dh = jnp.concatenate([
        dl + change + (KL_WEIGHT / total) * mu,
        0.5 * dl * jnp.exp(0.5 * lv) * eps[...].astype(F32) + (0.5 * KL_WEIGHT / total) * (jnp.exp(lv) - 1.0)]).astype(BF16)
    dbuf[pl.ds(0, 2 * LP), :] = dh
    bias = padded(mm(jnp.ones((8, cells), BF16), dh, NT))
    lower[pl.ds(4, 1), :] = turned(bias, ((0, L, 600), (LP, LP + L, 700)))[0:1]
    pbuf[...] = mm(wh[...], dh, NN)
    comes["lin2"].wait()
    comes["act2"].wait()

    def grads2():
        g = mm(act2[...], dbuf[pl.ds(0, 2 * LP), :], NT)
        gwh[...] = g[:, :LP]
        gwl[...] = g[:, LP:]
    norm(1, pbuf, lin2, hbuf, grads2)
    pbuf[...] = mm(w2[...], hbuf[...], NN)
    comes["lin1"].wait()
    comes["act1"].wait()

    def grads1():
        rows[pl.ds(2, H), pl.ds(0, H)] = mm(act1[...], hbuf[...], NT)
        pack()
    norm(0, pbuf, lin1, d1, grads1)
    rows[pl.ds(0, 1), :] = gnorm[1:2, :]
    rows[pl.ds(1, 1), :] = gnorm[0:1, :]

    def out(r):
        tail[r, :] = rows[r, pl.ds(0, H)].astype(BF16)
    rows_loop(1920, out, 16, 5)
    tail[pl.ds(1920, 16), :] = jnp.zeros((16, H), BF16)


def hidden_backward(total, g4, lin4, w2, wh, wd1, wd2, grows, stat, latent, heads, hot, eps, table, squares, acts, lins, cid=3):
    cells = lin4.shape[1]
    V = pltpu.VMEM
    vm = pl.BlockSpec(memory_space=V)
    hbm = pl.BlockSpec(memory_space=pl.ANY)
    S = jax.ShapeDtypeStruct
    return pl.pallas_call(
        functools.partial(backward_kernel, total),
        out_shape=(S((H, cells), BF16), S((1936, H), BF16), S((8, LP), F32)),
        in_specs=[vm] * 14 + [hbm] * 6,
        out_specs=[vm] * 3,
        scratch_shapes=[V((8, 896), F32), V((1936, 896), F32), V((912, 896), F32), V((912, 896), F32), V((H, LP), F32), V((H, LP), F32), *[V((H, cells), BF16)] * 3, *[V((H, cells), F32)] * 3, pltpu.SemaphoreType.DMA((6,)),
                        V((H, cells), F32), V((H, cells), BF16), V((H, cells), BF16),
                        V((4, 896, 128), F32), V((2, 896, 128), F32), V((LP, LP), F32), *sums_scratch(4, 1)],
        compiler_params=pltpu.CompilerParams(collective_id=cid, has_side_effects=True, vmem_limit_bytes=58 * 2**20),
        name="hidden_backward",
    )(g4, lin4, w2, wh, wd1, wd2, grows, stat, latent, heads, hot, eps, table, squares, *acts, *lins)


ZF, ZD = (0, 1, 2), (2, 3)

def reduce_kernel(FG, DG, fo, do, nf, pd, tF, tD, cF, cD, rF, rD, aF, aD, bF, bD, uF, uD, vF, vD, send, recv, loc, hsend, hrecv):
    z, x, y, c = place()
    XP, YP, CP = (z, 1 - x, y, c), (z, x, 1 - y, c), (z, x, y, 1 - c)
    UP, DN = (z + 1, x, y, c), (z - 1, x, y, c)
    me = index(z, x, y, c)
    numbered = lambda i: (lax.shift_right_arithmetic(i, 2), lax.bitwise_and(i, 3))
    before, after = numbered(jnp.maximum(me - 1, 0)), numbered(jnp.minimum(me + 1, 31))
    nf[...] = jnp.zeros_like(nf)
    pd[...] = jnp.zeros_like(pd)
    bar = pltpu.get_barrier_semaphore()
    sig = lambda d: pl.semaphore_signal(bar, inc=1, device_id=d, device_id_type=MESH)
    for d in (XP, YP, CP):
        sig(dev(*d))
    for cond, d in ((z > 0, dev(*DN)), (z < 3, dev(*UP)), (me > 0, before), (me < 31, after)):
        pl.when(cond)(functools.partial(sig, d))
    one = lambda cond: cond.astype(jnp.int32)
    pl.semaphore_wait(bar, 3 + one(z > 0) + one(z < 3) + one(me > 0) + one(me < 31))

    sems = {}
    def sem_index(key):
        return sems.setdefault(key, len(sems))
    started = []

    def cases(s, part):
        last = jnp.logical_and(s >= NF, four(s))
        f, d = s < NF, s >= NF
        if part == "all":
            return [(f, "F", 0, 496, 0), (d, "D", 0, 48, 0), (last, "D", 48, 16, 1)]
        if part == "a":
            return [(f, "F", 0, 240, 0), (d, "D", 0, 32, 0)]
        return [(f, "F", 240, 256, 0), (d, "D", 32, 16, 0), (last, "D", 48, 16, 1)]

    def land(pair, zz, b, col=None):
        buf = pair[0 if b == "F" else 1]
        zi = zz if b == "F" else zz - 2
        return buf.at[zi] if col is None else buf.at[col, zi]

    def grd(cond, guard, fn):
        pl.when(cond if guard is None else jnp.logical_and(cond, guard))(fn)

    def clampz(zz, b):
        return jnp.clip(zz, 0, 2) if b == "F" else jnp.clip(zz, 2, 3)

    def make(s, zz, part, key, target, src_of, dst_of):
        out = []
        for cond, b, off, rows, q in cases(s, part):
            k = sem_index((key, q))
            zc = clampz(zz, b)
            ref, base = src_of(b, zc)
            out.append((cond, pltpu.make_async_remote_copy(
                src_ref=ref.at[pl.ds(off if isinstance(base, int) else pl.multiple_of(base + off, 16), rows)],
                dst_ref=dst_of(b, zc)[0].at[pl.ds(off, rows)],
                send_sem=send.at[k], recv_sem=recv.at[k], device_id=dev(*target), device_id_type=MESH)))
        return out

    def go(guard, *a):
        for cond, cp in make(*a):
            grd(cond, guard, cp.start)
        started.append((guard, a))

    def got(guard, *a):
        for cond, cp in make(*a):
            grd(cond, guard, cp.wait_recv)

    def each(rows, off, fn):
        def body(i, _):
            fn(pl.ds(pl.multiple_of(off + 16 * i, 16), 16))
            return 0
        lax.fori_loop(0, rows // 16, body, 0)

    def total(s, guard, part, zz, dst, terms, out=None):
        for cond, b, off, rows, q in cases(s, part):
            zc = clampz(zz, b)
            def fn(b=b, off=off, rows=rows, zc=zc):
                refs = [t(b, zc)[0] for t in terms]
                def step(r):
                    v = refs[0][r, :].astype(jnp.float32)
                    for ref in refs[1:]:
                        v = v + ref[r, :].astype(jnp.float32)
                    if out is None:
                        dst(b, zc)[0][r, :] = v.astype(jnp.bfloat16)
                    else:
                        out[0 if b == "F" else 1][r, :] = v
                each(rows, off, step)
            grd(cond, guard, fn)

    C, R, A, B, U, V = (cF, cD), (rF, rD), (aF, aD), (bF, bD), (uF, uD), (vF, vD)
    cols = ((x, y), (1 - x, y), (x, 1 - y), (1 - x, 1 - y))
    tags = [(7, z - 3, z >= 3), (6, z + 3, z <= 0), (5, z - 2, z >= 2), (4, z + 2, z <= 1),
            (3, z - 1, z >= 1), (2, z + 1, z <= 2), (0, z, None)]

    def own_rows(s):
        return lambda b, zc: (FG, FROWS * s) if b == "F" else (DG, 16 * d_unit(s))
    on = lambda pair, col=None: (lambda b, zc: (land(pair, zc, b, col), 0))

    for tag, zz, guard in tags:
        for col in (3, 1, 2, 0):
            s = index(zz, *cols[col], 1 - c)
            go(guard, s, zz, "all", ("c", tag, col), CP, own_rows(s), on(C, col))

    order = [(tg, col) for tg in tags for col in (3, 1, 2, 0)]

    def load(k, what):
        (tag, zz, guard), col = order[k]
        s = index(zz, *cols[col], c)
        e = d_unit(s)
        for cond, b, off, rows, q in cases(s, "all"):
            src = FG.at[pl.ds(pl.multiple_of(FROWS * s + off, 16), rows)] if b == "F" else DG.at[pl.ds(pl.multiple_of(16 * e + off, 16), rows)]
            dst = (tF if b == "F" else tD).at[k % 2, pl.ds(off, rows)]
            cp = pltpu.make_async_copy(src, dst, loc.at[k % 2, q])
            grd(cond, guard, cp.start if what == "start" else cp.wait)

    def join(k):
        if k + 1 < len(order):
            load(k + 1, "start")
        load(k, "wait")
        (tag, zz, guard), col = order[k]
        s = index(zz, *cols[col], c)
        got(guard, s, zz, "all", ("c", tag, col), CP, own_rows(s), on(C, col))
        mine = lambda b, zc: ((tF if b == "F" else tD).at[k % 2], 0)
        total(s, guard, "all", zz, on(C, col), [on(C, col), mine])

    def first(i):
        tag, zz, guard = tags[i]
        join(4 * i)
        s = index(zz, *cols[3], c)
        go(guard, s, zz, "a", ("xa", tag), XP, on(C, 3), on(R, 1))
        go(guard, s, zz, "b", ("yb", tag), YP, on(C, 3), on(R, 0))
        for k in (1, 2, 3):
            join(4 * i + k)

    def second(i):
        tag, zz, guard = tags[i]
        sx, sy = index(zz, *cols[1], c), index(zz, *cols[2], c)
        got(guard, sx, zz, "b", ("yb", tag), YP, on(C, 3), on(R, 0))
        total(sx, guard, "b", zz, on(C, 1), [on(C, 1), on(R, 0)])
        go(guard, sx, zz, "all", ("X", tag), XP, on(C, 1), on(A))
        got(guard, sy, zz, "a", ("xa", tag), XP, on(C, 3), on(R, 1))
        total(sy, guard, "a", zz, on(C, 2), [on(C, 2), on(R, 1)])
        go(guard, sy, zz, "all", ("Y", tag), YP, on(C, 2), on(B))

    def third(i):
        tag, zz, guard = tags[i]
        s = index(zz, *cols[0], c)
        got(guard, s, zz, "all", ("X", tag), XP, on(C, 1), on(A))
        got(guard, s, zz, "all", ("Y", tag), YP, on(C, 2), on(B))
        t = {7: 3, 6: 3, 5: 2, 4: 2, 3: 1, 2: 1, 0: 0}[tag]
        base = [on(C, 0), on(A), on(B)]
        if t == 0:
            for cond, frm, pair, key in ((z < 3, UP, U, ("zd", 1)), (z > 0, DN, V, ("zu", 1))):
                got(cond, s, zz, "all", key, frm, on(C, 0), on(pair))
            inner = jnp.logical_and(z > 0, z < 3)
            total(s, inner, "all", zz, None, base + [on(U), on(V)], out=(fo, do))
            total(s, z == 0, "all", zz, None, base + [on(U)], out=(fo, do))
            total(s, z == 3, "all", zz, None, base + [on(V)], out=(fo, do))
            return
        down = tag in (7, 5, 3)
        to, frm, pair, name = (DN, UP, U, "zd") if down else (UP, DN, V, "zu")
        more = (z < 3) if down else (z > 0)
        if t < 3:
            got(jnp.logical_and(guard, more), s, zz, "all", (name, t + 1), frm, on(C, 0), on(pair))
            total(s, jnp.logical_and(guard, more), "all", zz, on(C, 0), base + [on(pair)])
            total(s, jnp.logical_and(guard, jnp.logical_not(more)), "all", zz, on(C, 0), base)
        else:
            total(s, guard, "all", zz, on(C, 0), base)
        go(guard, s, zz, "all", (name, t), to, on(C, 0), on(pair))

    @pl.when(me >= NF)
    def _(): fo[...] = jnp.zeros_like(fo)
    do[pl.ds(48, 16), :] = jnp.zeros((16, 7000), jnp.float32)
    @pl.when(me < NF)
    def _(): do[pl.ds(0, 48), :] = jnp.zeros((48, 7000), jnp.float32)
    load(0, "start")
    n = len(tags)
    for i in range(n + 2):
        if i < n:
            first(i)
        if 1 <= i <= n:
            second(i - 1)
        if i >= 2:
            third(i - 2)
    edge = lambda k, src, dst, to: pltpu.make_async_remote_copy(
        src_ref=src, dst_ref=dst, send_sem=hsend.at[k], recv_sem=hrecv.at[k], device_id=to, device_id_type=MESH)
    edges = [(jnp.logical_and(me >= 1, me < NF), me < NF - 1, edge(0, fo.at[pl.ds(0, 32)], nf, before)),
             (me == NF, me == NF - 1, edge(2, do.at[pl.ds(0, 16)], pd, before))]
    inner = jnp.logical_and(me >= NF, me < 31)
    edges += [(jnp.logical_and(inner, four(me)), jnp.logical_and(me > NF, four(me - 1)), edge(1, do.at[pl.ds(48, 16)], pd, after)),
              (jnp.logical_and(inner, jnp.logical_not(four(me))), jnp.logical_and(me > NF, jnp.logical_not(four(me - 1))),
               edge(1, do.at[pl.ds(32, 16)], pd, after))]
    for out, _, cp in edges:
        pl.when(out)(cp.start)
    for guard, a in started:
        for cond, cp in make(*a):
            grd(cond, guard, cp.wait_send)
    for out, into, cp in edges:
        pl.when(out)(cp.wait_send)
        pl.when(into)(cp.wait_recv)

def reduce(FG, DG, cid=2):
    B16 = jnp.bfloat16
    V = pltpu.VMEM
    pair = lambda *lead: [V(lead + (3, FROWS, 800), B16), V(lead + (2, DROWS, 7000), B16)]
    return pl.pallas_call(
        reduce_kernel,
        out_shape=(jax.ShapeDtypeStruct((FROWS, 800), jnp.float32), jax.ShapeDtypeStruct((DROWS, 7000), jnp.float32),
                   jax.ShapeDtypeStruct((32, 800), jnp.float32), jax.ShapeDtypeStruct((16, 7000), jnp.float32)),
        in_specs=[pl.BlockSpec(memory_space=pl.ANY)] * 2,
        out_specs=[pl.BlockSpec(memory_space=V)] * 4,
        scratch_shapes=[V((2, FROWS, 800), B16), V((2, DROWS, 7000), B16), *pair(4), *pair(2), *pair(), *pair(), *pair(), *pair(),
                        pltpu.SemaphoreType.DMA((192,)), pltpu.SemaphoreType.DMA((192,)), pltpu.SemaphoreType.DMA((2, 2)),
                        pltpu.SemaphoreType.DMA((3,)), pltpu.SemaphoreType.DMA((3,))],
        compiler_params=pltpu.CompilerParams(collective_id=cid, has_side_effects=True, vmem_limit_bytes=60 * 2**20),
        name="sum_gradients",
    )(FG, DG)

def flatten(fo, do, nf, pd):
    me = lax.axis_index("wide") * 4 + lax.axis_index("narrow")
    ff, nextf, edge = fo.reshape(-1), nf.reshape(-1)[:20800], pd.reshape(-1)
    a = lax.dynamic_slice(jnp.concatenate([ff, nextf]), (1152 * jnp.minimum(me, 16),), (SHARD,))
    b = jnp.concatenate([ff[19584:381000], edge[:36536]])
    off = 112000 - (112000 * d_unit(me) + FLATF - SHARD * me)
    c = lax.dynamic_slice(jnp.concatenate([edge, do.reshape(-1)]), (jnp.clip(off, 0, 560000 - SHARD),), (SHARD,))
    return jnp.where(me < 17, a, jnp.where(me == 17, b, c))


def allsum(arrays):
    return lax.psum(arrays, ("wide", "narrow"))


def norm_forward(values, gain, shift, total):
    sums, squares = allsum([jnp.sum(values, axis=1), jnp.sum(values * values, axis=1)])
    centre = sums / total
    inverse = lax.rsqrt(squares / total - centre * centre + EPSILON_NORM)
    normed = (values - centre[:, None]) * inverse[:, None]
    affine = gain.astype(F32)[:, None] * normed + shift.astype(F32)[:, None]
    return (normed, inverse, affine), jax.nn.silu(affine).astype(BF16)


def norm_backward(g, kept, gain, total):
    normed, inverse, affine = kept
    sigma = jax.nn.sigmoid(affine)
    p = g * sigma * (1.0 + affine * (1.0 - sigma))
    shift_part = jnp.sum(p, axis=1)
    gain_part = jnp.sum(p * normed, axis=1)
    shift_all, gain_all = allsum([shift_part, gain_part])
    d = (gain.astype(F32) * inverse)[:, None] * (p - (shift_all / total)[:, None] - normed * (gain_all / total)[:, None])
    return d.astype(BF16), gain_part, shift_part


def rows_of(params):
    flat = lax.all_gather(params, ("wide", "narrow"), axis=0, tiled=True)
    F = flat[:FROWS * NF * H].reshape(FROWS * NF, H)
    D = flat[FLATF:]
    D = jnp.pad(D, (0, max(0, HX * G - D.shape[0])))[:HX * G].reshape(HX, G)
    return F, D


def scatter_rows(FG, DG, length):
    flat = jnp.concatenate([FG.astype(F32).reshape(-1)[:FLATF], DG.astype(F32).reshape(-1)])
    flat = jnp.pad(flat, (0, max(0, length - flat.shape[0])))[:length]
    return lax.psum_scatter(flat, ("wide", "narrow"), scatter_dimension=0, tiled=True)


def unpack_rows(F):
    tail = jnp.concatenate([F[8004:8908, 200:], F[8005:8909, :200]], axis=1)
    return [None, F[7000], F[7001], F[7002:7802], F[7802], F[7803], F[7804:8004].reshape(H, 2 * L), F[8004, :200],
            tail[:100], tail[100], tail[101], tail[102:902], tail[902], tail[903]]


def pack_rows(g):
    g = [a.astype(BF16) for a in g]
    row = lambda a: a.reshape(1, -1)
    tail = jnp.concatenate([g[7], row(g[8]), row(g[9]), g[10], row(g[11]), row(g[12])])
    bent = jnp.concatenate([jnp.concatenate([row(g[6]), tail[:, 600:]]), jnp.pad(tail[:, :600], ((0, 1), (0, 0)))], axis=1)
    return jnp.concatenate([row(g[0]), row(g[1]), g[2], row(g[3]), row(g[4]), g[5].reshape(200, 800), bent,
                            jnp.zeros((FROWS * NF - 8909, 800), BF16)])


def by_halves(a, axis):
    wide = [(0, 0)] * a.ndim
    wide[axis] = (0, LP - L)
    return jnp.concatenate([jnp.pad(lax.slice_in_dim(a, i, i + L, axis=axis), wide) for i in (0, L)], axis=axis)


def one_hot(labels):
    return (labels[None, :] == jnp.arange(NC, dtype=jnp.int32)[:, None]).astype(BF16)


def fast_step(expression, epsilon, params, panels, labels):
    total = float(expression.shape[0] * 32)
    x = expression.T
    hot = one_hot(labels)
    F, D, lin1 = spread_and_first(*slots(params), x)
    w = unpack_rows(F)
    eps = jnp.pad(epsilon.T, ((0, LP - L), (0, 0)))
    wh = by_halves(w[6], 1)
    bh = by_halves(w[7].astype(F32), 0)[:, None]
    wd1 = jnp.pad(w[8], ((0, LP - L), (0, 0)))
    grows = jnp.pad(jnp.stack([w[i].astype(F32) for i in (1, 2, 4, 5, 9, 10, 12, 13)]), ((0, 0), (0, 896 - H)))
    act1, act2, act3, ends, heads, latent, lin2, lin3, lin4, stat, table = hidden_layers(
        total, lin1, w[3], wh, wd1, w[11], grows, bh, hot, eps)
    counts = table[:NC, LP - 1]
    cond_sums = table[:NC, :L]
    offset = cond_sums / counts[:, None] - jnp.sum(cond_sums, axis=0) / total
    mask_total = jnp.sum(counts * jnp.sum(panels.astype(F32), axis=1))
    rebuilt, direct, DG, g4, squares = output_layer(D, ends, x, panels.astype(BF16), hot, 2.0 / mask_total)
    d1, tail, sums2 = hidden_backward(
        total, g4, lin4, w[3], wh, wd1, w[11], grows, stat, latent, heads, hot, eps, table, squares,
        (act1, act2, act3), (lin1, lin2, lin3))
    FG, grad_cells = last_layer(x, F, d1, direct, FROWS * NF)
    FG = lax.dynamic_update_slice(FG, tail[:FROWS * NF - G], (G, 0))
    grad_params = flatten(*reduce(FG, DG, 4))
    divergence = -0.5 * table[NC, 0] / total
    loss = sums2[NC, 0] / mask_total + KL_WEIGHT * divergence
    columns = L // 4
    mine = lax.dynamic_slice(offset, (0, lax.axis_index("narrow") * columns), (NC, columns))
    return rebuilt.T, mine, loss, grad_cells.T, grad_params, divergence


def general_step(expression, epsilon, params, panels, labels):
    total = expression.shape[0] * lax.axis_size("wide") * lax.axis_size("narrow")
    x = expression.T
    noise = epsilon.T.astype(F32)
    F, D = rows_of(params)
    w = unpack_rows(F)
    hot = one_hot(labels)
    panel_sizes = jnp.sum(panels.astype(F32), axis=1)
    kept1, act1 = norm_forward(first_linear(F, x), w[1], w[2], total)
    kept2, act2 = norm_forward(mm(w[3], act1, TN), w[4], w[5], total)
    heads = (mm(w[6], act2, TN) + w[7].astype(F32)[:, None]).astype(BF16)
    mu, logvar = heads[:L].astype(F32), heads[L:].astype(F32)
    deviation = jnp.exp(0.5 * logvar)
    cond_sums, counts, kl = allsum([
        mm(hot, heads[:L], NT), jnp.sum(hot.astype(F32), axis=1),
        jnp.sum(1.0 + logvar - mu * mu - jnp.exp(logvar)).reshape(1)])
    offset = cond_sums / counts[:, None] - jnp.sum(cond_sums, axis=0) / total
    hotf = hot.astype(F32)
    choose = lambda table: sum(table[i][:, None] * hotf[i][None, :] for i in range(NC))
    latent = (mu + deviation * noise - choose(offset)).astype(BF16)
    kept3, act3 = norm_forward(mm(w[8], latent, TN), w[9], w[10], total)
    kept4, act4 = norm_forward(mm(w[11], act3, TN), w[12], w[13], total)
    mask_total = jnp.sum(counts * panel_sizes)
    ends = jnp.concatenate([act4, jnp.ones((1, act4.shape[1]), BF16), jnp.zeros((HX - H - 1, act4.shape[1]), BF16)])
    rebuilt, direct, DG, g4, squares = output_layer(D, ends, x, panels.astype(BF16), hot, 2.0 / mask_total)
    squared_part = jnp.sum(squares)
    d4, gain4, shift4 = norm_backward(g4[:H], kept4, w[12], total)
    grad_wd2 = mm(act3, d4, NT)
    d3, gain3, shift3 = norm_backward(mm(w[11], d4, NN), kept3, w[9], total)
    grad_wd1 = mm(latent, d3, NT)
    d_latent = mm(w[8], d3, NN).astype(BF16)
    cond_grad, squared = allsum([mm(hot, d_latent, NT), squared_part.reshape(1)])
    dl = d_latent.astype(F32)
    total_grad = jnp.sum(cond_grad, axis=0)
    d_mu = dl - choose(cond_grad / counts[:, None]) + (total_grad / total)[:, None] + KL_WEIGHT * mu / total
    d_logvar = 0.5 * dl * deviation * noise + KL_WEIGHT * 0.5 * (jnp.exp(logvar) - 1.0) / total
    d_heads = jnp.concatenate([d_mu, d_logvar]).astype(BF16)
    grad_bh = jnp.sum(d_heads.astype(F32), axis=1)
    grad_wh = mm(act2, d_heads, NT)
    d2, gain2, shift2 = norm_backward(mm(w[6], d_heads, NN), kept2, w[4], total)
    grad_w2 = mm(act1, d2, NT)
    d1, gain1, shift1 = norm_backward(mm(w[3], d2, NN), kept1, w[1], total)
    FG, grad_cells = last_layer(x, F, d1, direct, FROWS * NF)
    tail = pack_rows([gain1, shift1, grad_w2, gain2, shift2, grad_wh, grad_bh, grad_wd1, gain3, shift3, grad_wd2, gain4, shift4])
    FG = lax.dynamic_update_slice(FG, tail, (G, 0))
    grad_params = scatter_rows(FG, DG, params.shape[0] * lax.axis_size("wide") * lax.axis_size("narrow"))
    divergence = -0.5 * kl[0] / total
    loss = squared[0] / mask_total + KL_WEIGHT * divergence
    columns = L // lax.axis_size("narrow")
    mine = lax.dynamic_slice(offset, (0, lax.axis_index("narrow") * columns), (NC, columns))
    return rebuilt.T, mine, loss, grad_cells.T, grad_params, divergence


def solution(mesh):
    cells = P(("wide", "narrow"), None)
    flat = P(("wide", "narrow"))
    step = fast_step if dict(mesh.shape) == {"wide": 8, "narrow": 4} else general_step
    return jax.shard_map(step, mesh=mesh, in_specs=(cells, cells, flat, P(), flat),
                         out_specs=(cells, P(None, "narrow"), P(), cells, flat, P()), check_vma=False)
```

```python
import functools

import jax
import jax.numpy as jnp
from jax import lax
from jax.experimental import pallas as pl
from jax.experimental.pallas import tpu as pltpu
from jax.sharding import PartitionSpec as P

G, H, L, NC = 7000, 800, 100, 4
EPSILON_NORM = 1e-05
KL_WEIGHT = 5e-05
F32, BF16 = jnp.float32, jnp.bfloat16
TN = ((0,), (0,))
NN = ((1,), (0,))
NT = ((1,), (1,))
HX = 816


def mm(left, right, dims):
    return lax.dot_general(left, right, (dims, ((), ())), preferred_element_type=F32)


def params_of(limit=56):
    return pltpu.CompilerParams(dimension_semantics=("arbitrary",), vmem_limit_bytes=limit * 2**20)


def output_kernel(part, block, scale, d_ref, a_ref, x_ref, p_ref, h_ref, reb, direct, dg, g_ref, sq, dscr):
    i = pl.program_id(0)
    cells = a_ref.shape[1]

    @pl.when(i == 0)
    def _():
        g_ref[...] = jnp.zeros_like(g_ref)
        sq[...] = jnp.zeros_like(sq)

    lim = G - i * block
    for j in range(block // part):
        r = slice(j * part, (j + 1) * part)
        inside = lax.broadcasted_iota(jnp.int32, (part, 1), 0) + j * part < lim
        w = d_ref[:, r]
        out = mm(w, a_ref[...], TN)
        mask = jnp.where(inside, mm(p_ref[:, r], h_ref[...], TN), 0.0)
        t = jnp.exp(-jnp.abs(out))
        one = 1.0 + t
        soft = jnp.maximum(out, 0.0) + jnp.where(t < 1e-3, t - 0.5 * t * t, jnp.log(one))
        reb[r, :] = soft.astype(BF16)
        res = jnp.where(mask > 0.0, soft - x_ref[r, :].astype(F32), 0.0)
        sq[...] += jnp.sum((res * res).reshape(part // 8, 8, cells), axis=0)
        dr = scale[0] * res
        direct[r, :] = dr.astype(BF16)
        d = (dr * (jnp.where(out >= 0.0, 1.0, t) / one)).astype(BF16)
        lane = lax.broadcasted_iota(jnp.int32, (1, part), 1) + j * part < lim
        dscr[r, :] = d
    lane = lax.broadcasted_iota(jnp.int32, (1, block), 1) < lim
    dg[...] = mm(a_ref[...], dscr[...], NT).astype(BF16)
    g_ref[...] += mm(jnp.where(lane, d_ref[...], jnp.zeros((), BF16)), dscr[...], NN)


def output_layer(D, act, x, panels, hot, scale, block=1024, part=256):
    cells = x.shape[1]
    n = pl.cdiv(G, block)
    rows = lambda: pl.BlockSpec((block, cells), lambda i: (i, 0))
    whole = lambda r, c: pl.BlockSpec((r, c), lambda i: (0, 0))
    return pl.pallas_call(
        functools.partial(output_kernel, part, block),
        grid=(n,),
        out_shape=(jax.ShapeDtypeStruct((G, cells), BF16), jax.ShapeDtypeStruct((G, cells), BF16),
                   jax.ShapeDtypeStruct((HX, G), BF16), jax.ShapeDtypeStruct((HX, cells), F32),
                   jax.ShapeDtypeStruct((8, cells), F32)),
        in_specs=[pl.BlockSpec(memory_space=pltpu.SMEM), pl.BlockSpec((HX, block), lambda i: (0, i)), whole(HX, cells),
                  rows(), pl.BlockSpec((NC, block), lambda i: (0, i)), whole(NC, cells)],
        out_specs=[rows(), rows(), pl.BlockSpec((HX, block), lambda i: (0, i)), whole(HX, cells), whole(8, cells)],
        scratch_shapes=[pltpu.VMEM((block, cells), BF16)],
        compiler_params=params_of(),
        cost_estimate=pl.CostEstimate(flops=6 * G * H * cells, bytes_accessed=70_000_000, transcendentals=3 * G * cells),
        name="output_layer",
    )(scale.reshape(1), D, act, x, panels, hot)


def first_rows_kernel(block, w_ref, x_ref, o_ref):
    i = pl.program_id(0)

    @pl.when(i == 0)
    def _():
        o_ref[...] = jnp.zeros_like(o_ref)

    inside = lax.broadcasted_iota(jnp.int32, (block, 1), 0) < G - i * block
    zero = jnp.zeros((), BF16)

    @pl.when((i + 1) * block <= G)
    def _():
        o_ref[...] += mm(w_ref[...], x_ref[...], TN)

    @pl.when((i + 1) * block > G)
    def _():
        o_ref[...] += mm(jnp.where(inside, w_ref[...], zero), jnp.where(inside, x_ref[...], zero), TN)


def first_linear(F, x, block=1024):
    cells = x.shape[1]
    return pl.pallas_call(
        functools.partial(first_rows_kernel, block),
        grid=(pl.cdiv(G, block),),
        out_shape=jax.ShapeDtypeStruct((H, cells), F32),
        in_specs=[pl.BlockSpec((block, H), lambda i: (i, 0)), pl.BlockSpec((block, cells), lambda i: (i, 0))],
        out_specs=pl.BlockSpec((H, cells), lambda i: (0, 0)),
        compiler_params=params_of(),
        cost_estimate=pl.CostEstimate(flops=2 * G * H * cells, bytes_accessed=30_000_000, transcendentals=0),
        name="first_linear",
    )(F, x)


def last_kernel(x_ref, w_ref, d_ref, t_ref, fg, gc):
    fg[...] = mm(x_ref[...], d_ref[...], NT).astype(BF16)
    gc[...] = (mm(w_ref[...], d_ref[...], NN) - t_ref[...].astype(F32)).astype(BF16)


def last_layer(x, F, d1, direct, frows, block=512):
    cells = x.shape[1]
    rows = lambda c: pl.BlockSpec((block, c), lambda i: (i, 0))
    return pl.pallas_call(
        last_kernel,
        grid=(pl.cdiv(G, block),),
        out_shape=(jax.ShapeDtypeStruct((frows, H), BF16), jax.ShapeDtypeStruct((G, cells), BF16)),
        in_specs=[rows(cells), rows(H), pl.BlockSpec((H, cells), lambda i: (0, 0)), rows(cells)],
        out_specs=[rows(H), rows(cells)],
        compiler_params=params_of(),
        cost_estimate=pl.CostEstimate(flops=4 * G * H * cells, bytes_accessed=70_000_000, transcendentals=0),
        name="last_layer",
    )(x, F, d1, direct)


MESH = pl.DeviceIdType.MESH
FROWS, DROWS = 496, 64
NF = 18
SHARD = 397952
FLATF = 7126600
ALL = (0, 1, 2)


def d_unit(s):
    v = lax.shift_right_arithmetic(908 * (s - 19) + 1252, 8)
    return jnp.where(s <= NF, 0, v)


def place():
    w, n = lax.axis_index("wide"), lax.axis_index("narrow")
    return w // 2, w % 2, n // 2, n % 2


def dev(z, x, y, c):
    return (z * 2 + x, y * 2 + c)


def index(z, x, y, c):
    return (z * 2 + x) * 4 + y * 2 + c


def grd(cond, guard, fn):
    pl.when(cond if guard is None else jnp.logical_and(cond, guard))(fn)


def four(s):
    return lax.bitwise_and(lax.shift_right_arithmetic(0x355b, jnp.clip(s - NF, 0, 13)), 1) == 1


def greet(z, x, y, c, extra=()):
    bar = pltpu.get_barrier_semaphore()
    sig = lambda d: pl.semaphore_signal(bar, inc=1, device_id=d, device_id_type=MESH)
    for d in extra:
        sig(d)
    sig(dev(z, 1 - x, y, c))
    sig(dev(z, x, 1 - y, c))
    sig(dev(z, x, y, 1 - c))

    @pl.when(z > 0)
    def _():
        sig(dev(z - 1, x, y, c))

    @pl.when(z < 3)
    def _():
        sig(dev(z + 1, x, y, c))
    pl.semaphore_wait(bar, len(extra) + 3 + (z > 0).astype(jnp.int32) + (z < 3).astype(jnp.int32))


class Spread:
    VIA = {"F": (None, (0b0111, 0b0111), (0b0010, 0b0101), (0b0000, 0b0001)),
           "D": (None, (0b1100, 0b1100), (0b1000, 0b1100), (0b1000, 0b0000))}

    def __init__(self, kind, own, buf, send, recv, base=0):
        self.kind, self.own, self.buf, self.send, self.recv = kind, own, buf, send, recv
        self.place = z, x, y, c = place()
        self.sems, self.base, self.started = {}, base, []
        self.XP, self.YP, self.CP = (z, 1 - x, y, c), (z, x, 1 - y, c), (z, x, y, 1 - c)
        self.UP, self.DN = (z + 1, x, y, c), (z - 1, x, y, c)
        self.tags = {0: (0, z, None)}
        for t in (1, 2, 3):
            self.tags[2 * t] = (2 * t, z - t, z >= t)
            self.tags[2 * t + 1] = (2 * t + 1, z + t, z + t <= 3)

    def pieces(self, s, p):
        if self.kind == "F":
            return [] if p == 2 else [(s < NF, FROWS * s, (0, 240)[p], (240, 256)[p])]
        return [(None, 16 * d_unit(s), (0, 32, 48)[p], (32, 16, 16)[p])]

    def rows(self, s, p):
        for cond, base, off, n in self.pieces(s, p):
            yield cond, self.buf.at[pl.ds(pl.multiple_of(base + off, 16), n)], self.own.at[pl.ds(off, n)]

    def copy(self, s, p, key, target, local=False):
        k = self.base + self.sems.setdefault((key, p), len(self.sems))
        (_, dst, own), = self.rows(s, p)
        return pltpu.make_async_remote_copy(src_ref=own if local else dst, dst_ref=dst, send_sem=self.send.at[k],
                                            recv_sem=self.recv.at[k], device_id=dev(*target), device_id_type=MESH)

    def where(self, s, guard, fn):
        def last():
            fn((2,))

        def both():
            fn((0, 1))
            if self.kind == "D":
                pl.when(four(s))(last)
        grd(s < NF if self.kind == "F" else s >= NF, guard, both)

    def sends(self, s, guard, legs, local=False):
        def start(what, ps):
            for p in ps:
                for parts, key, target, more in legs:
                    if p in parts:
                        fn = getattr(self.copy(s, p, key, target, local), what)
                        fn() if more is None else pl.when(more)(fn)
        self.started.append((s, guard, functools.partial(start, "wait_send")))
        return functools.partial(start, "start")

    def gets(self, s, parts, key, target, more=None):
        def wait(ps):
            for p in ps:
                if p in parts:
                    fn = self.copy(s, p, key, target).wait_recv
                    fn() if more is None else pl.when(more)(fn)
        return wait

    def begin(self, loc, planes=True, names="ud"):
        z, x, y, c = self.place
        me = index(*self.place)
        fs = [self.sends(me, None, [(ALL, (name, 1), *((self.UP, z < 3) if name == "u" else (self.DN, z > 0)))], True) for name in names]
        fs += [self.planes(0, True)] if planes else []
        self.where(me, None, lambda ps: [f(ps) for f in fs])

        def start(what, ps):
            for p in ps:
                (_, dst, own), = self.rows(me, p)
                getattr(pltpu.make_async_copy(own, dst, loc.at[p]), what)()
        self.kept = lambda: self.where(me, None, functools.partial(start, "wait"))
        self.where(me, None, functools.partial(start, "start"))

    def own_in_place(self):
        self.kept()

    def planes(self, tag, local=False):
        _, zz, guard = self.tags[tag]
        z, x, y, c = self.place
        s = index(zz, x, y, c)
        return self.sends(s, guard, [(ALL, ("x", tag), self.XP, None), (ALL, ("y", tag), self.YP, None),
                                     (ALL, ("c0", tag), self.CP, None)], local)

    def along_z(self, t):
        z, x, y, c = self.place
        for name in "ud":
            tag = 2 * t + (name == "d")
            _, zz, ok = self.tags[tag]
            frm, to, more = (self.DN, self.UP, z < 3) if name == "u" else (self.UP, self.DN, z > 0)
            s = index(zz, x, y, c)
            fs = [self.sends(s, ok, [(ALL, (name, t + 1), to, more)])] if t < 3 else []
            fs.append(self.planes(tag))
            get = self.gets(s, ALL, (name, t), frm)

            def fn(ps):
                for p in ps:
                    get((p,))
                    for f in fs:
                        f((p,))
            self.where(s, ok, fn)

    def by_z(self, t, zz):
        first, others = self.VIA[self.kind][t]
        has = lambda planes: lax.bitwise_and(lax.shift_right_arithmetic(planes, jnp.clip(zz, 0, 3)), 1) == 1
        return has(first), has(others)

    def flat_parts(self, tag):
        _, zz, guard = self.tags[tag]
        if tag == 0:
            return guard, guard
        first, others = self.by_z(tag // 2, zz)
        return jnp.logical_and(guard, jnp.logical_not(others)), jnp.logical_and(guard, jnp.logical_not(first))

    def cross(self, tag):
        _, zz, guard = self.tags[tag]
        z, x, y, c = self.place
        second, half = self.flat_parts(tag)
        for s, name, frm, parts, leg, cond, core in (
                (index(zz, 1 - x, y, c), "x", self.XP, (1, 2), ("xy", tag, self.YP), second, "c1"),
                (index(zz, x, 1 - y, c), "y", self.YP, (0,), ("yx", tag, self.XP), half, "c2")):
            get = self.gets(s, ALL, (name, tag), frm)
            send = self.sends(s, guard, [(parts, leg[:2], leg[2], cond), (ALL, (core, tag), self.CP, None)])

            def fn(ps):
                get(ps)
                send(ps)
            self.where(s, guard, fn)

    def diag(self, tag):
        _, zz, guard = self.tags[tag]
        z, x, y, c = self.place
        sd = index(zz, 1 - x, 1 - y, c)
        second, half = self.flat_parts(tag)
        t, name = tag // 2, "ud"[tag % 2]
        both = lambda a, b: b if a is None else jnp.logical_and(a, b)
        gets, legs = [], []
        if tag:
            frm = self.DN if name == "u" else self.UP
            first, others = self.by_z(t, zz)
            gets = [self.gets(sd, (0,), ("g" + name, t), frm, both(guard, first)),
                    self.gets(sd, (1, 2), ("g" + name, t), frm, both(guard, others))]
        for name in ("ud"[tag % 2] if tag else "ud") if t < 3 else "":
            to, more = (self.UP, z < 3) if name == "u" else (self.DN, z > 0)
            first, others = self.by_z(t + 1, zz)
            legs += [((0,), ("g" + name, t + 1), to, both(first, more)), ((1, 2), ("g" + name, t + 1), to, both(others, more))]
        gets += [self.gets(sd, (1, 2), ("xy", tag), self.YP, second), self.gets(sd, (0,), ("yx", tag), self.XP, half)]
        send = self.sends(sd, guard, legs + [(ALL, ("c3", tag), self.CP, None)])

        def fn(ps):
            for get in gets:
                get(ps)
            send(ps)
        self.where(sd, guard, fn)

    def core(self, tag, i):
        _, zz, guard = self.tags[tag]
        z, x, y, c = self.place
        xx, yy = ((x, y), (1 - x, y), (x, 1 - y), (1 - x, 1 - y))[i]
        s = index(zz, xx, yy, 1 - c)
        self.where(s, guard, self.gets(s, ALL, ("c%d" % i, tag), self.CP))

    def end(self):
        for s, guard, fn in self.started:
            self.where(s, guard, fn)


def first_kernel(fs, x_hbm, ds, F, D, lin, fv, xv, send, recv, loc, fsem, xsem, dsend, drecv, dloc):
    z, x, y, c = place()
    xcopy = pltpu.make_async_copy(x_hbm, xv, xsem)
    xcopy.start()
    net = Spread("F", fs, fv, send, recv)
    late = Spread("D", ds, D, dsend, drecv)
    greet(z, x, y, c)
    net.begin(loc)
    late.begin(dloc)
    lin[...] = jnp.zeros_like(lin)
    out = []

    def store(s, k, guard):
        r = pl.ds(pl.multiple_of(FROWS * s, 16), FROWS)
        cp = pltpu.make_async_copy(fv.at[r], F.at[r], fsem.at[k])
        grd(s < NF, guard, cp.start)
        out.append((s < NF, guard, cp))

    def times(tag, i):
        _, zz, guard = net.tags[tag]
        xx, yy = ((x, y), (1 - x, y), (x, 1 - y), (1 - x, 1 - y))[i]
        m = (zz * 2 + xx) * 2 + yy

        def whole():
            r = pl.ds(pl.multiple_of(2 * FROWS * m, 16), 2 * FROWS)
            lin[...] += mm(fv[r, :], xv[r, :], TN)

        def rest():
            r = pl.ds(14 * FROWS, G - 14 * FROWS)
            lin[...] += mm(fv[r, :], xv[r, :], TN)
        grd(m < 7, guard, whole)
        grd(m == 7, guard, rest)
        k = 8 * tag + 2 * i
        store(2 * m, k, guard)
        store(2 * m + 1, k + 1, guard)

    def finish(tag, cols):
        for i in cols:
            net.core(tag, i)
            times(tag, i)

    def both(name, *tags):
        for n in (net, late):
            for tag in tags:
                getattr(n, name)(tag)

    def settle(tag, cols):
        for i in cols:
            late.core(tag, i)

    both("along_z", 1)
    both("cross", 0)
    both("along_z", 2)
    both("diag", 0)
    both("cross", 2, 3)
    net.own_in_place()
    late.own_in_place()
    xcopy.wait()
    finish(0, (0, 1, 2, 3))
    both("along_z", 3)
    both("diag", 2, 3)
    both("cross", 4, 5)
    finish(2, (0, 1, 2))
    finish(3, (0, 1, 2))
    both("diag", 4, 5)
    both("cross", 6, 7)
    finish(2, (3,))
    finish(3, (3,))
    finish(4, (0, 1, 2))
    finish(5, (0, 1, 2))
    both("diag", 6, 7)
    for tag in (4, 5):
        finish(tag, (3,))
    for tag in (6, 7):
        finish(tag, (0, 1, 2, 3))
    for tag in (0, 2, 3, 4, 5, 6, 7):
        settle(tag, (0, 1, 2, 3))
    net.end()
    late.end()
    for cond, guard, cp in out:
        grd(cond, guard, cp.wait)


def spread_and_first(fslot, dslot, x, cid=1):
    cells = x.shape[1]
    V = pltpu.VMEM
    return pl.pallas_call(
        first_kernel,
        out_shape=(jax.ShapeDtypeStruct((FROWS * NF, H), BF16), jax.ShapeDtypeStruct((HX, G), BF16), jax.ShapeDtypeStruct((H, cells), F32)),
        in_specs=[pl.BlockSpec(memory_space=pl.ANY)] * 3,
        out_specs=[pl.BlockSpec(memory_space=pl.ANY)] * 2 + [pl.BlockSpec(memory_space=V)],
        scratch_shapes=[V((FROWS * NF, H), BF16), V((G, cells), BF16), pltpu.SemaphoreType.DMA((144,)), pltpu.SemaphoreType.DMA((144,)),
                        pltpu.SemaphoreType.DMA((3,)), pltpu.SemaphoreType.DMA((64,)), pltpu.SemaphoreType.DMA,
                        pltpu.SemaphoreType.DMA((208,)), pltpu.SemaphoreType.DMA((208,)), pltpu.SemaphoreType.DMA((3,))],
        compiler_params=pltpu.CompilerParams(collective_id=cid, has_side_effects=True, vmem_limit_bytes=58 * 2**20),
        name="spread_and_first",
    )(fslot, x, dslot)


def slots(p):
    n = 32
    me = lax.axis_index("wide") * 4 + lax.axis_index("narrow")
    ax = ("wide", "narrow")
    head = lax.ppermute(p[-36864:], ax, [(i, i + 1) for i in range(n - 1)])
    tail = lax.ppermute(p[:112000], ax, [(i + 1, i) for i in range(n - 1)])
    ext = jnp.concatenate([head, p, tail, jnp.zeros((112000,), p.dtype)])
    f = lax.dynamic_slice(ext, (jnp.maximum(36864 - 1152 * me, 0),), (FROWS * 800,)).reshape(FROWS, 800)
    off = 36864 + FLATF + 112000 * d_unit(me) - SHARD * me
    d = lax.dynamic_slice(ext, (jnp.clip(off, 0, ext.shape[0] - DROWS * 7000),), (DROWS * 7000,)).reshape(DROWS, 7000)
    return f, d

LP = 128
STEP, UNROLL = 32, 5


def rows_loop(n, fn, step=STEP, unroll=UNROLL):
    def body(i, _):
        for j in range(unroll):
            fn(pl.ds(pl.multiple_of((i * unroll + j) * step, step), step))
        return 0
    lax.fori_loop(0, n // (step * unroll), body, 0)


def silu(u):
    return u * (0.5 + 0.5 * jnp.tanh(0.5 * u))


def by_lanes(v):
    return sum(v[:, 128 * i:128 * i + 128] for i in range(v.shape[1] // 128))


def over_rows(buf):
    return jnp.sum(jnp.transpose(buf), axis=0, keepdims=True)


def along_rows(row):
    return jnp.transpose(jnp.broadcast_to(row, (128, 896)))


def wide(col, cells):
    return jnp.concatenate([col] * (cells // 128), axis=1)


class Sums:
    def __init__(self, bufs, sems):
        self.bufs, self.sems, self.turn = bufs, sems, 0
        self.place = z, x, y, c = place()
        self.spot = x * 4 + y * 2 + c
        self.inside = [(k, lax.bitwise_xor(self.spot, k)) for k in range(1, 8)]
        self.planes = [(k, lax.bitwise_xor(z, k)) for k in range(1, 4)]

    def near_dev(self, q):
        return dev(self.place[0], q // 4, (q // 2) % 2, q % 2)

    def far_dev(self, q):
        return dev(q, *self.place[1:])

    def others(self):
        return [self.near_dev(q) for k, q in self.inside] + [self.far_dev(q) for k, q in self.planes]

    def __call__(self, kind, value, between=None, after=None):
        near, far = self.bufs[kind]
        i, t = self.turn, self.sems
        self.turn += 1
        j = self.count[kind] = self.count.get(kind, -1) + 1 if hasattr(self, "count") else self.first(kind)
        s, f = near.at[j], far.at[j]
        s[self.spot] = value
        cps = [pltpu.make_async_remote_copy(src_ref=s.at[self.spot], dst_ref=s.at[self.spot], send_sem=t[0].at[i, k], recv_sem=t[1].at[i, k],
                                            device_id=self.near_dev(q), device_id_type=MESH) for k, q in self.inside]
        for cp in cps:
            cp.start()
        if between:
            between()
        for cp in cps:
            cp.wait_recv()
        z = self.place[0]
        f[z] = jnp.sum(s[...], axis=0)
        cpz = [pltpu.make_async_remote_copy(src_ref=f.at[z], dst_ref=f.at[z], send_sem=t[2].at[i, k], recv_sem=t[3].at[i, k],
                                            device_id=self.far_dev(q), device_id_type=MESH) for k, q in self.planes]
        for cp in cpz:
            cp.start()
        for cp in cps:
            cp.wait_send()
        if after:
            after()
        for cp in cpz:
            cp.wait()
        return jnp.sum(f[...], axis=0)

    def first(self, kind):
        self.count = {}
        return 0


def sums_scratch(stats, tables):
    V = pltpu.VMEM
    n = stats + tables
    dma = pltpu.SemaphoreType.DMA
    return [V((stats, 8, 2, 896), F32), V((stats, 4, 2, 896), F32), V((max(tables, 1), 8, 8, 128), F32), V((max(tables, 1), 4, 8, 128), F32),
            dma((n, 8)), dma((n, 8)), dma((n, 4)), dma((n, 4))]


def turned(v, places):
    lane = lax.broadcasted_iota(jnp.int32, v.shape, 1)
    return sum(jnp.where(jnp.logical_and(lane >= to, lane < to + stop - start), pltpu.roll(v, (to - start) % 896, 1), 0.0)
               for start, stop, to in places)


def padded(v):
    return jnp.concatenate([v, jnp.zeros((v.shape[0], 896 - v.shape[1]), F32)], axis=1)


def forward_kernel(total, lin1, F, hot, eps, w2, wh, wd1, wd2, grows,
                   act1o, act2o, act3o, ends, heads, latent, lin2o, lin3o, lin4, stat, table,
                   packed, msem, rows, tail, whm, whl, bh, act1, act2, act3, lin2, lin3, osem, bufs, square, n1, f1, n2, f2, a1, a2, a3, a4):
    z, x, y, c = place()
    sums = Sums({"stat": (n1, f1), "table": (n2, f2)}, (a1, a2, a3, a4))
    cells = lin1.shape[1]
    brings = pltpu.make_async_copy(F.at[pl.ds(6992, 1920)], packed, msem)
    brings.start()
    for i in range(2):
        bufs[i, pl.ds(H, 96), :] = jnp.zeros((96, 128), F32)
    square[...] = jnp.zeros_like(square)
    greet_all(sums.others())

    def stats(lin):
        def one(r):
            v = lin[r, :]
            bufs[0, r, :] = by_lanes(v)
            bufs[1, r, :] = by_lanes(v * v)
        rows_loop(H, one)
        return jnp.concatenate([over_rows(bufs[0]), over_rows(bufs[1])])

    def norm(k, lin, out, between=None, after=None):
        t = sums("stat", stats(lin), between, after)
        centre = t[0:1, :] / total
        inverse = lax.rsqrt(t[1:2, :] / total - centre * centre + EPSILON_NORM)
        stat[pl.ds(2 * k, 1), :] = centre
        stat[pl.ds(2 * k + 1, 1), :] = inverse
        scale = inverse * grows[2 * k:2 * k + 1, :]
        bufs[0] = along_rows(scale)
        bufs[1] = along_rows(grows[2 * k + 1:2 * k + 2, :] - centre * scale)

        def one(r):
            out[r, :] = silu(lin[r, :] * wide(bufs[0, r, :], cells) + wide(bufs[1, r, :], cells)).astype(BF16)
        rows_loop(H, one)

    def unpack():
        brings.wait()

        def widen(r):
            rows[r, :] = padded(packed[r, :].astype(F32))
        rows_loop(1920, widen, 32, 5)
        lane = lax.broadcasted_iota(jnp.int32, (904, 896), 1)
        t = jnp.where(lane < 600, pltpu.roll(rows[pl.ds(1012, 904), :], 696, 1), pltpu.roll(rows[pl.ds(1013, 904), :], 600, 1))
        tail[...] = jnp.where(lane < H, t, 0.0)
        for i, (buf, r) in enumerate(((rows, 8), (rows, 9), (rows, 810), (rows, 811), (tail, 100), (tail, 101), (tail, 902), (tail, 903))):
            grows[pl.ds(i, 1), :] = buf[pl.ds(r, 1), :]
        w2[...] = rows[pl.ds(10, H), pl.ds(0, H)].astype(BF16)
        wd2[...] = tail[pl.ds(102, H), pl.ds(0, H)].astype(BF16)
        top = lax.broadcasted_iota(jnp.int32, (LP, H), 0) < L
        wd1[...] = jnp.where(top, tail[pl.ds(0, LP), pl.ds(0, H)], 0.0).astype(BF16)
        v = rows[pl.ds(812, 200), :]
        for i in range(4):
            for k, half in enumerate((whm, whl)):
                half[pl.ds(i, 200, stride=4), :] = turned(v, ((200 * i + L * k, 200 * i + L * k + L, 0),))[:, :LP]
        wh[:, pl.ds(0, LP)] = whm[...].astype(BF16)
        wh[:, pl.ds(LP, LP)] = whl[...].astype(BF16)
        b = turned(rows[pl.ds(1012, 1), :], ((0, L, 0), (L, 2 * L, LP)))[:, :2 * LP]
        bh[...] = jnp.transpose(jnp.broadcast_to(b, (LP, 2 * LP)))

    leaving = []

    def leave(src, dst):
        cp = pltpu.make_async_copy(src, dst, osem.at[len(leaving)])
        cp.start()
        leaving.append(cp)

    norm(0, lin1, act1, unpack)
    lin2[...] = mm(w2[...], act1[...], TN)
    leave(act1, act1o)
    leave(lin2, lin2o)
    norm(1, lin2, act2)
    leave(act2, act2o)
    h = (mm(wh[...], act2[...], TN) + bh[:, 0:1]).astype(BF16)
    heads[...] = h
    mu, lv = h[:LP].astype(F32), h[LP:].astype(F32)
    part = mm(hot[...], h[:LP], NT)
    hf = hot[...].astype(F32)
    lane = lax.broadcasted_iota(jnp.int32, (NC, LP), 1)
    top = jnp.where(lane == LP - 1, jnp.sum(hf, axis=1, keepdims=True), part)
    kl = jnp.sum(jnp.sum(1.0 + lv - mu * mu - jnp.exp(lv), axis=0, keepdims=True), axis=1, keepdims=True)
    low = jnp.where(lax.broadcasted_iota(jnp.int32, (4, LP), 0) == 0, kl, 0.0)

    t = sums("table", jnp.concatenate([top, low]))
    table[...] = t
    cond = t[0:NC, :]
    counts = cond[:, LP - 1:LP]
    cond = jnp.where(lane == LP - 1, 0.0, cond)
    off = cond / counts - jnp.sum(cond, axis=0, keepdims=True) / total
    square[pl.ds(0, NC), :] = off
    offc = jnp.transpose(square[...])
    chosen = sum(offc[:, i:i + 1] * hf[i:i + 1, :] for i in range(NC))
    lat = (mu + jnp.exp(0.5 * lv) * eps[...].astype(F32) - chosen).astype(BF16)
    latent[...] = lat
    lin3[...] = mm(wd1[...], latent[...], TN)
    leave(lin3, lin3o)
    norm(2, lin3, act3)
    leave(act3, act3o)
    lin4[...] = mm(wd2[...], act3[...], TN)

    norm(3, lin4, ends)
    ends[pl.ds(H, 16), :] = jnp.where(lax.broadcasted_iota(jnp.int32, (16, ends.shape[1]), 0) == 0, 1.0, 0.0).astype(BF16)
    for cp in leaving:
        cp.wait()


def greet_all(devices):
    bar = pltpu.get_barrier_semaphore()
    for d in devices:
        pl.semaphore_signal(bar, inc=1, device_id=d, device_id_type=MESH)
    pl.semaphore_wait(bar, len(devices))


def hidden_layers(total, lin1, F, hot, eps, cid=2):
    cells = lin1.shape[1]
    V = pltpu.VMEM
    vm = pl.BlockSpec(memory_space=V)
    hbm = pl.BlockSpec(memory_space=pl.ANY)
    S = jax.ShapeDtypeStruct
    return pl.pallas_call(
        functools.partial(forward_kernel, total),
        out_shape=(S((H, H), BF16), S((H, 2 * LP), BF16), S((LP, H), BF16), S((H, H), BF16), S((8, 896), F32),
                   S((H, cells), BF16), S((H, cells), BF16), S((H, cells), BF16), S((HX, cells), BF16), S((2 * LP, cells), BF16),
                   S((LP, cells), BF16), S((H, cells), F32), S((H, cells), F32), S((H, cells), F32), S((8, 896), F32),
                   S((8, LP), F32)),
        in_specs=[vm, hbm, vm, vm],
        out_specs=[vm] * 5 + [hbm] * 3 + [vm] * 3 + [hbm] * 2 + [vm] * 3,
        scratch_shapes=[V((1920, H), BF16), pltpu.SemaphoreType.DMA, V((1920, 896), F32), V((904, 896), F32), V((H, LP), F32), V((H, LP), F32),
                        V((2 * LP, LP), F32), *[V((H, cells), BF16)] * 3, *[V((H, cells), F32)] * 2, pltpu.SemaphoreType.DMA((8,)), V((2, 896, 128), F32), V((LP, LP), F32), *sums_scratch(4, 1)],
        compiler_params=pltpu.CompilerParams(collective_id=cid, has_side_effects=True, vmem_limit_bytes=58 * 2**20),
        name="hidden_layers",
    )(lin1, F, hot, eps)


def backward_kernel(total, g4, lin4, w2, wh, wd1, wd2, grows, stat, latent, heads, hot, eps, table, squares, act1i, act2i, act3i, lin1i, lin2i, lin3i,
                    d1, tail, sums2,
                    gnorm, rows, upper, lower, gwh, gwl, act1, act2, act3, lin1, lin2, lin3, isem, pbuf, dbuf, hbuf, bufs, part, square, n1, f1, n2, f2, a1, a2, a3, a4):
    cells = lin4.shape[1]
    sums = Sums({"stat": (n1, f1), "table": (n2, f2)}, (a1, a2, a3, a4))
    comes = {}
    for i, (name, src, dst) in enumerate((("lin3", lin3i, lin3), ("act3", act3i, act3), ("lin2", lin2i, lin2), ("act2", act2i, act2),
                                          ("lin1", lin1i, lin1), ("act1", act1i, act1))):
        comes[name] = pltpu.make_async_copy(src, dst, isem.at[i])
        comes[name].start()
    for i in range(2):
        part[i, pl.ds(H, 96), :] = jnp.zeros((96, 128), F32)
    square[...] = jnp.zeros_like(square)
    for buf in (upper, lower):
        buf[pl.ds(0, 8), :] = jnp.zeros((8, 896), F32)
        buf[pl.ds(904, 8), :] = jnp.zeros((8, 896), F32)
    rows[pl.ds(1904, 32), :] = jnp.zeros((32, 896), F32)
    greet_all(sums.others())

    def keep(r, v):
        upper[pl.ds(r + 4, v.shape[0]), pl.ds(0, H)] = v
        lower[pl.ds(r + 5, v.shape[0]), pl.ds(0, H)] = v

    def pack():
        keep(100, gnorm[5:6, pl.ds(0, H)])
        keep(101, gnorm[4:5, pl.ds(0, H)])
        keep(902, gnorm[7:8, pl.ds(0, H)])
        keep(903, gnorm[6:7, pl.ds(0, H)])

        def bend(r):
            lane = lax.broadcasted_iota(jnp.int32, (16, 896), 1)
            rows[pl.ds(pl.multiple_of(1000 + r.start, 8), 16), :] = jnp.where(
                lane < 200, pltpu.roll(lower[r, :], 296, 1), pltpu.roll(upper[r, :], 200, 1))
        rows_loop(912, bend, 16, 3)
        acc = 0.0
        for i in range(4):
            for j, half in enumerate((gwh, gwl)):
                acc = acc + turned(padded(half[pl.ds(i, 200, stride=4), :]), ((0, L, 200 * i + L * j),))
        rows[pl.ds(804, 200), :] = acc
        rows[pl.ds(802, 1), :] = gnorm[3:4, :]
        rows[pl.ds(803, 1), :] = gnorm[2:3, :]

    def norm(k, g, lin, out, between=None):
        centre, inverse = stat[2 * k:2 * k + 1, :], stat[2 * k + 1:2 * k + 2, :]
        gain, shift = grows[2 * k:2 * k + 1, :], grows[2 * k + 1:2 * k + 2, :]
        bufs[0] = along_rows(inverse)
        bufs[1] = along_rows(-centre * inverse)
        bufs[2] = along_rows(gain)
        bufs[3] = along_rows(shift)

        def one(r):
            n = lin[r, :] * wide(bufs[0, r, :], cells) + wide(bufs[1, r, :], cells)
            u = n * wide(bufs[2, r, :], cells) + wide(bufs[3, r, :], cells)
            s = 0.5 + 0.5 * jnp.tanh(0.5 * u)
            p = g[r, :] * s * (1.0 + u * (1.0 - s))
            pbuf[r, :] = p
            part[0, r, :] = by_lanes(p)
            part[1, r, :] = by_lanes(p * n)
        rows_loop(H, one)
        local = jnp.concatenate([over_rows(part[0]), over_rows(part[1])])
        gnorm[pl.ds(2 * k, 2), :] = local
        t = sums("stat", local, between)
        a = gain * inverse
        b = -a * t[1:2, :] / total
        bufs[0] = along_rows(a)
        bufs[1] = along_rows(b * inverse)
        bufs[2] = along_rows(-b * centre * inverse - a * t[0:1, :] / total)

        def two(r):
            out[r, :] = (pbuf[r, :] * wide(bufs[0, r, :], cells) + lin[r, :] * wide(bufs[1, r, :], cells)
                         + wide(bufs[2, r, :], cells)).astype(BF16)
        rows_loop(H, two)

    norm(3, g4, lin4, dbuf)
    pbuf[...] = mm(wd2[...], dbuf[...], NN)
    comes["lin3"].wait()
    comes["act3"].wait()

    def grads4():
        keep(102, mm(act3[...], dbuf[...], NT))
    norm(2, pbuf, lin3, hbuf, grads4)
    dl = mm(wd1[...], hbuf[...], NN).astype(BF16)
    cond = mm(hot[...], dl, NT)
    sq = jnp.sum(jnp.sum(squares[...], axis=0, keepdims=True), axis=1, keepdims=True)
    low = jnp.where(lax.broadcasted_iota(jnp.int32, (4, LP), 0) == 0, sq, 0.0)

    def grads3():
        keep(0, mm(latent[...], hbuf[...], NT)[:L])
    t = sums("table", jnp.concatenate([cond, low]), grads3)
    sums2[...] = t
    cond = t[0:NC, :]
    counts = table[0:NC, LP - 1:LP]
    square[pl.ds(0, NC), :] = jnp.sum(cond, axis=0, keepdims=True) / total - cond / counts
    take = jnp.transpose(square[...])
    hf = hot[...].astype(F32)
    change = sum(take[:, i:i + 1] * hf[i:i + 1, :] for i in range(NC))
    mu, lv = heads[pl.ds(0, LP), :].astype(F32), heads[pl.ds(LP, LP), :].astype(F32)
    dl = dl.astype(F32)
    dh = jnp.concatenate([
        dl + change + (KL_WEIGHT / total) * mu,
        0.5 * dl * jnp.exp(0.5 * lv) * eps[...].astype(F32) + (0.5 * KL_WEIGHT / total) * (jnp.exp(lv) - 1.0)]).astype(BF16)
    dbuf[pl.ds(0, 2 * LP), :] = dh
    bias = padded(mm(jnp.ones((8, cells), BF16), dh, NT))
    lower[pl.ds(4, 1), :] = turned(bias, ((0, L, 600), (LP, LP + L, 700)))[0:1]
    pbuf[...] = mm(wh[...], dh, NN)
    comes["lin2"].wait()
    comes["act2"].wait()

    def grads2():
        g = mm(act2[...], dbuf[pl.ds(0, 2 * LP), :], NT)
        gwh[...] = g[:, :LP]
        gwl[...] = g[:, LP:]
    norm(1, pbuf, lin2, hbuf, grads2)
    pbuf[...] = mm(w2[...], hbuf[...], NN)
    comes["lin1"].wait()
    comes["act1"].wait()

    def grads1():
        rows[pl.ds(2, H), pl.ds(0, H)] = mm(act1[...], hbuf[...], NT)
        pack()
    norm(0, pbuf, lin1, d1, grads1)
    rows[pl.ds(0, 1), :] = gnorm[1:2, :]
    rows[pl.ds(1, 1), :] = gnorm[0:1, :]

    def out(r):
        tail[r, :] = rows[r, pl.ds(0, H)].astype(BF16)
    rows_loop(1920, out, 16, 5)
    tail[pl.ds(1920, 16), :] = jnp.zeros((16, H), BF16)


def hidden_backward(total, g4, lin4, w2, wh, wd1, wd2, grows, stat, latent, heads, hot, eps, table, squares, acts, lins, cid=3):
    cells = lin4.shape[1]
    V = pltpu.VMEM
    vm = pl.BlockSpec(memory_space=V)
    hbm = pl.BlockSpec(memory_space=pl.ANY)
    S = jax.ShapeDtypeStruct
    return pl.pallas_call(
        functools.partial(backward_kernel, total),
        out_shape=(S((H, cells), BF16), S((1936, H), BF16), S((8, LP), F32)),
        in_specs=[vm] * 14 + [hbm] * 6,
        out_specs=[vm] * 3,
        scratch_shapes=[V((8, 896), F32), V((1936, 896), F32), V((912, 896), F32), V((912, 896), F32), V((H, LP), F32), V((H, LP), F32), *[V((H, cells), BF16)] * 3, *[V((H, cells), F32)] * 3, pltpu.SemaphoreType.DMA((6,)),
                        V((H, cells), F32), V((H, cells), BF16), V((H, cells), BF16),
                        V((4, 896, 128), F32), V((2, 896, 128), F32), V((LP, LP), F32), *sums_scratch(4, 1)],
        compiler_params=pltpu.CompilerParams(collective_id=cid, has_side_effects=True, vmem_limit_bytes=58 * 2**20),
        name="hidden_backward",
    )(g4, lin4, w2, wh, wd1, wd2, grows, stat, latent, heads, hot, eps, table, squares, *acts, *lins)


ZF, ZD = (0, 1, 2), (2, 3)

def reduce_kernel(FG, DG, fo, do, nf, pd, tF, tD, cF, cD, rF, rD, aF, aD, bF, bD, uF, uD, vF, vD, send, recv, loc, hsend, hrecv):
    z, x, y, c = place()
    XP, YP, CP = (z, 1 - x, y, c), (z, x, 1 - y, c), (z, x, y, 1 - c)
    UP, DN = (z + 1, x, y, c), (z - 1, x, y, c)
    me = index(z, x, y, c)
    numbered = lambda i: (lax.shift_right_arithmetic(i, 2), lax.bitwise_and(i, 3))
    before, after = numbered(jnp.maximum(me - 1, 0)), numbered(jnp.minimum(me + 1, 31))
    nf[...] = jnp.zeros_like(nf)
    pd[...] = jnp.zeros_like(pd)
    bar = pltpu.get_barrier_semaphore()
    sig = lambda d: pl.semaphore_signal(bar, inc=1, device_id=d, device_id_type=MESH)
    for d in (XP, YP, CP):
        sig(dev(*d))
    for cond, d in ((z > 0, dev(*DN)), (z < 3, dev(*UP)), (me > 0, before), (me < 31, after)):
        pl.when(cond)(functools.partial(sig, d))
    one = lambda cond: cond.astype(jnp.int32)
    pl.semaphore_wait(bar, 3 + one(z > 0) + one(z < 3) + one(me > 0) + one(me < 31))

    sems = {}
    def sem_index(key):
        return sems.setdefault(key, len(sems))
    started = []

    def cases(s, part):
        last = jnp.logical_and(s >= NF, four(s))
        f, d = s < NF, s >= NF
        if part == "all":
            return [(f, "F", 0, 496, 0), (d, "D", 0, 48, 0), (last, "D", 48, 16, 1)]
        if part == "a":
            return [(f, "F", 0, 240, 0), (d, "D", 0, 32, 0)]
        return [(f, "F", 240, 256, 0), (d, "D", 32, 16, 0), (last, "D", 48, 16, 1)]

    def land(pair, zz, b, col=None):
        buf = pair[0 if b == "F" else 1]
        zi = zz if b == "F" else zz - 2
        return buf.at[zi] if col is None else buf.at[col, zi]

    def grd(cond, guard, fn):
        pl.when(cond if guard is None else jnp.logical_and(cond, guard))(fn)

    def clampz(zz, b):
        return jnp.clip(zz, 0, 2) if b == "F" else jnp.clip(zz, 2, 3)

    def make(s, zz, part, key, target, src_of, dst_of):
        out = []
        for cond, b, off, rows, q in cases(s, part):
            k = sem_index((key, q))
            zc = clampz(zz, b)
            ref, base = src_of(b, zc)
            out.append((cond, pltpu.make_async_remote_copy(
                src_ref=ref.at[pl.ds(off if isinstance(base, int) else pl.multiple_of(base + off, 16), rows)],
                dst_ref=dst_of(b, zc)[0].at[pl.ds(off, rows)],
                send_sem=send.at[k], recv_sem=recv.at[k], device_id=dev(*target), device_id_type=MESH)))
        return out

    def go(guard, *a):
        for cond, cp in make(*a):
            grd(cond, guard, cp.start)
        started.append((guard, a))

    def got(guard, *a):
        for cond, cp in make(*a):
            grd(cond, guard, cp.wait_recv)

    def each(rows, off, fn):
        def body(i, _):
            fn(pl.ds(pl.multiple_of(off + 16 * i, 16), 16))
            return 0
        lax.fori_loop(0, rows // 16, body, 0)

    def total(s, guard, part, zz, dst, terms, out=None):
        for cond, b, off, rows, q in cases(s, part):
            zc = clampz(zz, b)
            def fn(b=b, off=off, rows=rows, zc=zc):
                refs = [t(b, zc)[0] for t in terms]
                def step(r):
                    v = refs[0][r, :].astype(jnp.float32)
                    for ref in refs[1:]:
                        v = v + ref[r, :].astype(jnp.float32)
                    if out is None:
                        dst(b, zc)[0][r, :] = v.astype(jnp.bfloat16)
                    else:
                        out[0 if b == "F" else 1][r, :] = v
                each(rows, off, step)
            grd(cond, guard, fn)

    C, R, A, B, U, V = (cF, cD), (rF, rD), (aF, aD), (bF, bD), (uF, uD), (vF, vD)
    cols = ((x, y), (1 - x, y), (x, 1 - y), (1 - x, 1 - y))
    tags = [(7, z - 3, z >= 3), (6, z + 3, z <= 0), (5, z - 2, z >= 2), (4, z + 2, z <= 1),
            (3, z - 1, z >= 1), (2, z + 1, z <= 2), (0, z, None)]

    def own_rows(s):
        return lambda b, zc: (FG, FROWS * s) if b == "F" else (DG, 16 * d_unit(s))
    on = lambda pair, col=None: (lambda b, zc: (land(pair, zc, b, col), 0))

    for tag, zz, guard in tags:
        for col in (3, 1, 2, 0):
            s = index(zz, *cols[col], 1 - c)
            go(guard, s, zz, "all", ("c", tag, col), CP, own_rows(s), on(C, col))

    order = [(tg, col) for tg in tags for col in (3, 1, 2, 0)]

    def load(k, what):
        (tag, zz, guard), col = order[k]
        s = index(zz, *cols[col], c)
        e = d_unit(s)
        for cond, b, off, rows, q in cases(s, "all"):
            src = FG.at[pl.ds(pl.multiple_of(FROWS * s + off, 16), rows)] if b == "F" else DG.at[pl.ds(pl.multiple_of(16 * e + off, 16), rows)]
            dst = (tF if b == "F" else tD).at[k % 2, pl.ds(off, rows)]
            cp = pltpu.make_async_copy(src, dst, loc.at[k % 2, q])
            grd(cond, guard, cp.start if what == "start" else cp.wait)

    def join(k):
        if k + 1 < len(order):
            load(k + 1, "start")
        load(k, "wait")
        (tag, zz, guard), col = order[k]
        s = index(zz, *cols[col], c)
        got(guard, s, zz, "all", ("c", tag, col), CP, own_rows(s), on(C, col))
        mine = lambda b, zc: ((tF if b == "F" else tD).at[k % 2], 0)
        total(s, guard, "all", zz, on(C, col), [on(C, col), mine])

    def first(i):
        tag, zz, guard = tags[i]
        join(4 * i)
        s = index(zz, *cols[3], c)
        go(guard, s, zz, "a", ("xa", tag), XP, on(C, 3), on(R, 1))
        go(guard, s, zz, "b", ("yb", tag), YP, on(C, 3), on(R, 0))
        for k in (1, 2, 3):
            join(4 * i + k)

    def second(i):
        tag, zz, guard = tags[i]
        sx, sy = index(zz, *cols[1], c), index(zz, *cols[2], c)
        got(guard, sx, zz, "b", ("yb", tag), YP, on(C, 3), on(R, 0))
        total(sx, guard, "b", zz, on(C, 1), [on(C, 1), on(R, 0)])
        go(guard, sx, zz, "all", ("X", tag), XP, on(C, 1), on(A))
        got(guard, sy, zz, "a", ("xa", tag), XP, on(C, 3), on(R, 1))
        total(sy, guard, "a", zz, on(C, 2), [on(C, 2), on(R, 1)])
        go(guard, sy, zz, "all", ("Y", tag), YP, on(C, 2), on(B))

    def third(i):
        tag, zz, guard = tags[i]
        s = index(zz, *cols[0], c)
        got(guard, s, zz, "all", ("X", tag), XP, on(C, 1), on(A))
        got(guard, s, zz, "all", ("Y", tag), YP, on(C, 2), on(B))
        t = {7: 3, 6: 3, 5: 2, 4: 2, 3: 1, 2: 1, 0: 0}[tag]
        base = [on(C, 0), on(A), on(B)]
        if t == 0:
            for cond, frm, pair, key in ((z < 3, UP, U, ("zd", 1)), (z > 0, DN, V, ("zu", 1))):
                got(cond, s, zz, "all", key, frm, on(C, 0), on(pair))
            inner = jnp.logical_and(z > 0, z < 3)
            total(s, inner, "all", zz, None, base + [on(U), on(V)], out=(fo, do))
            total(s, z == 0, "all", zz, None, base + [on(U)], out=(fo, do))
            total(s, z == 3, "all", zz, None, base + [on(V)], out=(fo, do))
            return
        down = tag in (7, 5, 3)
        to, frm, pair, name = (DN, UP, U, "zd") if down else (UP, DN, V, "zu")
        more = (z < 3) if down else (z > 0)
        if t < 3:
            got(jnp.logical_and(guard, more), s, zz, "all", (name, t + 1), frm, on(C, 0), on(pair))
            total(s, jnp.logical_and(guard, more), "all", zz, on(C, 0), base + [on(pair)])
            total(s, jnp.logical_and(guard, jnp.logical_not(more)), "all", zz, on(C, 0), base)
        else:
            total(s, guard, "all", zz, on(C, 0), base)
        go(guard, s, zz, "all", (name, t), to, on(C, 0), on(pair))

    @pl.when(me >= NF)
    def _(): fo[...] = jnp.zeros_like(fo)
    do[pl.ds(48, 16), :] = jnp.zeros((16, 7000), jnp.float32)
    @pl.when(me < NF)
    def _(): do[pl.ds(0, 48), :] = jnp.zeros((48, 7000), jnp.float32)
    load(0, "start")
    n = len(tags)
    for i in range(n + 2):
        if i < n:
            first(i)
        if 1 <= i <= n:
            second(i - 1)
        if i >= 2:
            third(i - 2)
    edge = lambda k, src, dst, to: pltpu.make_async_remote_copy(
        src_ref=src, dst_ref=dst, send_sem=hsend.at[k], recv_sem=hrecv.at[k], device_id=to, device_id_type=MESH)
    edges = [(jnp.logical_and(me >= 1, me < NF), me < NF - 1, edge(0, fo.at[pl.ds(0, 32)], nf, before)),
             (me == NF, me == NF - 1, edge(2, do.at[pl.ds(0, 16)], pd, before))]
    inner = jnp.logical_and(me >= NF, me < 31)
    edges += [(jnp.logical_and(inner, four(me)), jnp.logical_and(me > NF, four(me - 1)), edge(1, do.at[pl.ds(48, 16)], pd, after)),
              (jnp.logical_and(inner, jnp.logical_not(four(me))), jnp.logical_and(me > NF, jnp.logical_not(four(me - 1))),
               edge(1, do.at[pl.ds(32, 16)], pd, after))]
    for out, _, cp in edges:
        pl.when(out)(cp.start)
    for guard, a in started:
        for cond, cp in make(*a):
            grd(cond, guard, cp.wait_send)
    for out, into, cp in edges:
        pl.when(out)(cp.wait_send)
        pl.when(into)(cp.wait_recv)

def reduce(FG, DG, cid=2):
    B16 = jnp.bfloat16
    V = pltpu.VMEM
    pair = lambda *lead: [V(lead + (3, FROWS, 800), B16), V(lead + (2, DROWS, 7000), B16)]
    return pl.pallas_call(
        reduce_kernel,
        out_shape=(jax.ShapeDtypeStruct((FROWS, 800), jnp.float32), jax.ShapeDtypeStruct((DROWS, 7000), jnp.float32),
                   jax.ShapeDtypeStruct((32, 800), jnp.float32), jax.ShapeDtypeStruct((16, 7000), jnp.float32)),
        in_specs=[pl.BlockSpec(memory_space=pl.ANY)] * 2,
        out_specs=[pl.BlockSpec(memory_space=V)] * 4,
        scratch_shapes=[V((2, FROWS, 800), B16), V((2, DROWS, 7000), B16), *pair(4), *pair(2), *pair(), *pair(), *pair(), *pair(),
                        pltpu.SemaphoreType.DMA((192,)), pltpu.SemaphoreType.DMA((192,)), pltpu.SemaphoreType.DMA((2, 2)),
                        pltpu.SemaphoreType.DMA((3,)), pltpu.SemaphoreType.DMA((3,))],
        compiler_params=pltpu.CompilerParams(collective_id=cid, has_side_effects=True, vmem_limit_bytes=60 * 2**20),
        name="sum_gradients",
    )(FG, DG)

def flatten(fo, do, nf, pd):
    me = lax.axis_index("wide") * 4 + lax.axis_index("narrow")
    ff, nextf, edge = fo.reshape(-1), nf.reshape(-1)[:20800], pd.reshape(-1)
    a = lax.dynamic_slice(jnp.concatenate([ff, nextf]), (1152 * jnp.minimum(me, 16),), (SHARD,))
    b = jnp.concatenate([ff[19584:381000], edge[:36536]])
    off = 112000 - (112000 * d_unit(me) + FLATF - SHARD * me)
    c = lax.dynamic_slice(jnp.concatenate([edge, do.reshape(-1)]), (jnp.clip(off, 0, 560000 - SHARD),), (SHARD,))
    return jnp.where(me < 17, a, jnp.where(me == 17, b, c))


def allsum(arrays):
    return lax.psum(arrays, ("wide", "narrow"))


def norm_forward(values, gain, shift, total):
    sums, squares = allsum([jnp.sum(values, axis=1), jnp.sum(values * values, axis=1)])
    centre = sums / total
    inverse = lax.rsqrt(squares / total - centre * centre + EPSILON_NORM)
    normed = (values - centre[:, None]) * inverse[:, None]
    affine = gain.astype(F32)[:, None] * normed + shift.astype(F32)[:, None]
    return (normed, inverse, affine), jax.nn.silu(affine).astype(BF16)


def norm_backward(g, kept, gain, total):
    normed, inverse, affine = kept
    sigma = jax.nn.sigmoid(affine)
    p = g * sigma * (1.0 + affine * (1.0 - sigma))
    shift_part = jnp.sum(p, axis=1)
    gain_part = jnp.sum(p * normed, axis=1)
    shift_all, gain_all = allsum([shift_part, gain_part])
    d = (gain.astype(F32) * inverse)[:, None] * (p - (shift_all / total)[:, None] - normed * (gain_all / total)[:, None])
    return d.astype(BF16), gain_part, shift_part


def rows_of(params):
    flat = lax.all_gather(params, ("wide", "narrow"), axis=0, tiled=True)
    F = flat[:FROWS * NF * H].reshape(FROWS * NF, H)
    D = flat[FLATF:]
    D = jnp.pad(D, (0, max(0, HX * G - D.shape[0])))[:HX * G].reshape(HX, G)
    return F, D


def scatter_rows(FG, DG, length):
    flat = jnp.concatenate([FG.astype(F32).reshape(-1)[:FLATF], DG.astype(F32).reshape(-1)])
    flat = jnp.pad(flat, (0, max(0, length - flat.shape[0])))[:length]
    return lax.psum_scatter(flat, ("wide", "narrow"), scatter_dimension=0, tiled=True)


def unpack_rows(F):
    tail = jnp.concatenate([F[8004:8908, 200:], F[8005:8909, :200]], axis=1)
    return [None, F[7000], F[7001], F[7002:7802], F[7802], F[7803], F[7804:8004].reshape(H, 2 * L), F[8004, :200],
            tail[:100], tail[100], tail[101], tail[102:902], tail[902], tail[903]]


def pack_rows(g):
    g = [a.astype(BF16) for a in g]
    row = lambda a: a.reshape(1, -1)
    tail = jnp.concatenate([g[7], row(g[8]), row(g[9]), g[10], row(g[11]), row(g[12])])
    bent = jnp.concatenate([jnp.concatenate([row(g[6]), tail[:, 600:]]), jnp.pad(tail[:, :600], ((0, 1), (0, 0)))], axis=1)
    return jnp.concatenate([row(g[0]), row(g[1]), g[2], row(g[3]), row(g[4]), g[5].reshape(200, 800), bent,
                            jnp.zeros((FROWS * NF - 8909, 800), BF16)])


def one_hot(labels):
    return (labels[None, :] == jnp.arange(NC, dtype=jnp.int32)[:, None]).astype(BF16)


def fast_step(expression, epsilon, params, panels, labels):
    total = float(expression.shape[0] * 32)
    x = expression.T
    hot = one_hot(labels)
    F, D, lin1 = spread_and_first(*slots(params), x)
    eps = jnp.pad(epsilon.T, ((0, LP - L), (0, 0)))
    w2, wh, wd1, wd2, grows, act1, act2, act3, ends, heads, latent, lin2, lin3, lin4, stat, table = hidden_layers(
        total, lin1, F, hot, eps)
    counts = table[:NC, LP - 1]
    cond_sums = table[:NC, :L]
    offset = cond_sums / counts[:, None] - jnp.sum(cond_sums, axis=0) / total
    mask_total = jnp.sum(counts * jnp.sum(panels.astype(F32), axis=1))
    rebuilt, direct, DG, g4, squares = output_layer(D, ends, x, panels.astype(BF16), hot, 2.0 / mask_total)
    d1, tail, sums2 = hidden_backward(
        total, g4, lin4, w2, wh, wd1, wd2, grows, stat, latent, heads, hot, eps, table, squares,
        (act1, act2, act3), (lin1, lin2, lin3))
    FG, grad_cells = last_layer(x, F, d1, direct, FROWS * NF)
    FG = lax.dynamic_update_slice(FG, tail[:FROWS * NF - G], (G, 0))
    grad_params = flatten(*reduce(FG, DG, 4))
    divergence = -0.5 * table[NC, 0] / total
    loss = sums2[NC, 0] / mask_total + KL_WEIGHT * divergence
    columns = L // 4
    mine = lax.dynamic_slice(offset, (0, lax.axis_index("narrow") * columns), (NC, columns))
    return rebuilt.T, mine, loss, grad_cells.T, grad_params, divergence


def general_step(expression, epsilon, params, panels, labels):
    total = expression.shape[0] * lax.axis_size("wide") * lax.axis_size("narrow")
    x = expression.T
    noise = epsilon.T.astype(F32)
    F, D = rows_of(params)
    w = unpack_rows(F)
    hot = one_hot(labels)
    panel_sizes = jnp.sum(panels.astype(F32), axis=1)
    kept1, act1 = norm_forward(first_linear(F, x), w[1], w[2], total)
    kept2, act2 = norm_forward(mm(w[3], act1, TN), w[4], w[5], total)
    heads = (mm(w[6], act2, TN) + w[7].astype(F32)[:, None]).astype(BF16)
    mu, logvar = heads[:L].astype(F32), heads[L:].astype(F32)
    deviation = jnp.exp(0.5 * logvar)
    cond_sums, counts, kl = allsum([
        mm(hot, heads[:L], NT), jnp.sum(hot.astype(F32), axis=1),
        jnp.sum(1.0 + logvar - mu * mu - jnp.exp(logvar)).reshape(1)])
    offset = cond_sums / counts[:, None] - jnp.sum(cond_sums, axis=0) / total
    hotf = hot.astype(F32)
    choose = lambda table: sum(table[i][:, None] * hotf[i][None, :] for i in range(NC))
    latent = (mu + deviation * noise - choose(offset)).astype(BF16)
    kept3, act3 = norm_forward(mm(w[8], latent, TN), w[9], w[10], total)
    kept4, act4 = norm_forward(mm(w[11], act3, TN), w[12], w[13], total)
    mask_total = jnp.sum(counts * panel_sizes)
    ends = jnp.concatenate([act4, jnp.ones((1, act4.shape[1]), BF16), jnp.zeros((HX - H - 1, act4.shape[1]), BF16)])
    rebuilt, direct, DG, g4, squares = output_layer(D, ends, x, panels.astype(BF16), hot, 2.0 / mask_total)
    squared_part = jnp.sum(squares)
    d4, gain4, shift4 = norm_backward(g4[:H], kept4, w[12], total)
    grad_wd2 = mm(act3, d4, NT)
    d3, gain3, shift3 = norm_backward(mm(w[11], d4, NN), kept3, w[9], total)
    grad_wd1 = mm(latent, d3, NT)
    d_latent = mm(w[8], d3, NN).astype(BF16)
    cond_grad, squared = allsum([mm(hot, d_latent, NT), squared_part.reshape(1)])
    dl = d_latent.astype(F32)
    total_grad = jnp.sum(cond_grad, axis=0)
    d_mu = dl - choose(cond_grad / counts[:, None]) + (total_grad / total)[:, None] + KL_WEIGHT * mu / total
    d_logvar = 0.5 * dl * deviation * noise + KL_WEIGHT * 0.5 * (jnp.exp(logvar) - 1.0) / total
    d_heads = jnp.concatenate([d_mu, d_logvar]).astype(BF16)
    grad_bh = jnp.sum(d_heads.astype(F32), axis=1)
    grad_wh = mm(act2, d_heads, NT)
    d2, gain2, shift2 = norm_backward(mm(w[6], d_heads, NN), kept2, w[4], total)
    grad_w2 = mm(act1, d2, NT)
    d1, gain1, shift1 = norm_backward(mm(w[3], d2, NN), kept1, w[1], total)
    FG, grad_cells = last_layer(x, F, d1, direct, FROWS * NF)
    tail = pack_rows([gain1, shift1, grad_w2, gain2, shift2, grad_wh, grad_bh, grad_wd1, gain3, shift3, grad_wd2, gain4, shift4])
    FG = lax.dynamic_update_slice(FG, tail, (G, 0))
    grad_params = scatter_rows(FG, DG, params.shape[0] * lax.axis_size("wide") * lax.axis_size("narrow"))
    divergence = -0.5 * kl[0] / total
    loss = squared[0] / mask_total + KL_WEIGHT * divergence
    columns = L // lax.axis_size("narrow")
    mine = lax.dynamic_slice(offset, (0, lax.axis_index("narrow") * columns), (NC, columns))
    return rebuilt.T, mine, loss, grad_cells.T, grad_params, divergence


def solution(mesh):
    cells = P(("wide", "narrow"), None)
    flat = P(("wide", "narrow"))
    step = fast_step if dict(mesh.shape) == {"wide": 8, "narrow": 4} else general_step
    return jax.shard_map(step, mesh=mesh, in_specs=(cells, cells, flat, P(), flat),
                         out_specs=(cells, P(None, "narrow"), P(), cells, flat, P()), check_vma=False)
```

```python
import functools

import jax
import jax.numpy as jnp
from jax import lax
from jax.experimental import pallas as pl
from jax.experimental.pallas import tpu as pltpu
from jax.sharding import PartitionSpec as P

G, H, L, NC = 7000, 800, 100, 4
EPSILON_NORM = 1e-05
KL_WEIGHT = 5e-05
F32, BF16 = jnp.float32, jnp.bfloat16
TN = ((0,), (0,))
NN = ((1,), (0,))
NT = ((1,), (1,))
HX = 816


def mm(left, right, dims):
    return lax.dot_general(left, right, (dims, ((), ())), preferred_element_type=F32)


def params_of(limit=56):
    return pltpu.CompilerParams(dimension_semantics=("arbitrary",), vmem_limit_bytes=limit * 2**20)


def output_kernel(part, block, scale, d_ref, a_ref, x_ref, p_ref, h_ref, reb, direct, dg, g_ref, sq, dscr):
    i = pl.program_id(0)
    cells = a_ref.shape[1]

    @pl.when(i == 0)
    def _():
        g_ref[...] = jnp.zeros_like(g_ref)
        sq[...] = jnp.zeros_like(sq)

    lim = G - i * block
    for j in range(block // part):
        r = slice(j * part, (j + 1) * part)
        inside = lax.broadcasted_iota(jnp.int32, (part, 1), 0) + j * part < lim
        w = d_ref[:, r]
        out = mm(w, a_ref[...], TN)
        mask = jnp.where(inside, mm(p_ref[:, r], h_ref[...], TN), 0.0)
        t = jnp.exp(-jnp.abs(out))
        one = 1.0 + t
        soft = jnp.maximum(out, 0.0) + jnp.where(t < 1e-3, t - 0.5 * t * t, jnp.log(one))
        reb[r, :] = soft.astype(BF16)
        res = jnp.where(mask > 0.0, soft - x_ref[r, :].astype(F32), 0.0)
        sq[...] += jnp.sum((res * res).reshape(part // 8, 8, cells), axis=0)
        dr = scale[0] * res
        direct[r, :] = dr.astype(BF16)
        d = (dr * (jnp.where(out >= 0.0, 1.0, t) / one)).astype(BF16)
        lane = lax.broadcasted_iota(jnp.int32, (1, part), 1) + j * part < lim
        dscr[r, :] = d
    lane = lax.broadcasted_iota(jnp.int32, (1, block), 1) < lim
    dg[...] = mm(a_ref[...], dscr[...], NT).astype(BF16)
    g_ref[...] += mm(jnp.where(lane, d_ref[...], jnp.zeros((), BF16)), dscr[...], NN)


def output_layer(D, act, x, panels, hot, scale, block=1024, part=256):
    cells = x.shape[1]
    n = pl.cdiv(G, block)
    rows = lambda: pl.BlockSpec((block, cells), lambda i: (i, 0))
    whole = lambda r, c: pl.BlockSpec((r, c), lambda i: (0, 0))
    return pl.pallas_call(
        functools.partial(output_kernel, part, block),
        grid=(n,),
        out_shape=(jax.ShapeDtypeStruct((G, cells), BF16), jax.ShapeDtypeStruct((G, cells), BF16),
                   jax.ShapeDtypeStruct((HX, G), BF16), jax.ShapeDtypeStruct((HX, cells), F32),
                   jax.ShapeDtypeStruct((8, cells), F32)),
        in_specs=[pl.BlockSpec(memory_space=pltpu.SMEM), pl.BlockSpec((HX, block), lambda i: (0, i)), whole(HX, cells),
                  rows(), pl.BlockSpec((NC, block), lambda i: (0, i)), whole(NC, cells)],
        out_specs=[rows(), rows(), pl.BlockSpec((HX, block), lambda i: (0, i)), whole(HX, cells), whole(8, cells)],
        scratch_shapes=[pltpu.VMEM((block, cells), BF16)],
        compiler_params=params_of(),
        cost_estimate=pl.CostEstimate(flops=6 * G * H * cells, bytes_accessed=70_000_000, transcendentals=3 * G * cells),
        name="output_layer",
    )(scale.reshape(1), D, act, x, panels, hot)


def first_rows_kernel(block, w_ref, x_ref, o_ref):
    i = pl.program_id(0)

    @pl.when(i == 0)
    def _():
        o_ref[...] = jnp.zeros_like(o_ref)

    inside = lax.broadcasted_iota(jnp.int32, (block, 1), 0) < G - i * block
    zero = jnp.zeros((), BF16)

    @pl.when((i + 1) * block <= G)
    def _():
        o_ref[...] += mm(w_ref[...], x_ref[...], TN)

    @pl.when((i + 1) * block > G)
    def _():
        o_ref[...] += mm(jnp.where(inside, w_ref[...], zero), jnp.where(inside, x_ref[...], zero), TN)


def first_linear(F, x, block=1024):
    cells = x.shape[1]
    return pl.pallas_call(
        functools.partial(first_rows_kernel, block),
        grid=(pl.cdiv(G, block),),
        out_shape=jax.ShapeDtypeStruct((H, cells), F32),
        in_specs=[pl.BlockSpec((block, H), lambda i: (i, 0)), pl.BlockSpec((block, cells), lambda i: (i, 0))],
        out_specs=pl.BlockSpec((H, cells), lambda i: (0, 0)),
        compiler_params=params_of(),
        cost_estimate=pl.CostEstimate(flops=2 * G * H * cells, bytes_accessed=30_000_000, transcendentals=0),
        name="first_linear",
    )(F, x)


def last_kernel(x_ref, w_ref, d_ref, t_ref, fg, gc):
    fg[...] = mm(x_ref[...], d_ref[...], NT).astype(BF16)
    gc[...] = (mm(w_ref[...], d_ref[...], NN) - t_ref[...].astype(F32)).astype(BF16)


def last_layer(x, F, d1, direct, frows, block=512):
    cells = x.shape[1]
    rows = lambda c: pl.BlockSpec((block, c), lambda i: (i, 0))
    return pl.pallas_call(
        last_kernel,
        grid=(pl.cdiv(G, block),),
        out_shape=(jax.ShapeDtypeStruct((frows, H), BF16), jax.ShapeDtypeStruct((G, cells), BF16)),
        in_specs=[rows(cells), rows(H), pl.BlockSpec((H, cells), lambda i: (0, 0)), rows(cells)],
        out_specs=[rows(H), rows(cells)],
        compiler_params=params_of(),
        cost_estimate=pl.CostEstimate(flops=4 * G * H * cells, bytes_accessed=70_000_000, transcendentals=0),
        name="last_layer",
    )(x, F, d1, direct)


MESH = pl.DeviceIdType.MESH
FROWS, DROWS = 496, 64
NF = 18
SHARD = 397952
FLATF = 7126600
ALL = (0, 1, 2)


def d_unit(s):
    v = lax.shift_right_arithmetic(908 * (s - 19) + 1252, 8)
    return jnp.where(s <= NF, 0, v)


def place():
    w, n = lax.axis_index("wide"), lax.axis_index("narrow")
    return w // 2, w % 2, n // 2, n % 2


def dev(z, x, y, c):
    return (z * 2 + x, y * 2 + c)


def index(z, x, y, c):
    return (z * 2 + x) * 4 + y * 2 + c


def grd(cond, guard, fn):
    pl.when(cond if guard is None else jnp.logical_and(cond, guard))(fn)


def four(s):
    return lax.bitwise_and(lax.shift_right_arithmetic(0x355b, jnp.clip(s - NF, 0, 13)), 1) == 1


def greet(z, x, y, c, extra=()):
    bar = pltpu.get_barrier_semaphore()
    sig = lambda d: pl.semaphore_signal(bar, inc=1, device_id=d, device_id_type=MESH)
    for d in extra:
        sig(d)
    sig(dev(z, 1 - x, y, c))
    sig(dev(z, x, 1 - y, c))
    sig(dev(z, x, y, 1 - c))

    @pl.when(z > 0)
    def _():
        sig(dev(z - 1, x, y, c))

    @pl.when(z < 3)
    def _():
        sig(dev(z + 1, x, y, c))
    pl.semaphore_wait(bar, len(extra) + 3 + (z > 0).astype(jnp.int32) + (z < 3).astype(jnp.int32))


class Spread:
    VIA = {"F": (None, (0b0111, 0b0111), (0b0010, 0b0101), (0b0000, 0b0001)),
           "D": (None, (0b1100, 0b1100), (0b1000, 0b1100), (0b1000, 0b0000))}

    def __init__(self, kind, own, buf, send, recv, base=0):
        self.kind, self.own, self.buf, self.send, self.recv = kind, own, buf, send, recv
        self.place = z, x, y, c = place()
        self.sems, self.base, self.started = {}, base, []
        self.XP, self.YP, self.CP = (z, 1 - x, y, c), (z, x, 1 - y, c), (z, x, y, 1 - c)
        self.UP, self.DN = (z + 1, x, y, c), (z - 1, x, y, c)
        self.tags = {0: (0, z, None)}
        for t in (1, 2, 3):
            self.tags[2 * t] = (2 * t, z - t, z >= t)
            self.tags[2 * t + 1] = (2 * t + 1, z + t, z + t <= 3)

    def pieces(self, s, p):
        if self.kind == "F":
            return [] if p == 2 else [(s < NF, FROWS * s, (0, 240)[p], (240, 256)[p])]
        return [(None, 16 * d_unit(s), (0, 32, 48)[p], (32, 16, 16)[p])]

    def rows(self, s, p):
        for cond, base, off, n in self.pieces(s, p):
            yield cond, self.buf.at[pl.ds(pl.multiple_of(base + off, 16), n)], self.own.at[pl.ds(off, n)]

    def copy(self, s, p, key, target, local=False):
        k = self.base + self.sems.setdefault((key, p), len(self.sems))
        (_, dst, own), = self.rows(s, p)
        return pltpu.make_async_remote_copy(src_ref=own if local else dst, dst_ref=dst, send_sem=self.send.at[k],
                                            recv_sem=self.recv.at[k], device_id=dev(*target), device_id_type=MESH)

    def where(self, s, guard, fn):
        def last():
            fn((2,))

        def both():
            fn((0, 1))
            if self.kind == "D":
                pl.when(four(s))(last)
        grd(s < NF if self.kind == "F" else s >= NF, guard, both)

    def sends(self, s, guard, legs, local=False):
        def start(what, ps):
            for p in ps:
                for parts, key, target, more in legs:
                    if p in parts:
                        fn = getattr(self.copy(s, p, key, target, local), what)
                        fn() if more is None else pl.when(more)(fn)
        self.started.append((s, guard, functools.partial(start, "wait_send")))
        return functools.partial(start, "start")

    def gets(self, s, parts, key, target, more=None):
        def wait(ps):
            for p in ps:
                if p in parts:
                    fn = self.copy(s, p, key, target).wait_recv
                    fn() if more is None else pl.when(more)(fn)
        return wait

    def begin(self, loc, planes=True, names="ud"):
        z, x, y, c = self.place
        me = index(*self.place)
        fs = [self.sends(me, None, [(ALL, (name, 1), *((self.UP, z < 3) if name == "u" else (self.DN, z > 0)))], True) for name in names]
        fs += [self.planes(0, True)] if planes else []
        self.where(me, None, lambda ps: [f(ps) for f in fs])

        def start(what, ps):
            for p in ps:
                (_, dst, own), = self.rows(me, p)
                getattr(pltpu.make_async_copy(own, dst, loc.at[p]), what)()
        self.kept = lambda: self.where(me, None, functools.partial(start, "wait"))
        self.where(me, None, functools.partial(start, "start"))

    def own_in_place(self):
        self.kept()

    def planes(self, tag, local=False):
        _, zz, guard = self.tags[tag]
        z, x, y, c = self.place
        s = index(zz, x, y, c)
        return self.sends(s, guard, [(ALL, ("x", tag), self.XP, None), (ALL, ("y", tag), self.YP, None),
                                     (ALL, ("c0", tag), self.CP, None)], local)

    def along_z(self, t):
        z, x, y, c = self.place
        for name in "ud":
            tag = 2 * t + (name == "d")
            _, zz, ok = self.tags[tag]
            frm, to, more = (self.DN, self.UP, z < 3) if name == "u" else (self.UP, self.DN, z > 0)
            s = index(zz, x, y, c)
            fs = [self.sends(s, ok, [(ALL, (name, t + 1), to, more)])] if t < 3 else []
            fs.append(self.planes(tag))
            get = self.gets(s, ALL, (name, t), frm)

            def fn(ps):
                for p in ps:
                    get((p,))
                    for f in fs:
                        f((p,))
            self.where(s, ok, fn)

    def by_z(self, t, zz):
        first, others = self.VIA[self.kind][t]
        has = lambda planes: lax.bitwise_and(lax.shift_right_arithmetic(planes, jnp.clip(zz, 0, 3)), 1) == 1
        return has(first), has(others)

    def flat_parts(self, tag):
        _, zz, guard = self.tags[tag]
        if tag == 0:
            return guard, guard
        first, others = self.by_z(tag // 2, zz)
        return jnp.logical_and(guard, jnp.logical_not(others)), jnp.logical_and(guard, jnp.logical_not(first))

    def cross(self, tag):
        _, zz, guard = self.tags[tag]
        z, x, y, c = self.place
        second, half = self.flat_parts(tag)
        for s, name, frm, parts, leg, cond, core in (
                (index(zz, 1 - x, y, c), "x", self.XP, (1, 2), ("xy", tag, self.YP), second, "c1"),
                (index(zz, x, 1 - y, c), "y", self.YP, (0,), ("yx", tag, self.XP), half, "c2")):
            get = self.gets(s, ALL, (name, tag), frm)
            send = self.sends(s, guard, [(parts, leg[:2], leg[2], cond), (ALL, (core, tag), self.CP, None)])

            def fn(ps):
                get(ps)
                send(ps)
            self.where(s, guard, fn)

    def diag(self, tag):
        _, zz, guard = self.tags[tag]
        z, x, y, c = self.place
        sd = index(zz, 1 - x, 1 - y, c)
        second, half = self.flat_parts(tag)
        t, name = tag // 2, "ud"[tag % 2]
        both = lambda a, b: b if a is None else jnp.logical_and(a, b)
        gets, legs = [], []
        if tag:
            frm = self.DN if name == "u" else self.UP
            first, others = self.by_z(t, zz)
            gets = [self.gets(sd, (0,), ("g" + name, t), frm, both(guard, first)),
                    self.gets(sd, (1, 2), ("g" + name, t), frm, both(guard, others))]
        for name in ("ud"[tag % 2] if tag else "ud") if t < 3 else "":
            to, more = (self.UP, z < 3) if name == "u" else (self.DN, z > 0)
            first, others = self.by_z(t + 1, zz)
            legs += [((0,), ("g" + name, t + 1), to, both(first, more)), ((1, 2), ("g" + name, t + 1), to, both(others, more))]
        gets += [self.gets(sd, (1, 2), ("xy", tag), self.YP, second), self.gets(sd, (0,), ("yx", tag), self.XP, half)]
        send = self.sends(sd, guard, legs + [(ALL, ("c3", tag), self.CP, None)])

        def fn(ps):
            for get in gets:
                get(ps)
            send(ps)
        self.where(sd, guard, fn)

    def core(self, tag, i):
        _, zz, guard = self.tags[tag]
        z, x, y, c = self.place
        xx, yy = ((x, y), (1 - x, y), (x, 1 - y), (1 - x, 1 - y))[i]
        s = index(zz, xx, yy, 1 - c)
        self.where(s, guard, self.gets(s, ALL, ("c%d" % i, tag), self.CP))

    def end(self):
        for s, guard, fn in self.started:
            self.where(s, guard, fn)


def first_kernel(fs, x_hbm, ds, F, D, lin, fv, xv, send, recv, loc, fsem, xsem, dsend, drecv, dloc):
    z, x, y, c = place()
    xcopy = pltpu.make_async_copy(x_hbm, xv, xsem)
    xcopy.start()
    net = Spread("F", fs, fv, send, recv)
    late = Spread("D", ds, D, dsend, drecv)
    greet(z, x, y, c)
    net.begin(loc)
    late.begin(dloc)
    lin[...] = jnp.zeros_like(lin)
    out = []

    def store(s, k, guard):
        r = pl.ds(pl.multiple_of(FROWS * s, 16), FROWS)
        cp = pltpu.make_async_copy(fv.at[r], F.at[r], fsem.at[k])
        grd(s < NF, guard, cp.start)
        out.append((s < NF, guard, cp))

    def times(tag, i):
        _, zz, guard = net.tags[tag]
        xx, yy = ((x, y), (1 - x, y), (x, 1 - y), (1 - x, 1 - y))[i]
        m = (zz * 2 + xx) * 2 + yy

        def whole():
            r = pl.ds(pl.multiple_of(2 * FROWS * m, 16), 2 * FROWS)
            lin[...] += mm(fv[r, :], xv[r, :], TN)

        def rest():
            r = pl.ds(14 * FROWS, G - 14 * FROWS)
            lin[...] += mm(fv[r, :], xv[r, :], TN)
        grd(m < 7, guard, whole)
        grd(m == 7, guard, rest)
        k = 8 * tag + 2 * i
        store(2 * m, k, guard)
        store(2 * m + 1, k + 1, guard)

    def finish(tag, cols):
        for i in cols:
            net.core(tag, i)
            times(tag, i)

    def both(name, *tags):
        for n in (net, late):
            for tag in tags:
                getattr(n, name)(tag)

    def settle(tag, cols):
        for i in cols:
            late.core(tag, i)

    both("along_z", 1)
    both("cross", 0)
    both("along_z", 2)
    both("diag", 0)
    both("cross", 2, 3)
    net.own_in_place()
    late.own_in_place()
    xcopy.wait()
    finish(0, (0, 1, 2, 3))
    both("along_z", 3)
    both("diag", 2, 3)
    both("cross", 4, 5)
    finish(2, (0, 1, 2))
    finish(3, (0, 1, 2))
    both("diag", 4, 5)
    both("cross", 6, 7)
    finish(2, (3,))
    finish(3, (3,))
    finish(4, (0, 1, 2))
    finish(5, (0, 1, 2))
    both("diag", 6, 7)
    for tag in (4, 5):
        finish(tag, (3,))
    for tag in (6, 7):
        finish(tag, (0, 1, 2, 3))
    for tag in (0, 2, 3, 4, 5, 6, 7):
        settle(tag, (0, 1, 2, 3))
    net.end()
    late.end()
    for cond, guard, cp in out:
        grd(cond, guard, cp.wait)


def spread_and_first(fslot, dslot, x, cid=1):
    cells = x.shape[1]
    V = pltpu.VMEM
    return pl.pallas_call(
        first_kernel,
        out_shape=(jax.ShapeDtypeStruct((FROWS * NF, H), BF16), jax.ShapeDtypeStruct((HX, G), BF16), jax.ShapeDtypeStruct((H, cells), F32)),
        in_specs=[pl.BlockSpec(memory_space=pl.ANY)] * 3,
        out_specs=[pl.BlockSpec(memory_space=pl.ANY)] * 2 + [pl.BlockSpec(memory_space=V)],
        scratch_shapes=[V((FROWS * NF, H), BF16), V((G, cells), BF16), pltpu.SemaphoreType.DMA((144,)), pltpu.SemaphoreType.DMA((144,)),
                        pltpu.SemaphoreType.DMA((3,)), pltpu.SemaphoreType.DMA((64,)), pltpu.SemaphoreType.DMA,
                        pltpu.SemaphoreType.DMA((208,)), pltpu.SemaphoreType.DMA((208,)), pltpu.SemaphoreType.DMA((3,))],
        compiler_params=pltpu.CompilerParams(collective_id=cid, has_side_effects=True, vmem_limit_bytes=58 * 2**20),
        name="spread_and_first",
    )(fslot, x, dslot)


def slots(p):
    n = 32
    me = lax.axis_index("wide") * 4 + lax.axis_index("narrow")
    ax = ("wide", "narrow")
    head = lax.ppermute(p[-36864:], ax, [(i, i + 1) for i in range(n - 1)])
    tail = lax.ppermute(p[:112000], ax, [(i + 1, i) for i in range(n - 1)])
    ext = jnp.concatenate([head, p, tail, jnp.zeros((112000,), p.dtype)])
    f = lax.dynamic_slice(ext, (jnp.maximum(36864 - 1152 * me, 0),), (FROWS * 800,)).reshape(FROWS, 800)
    off = 36864 + FLATF + 112000 * d_unit(me) - SHARD * me
    d = lax.dynamic_slice(ext, (jnp.clip(off, 0, ext.shape[0] - DROWS * 7000),), (DROWS * 7000,)).reshape(DROWS, 7000)
    return f, d

LP = 128
STEP, UNROLL = 32, 5


def rows_loop(n, fn, step=STEP, unroll=UNROLL):
    def body(i, _):
        for j in range(unroll):
            fn(pl.ds(pl.multiple_of((i * unroll + j) * step, step), step))
        return 0
    lax.fori_loop(0, n // (step * unroll), body, 0)


def silu(u):
    return u * (0.5 + 0.5 * jnp.tanh(0.5 * u))


def by_lanes(v):
    return sum(v[:, 128 * i:128 * i + 128] for i in range(v.shape[1] // 128))


def over_rows(buf):
    return jnp.sum(jnp.transpose(buf), axis=0, keepdims=True)


def along_rows(row):
    return jnp.transpose(jnp.broadcast_to(row, (128, 896)))


def wide(col, cells):
    return jnp.concatenate([col] * (cells // 128), axis=1)


class Sums:
    def __init__(self, bufs, sems):
        self.bufs, self.sems, self.turn = bufs, sems, 0
        self.place = z, x, y, c = place()
        self.spot = x * 4 + y * 2 + c
        self.inside = [(k, lax.bitwise_xor(self.spot, k)) for k in range(1, 8)]
        self.planes = [(k, lax.bitwise_xor(z, k)) for k in range(1, 4)]

    def near_dev(self, q):
        return dev(self.place[0], q // 4, (q // 2) % 2, q % 2)

    def far_dev(self, q):
        return dev(q, *self.place[1:])

    def others(self):
        return [self.near_dev(q) for k, q in self.inside] + [self.far_dev(q) for k, q in self.planes]

    def __call__(self, kind, value, between=None, after=None):
        near, far = self.bufs[kind]
        i, t = self.turn, self.sems
        self.turn += 1
        j = self.count[kind] = self.count.get(kind, -1) + 1 if hasattr(self, "count") else self.first(kind)
        s, f = near.at[j], far.at[j]
        s[self.spot] = value
        cps = [pltpu.make_async_remote_copy(src_ref=s.at[self.spot], dst_ref=s.at[self.spot], send_sem=t[0].at[i, k], recv_sem=t[1].at[i, k],
                                            device_id=self.near_dev(q), device_id_type=MESH) for k, q in self.inside]
        for cp in cps:
            cp.start()
        if between:
            between()
        for cp in cps:
            cp.wait_recv()
        z = self.place[0]
        f[z] = jnp.sum(s[...], axis=0)
        cpz = [pltpu.make_async_remote_copy(src_ref=f.at[z], dst_ref=f.at[z], send_sem=t[2].at[i, k], recv_sem=t[3].at[i, k],
                                            device_id=self.far_dev(q), device_id_type=MESH) for k, q in self.planes]
        for cp in cpz:
            cp.start()
        for cp in cps:
            cp.wait_send()
        if after:
            after()
        for cp in cpz:
            cp.wait()
        return jnp.sum(f[...], axis=0)

    def first(self, kind):
        self.count = {}
        return 0


def sums_scratch(stats, tables):
    V = pltpu.VMEM
    n = stats + tables
    dma = pltpu.SemaphoreType.DMA
    return [V((stats, 8, 2, 896), F32), V((stats, 4, 2, 896), F32), V((max(tables, 1), 8, 8, 128), F32), V((max(tables, 1), 4, 8, 128), F32),
            dma((n, 8)), dma((n, 8)), dma((n, 4)), dma((n, 4))]


def turned(v, places):
    lane = lax.broadcasted_iota(jnp.int32, v.shape, 1)
    return sum(jnp.where(jnp.logical_and(lane >= to, lane < to + stop - start), pltpu.roll(v, (to - start) % 896, 1), 0.0)
               for start, stop, to in places)


def padded(v):
    return jnp.concatenate([v, jnp.zeros((v.shape[0], 896 - v.shape[1]), F32)], axis=1)


def forward_kernel(total, lin1, F, hot, eps, w2, wh, wd1, wd2, grows,
                   act1o, act2o, act3o, ends, heads, latent, lin2o, lin3o, lin4, stat, table,
                   packed, msem, rows, tail, whm, whl, bh, act1, act2, act3, lin2, lin3, osem, bufs, square, n1, f1, n2, f2, a1, a2, a3, a4):
    z, x, y, c = place()
    sums = Sums({"stat": (n1, f1), "table": (n2, f2)}, (a1, a2, a3, a4))
    cells = lin1.shape[1]
    brings = pltpu.make_async_copy(F.at[pl.ds(6992, 1920)], packed, msem)
    brings.start()
    for i in range(2):
        bufs[i, pl.ds(H, 96), :] = jnp.zeros((96, 128), F32)
    square[...] = jnp.zeros_like(square)
    greet_all(sums.others())

    def stats(lin):
        def one(r):
            v = lin[r, :]
            bufs[0, r, :] = by_lanes(v)
            bufs[1, r, :] = by_lanes(v * v)
        rows_loop(H, one)
        return jnp.concatenate([over_rows(bufs[0]), over_rows(bufs[1])])

    def norm(k, lin, out, between=None, after=None):
        t = sums("stat", stats(lin), between, after)
        centre = t[0:1, :] / total
        inverse = lax.rsqrt(t[1:2, :] / total - centre * centre + EPSILON_NORM)
        stat[pl.ds(2 * k, 1), :] = centre
        stat[pl.ds(2 * k + 1, 1), :] = inverse
        scale = inverse * grows[2 * k:2 * k + 1, :]
        bufs[0] = along_rows(scale)
        bufs[1] = along_rows(grows[2 * k + 1:2 * k + 2, :] - centre * scale)

        def one(r):
            out[r, :] = silu(lin[r, :] * wide(bufs[0, r, :], cells) + wide(bufs[1, r, :], cells)).astype(BF16)
        rows_loop(H, one)

    def unpack():
        brings.wait()

        def widen(r):
            rows[r, :] = padded(packed[r, :].astype(F32))
        rows_loop(1920, widen, 32, 5)
        lane = lax.broadcasted_iota(jnp.int32, (904, 896), 1)
        t = jnp.where(lane < 600, pltpu.roll(rows[pl.ds(1012, 904), :], 696, 1), pltpu.roll(rows[pl.ds(1013, 904), :], 600, 1))
        tail[...] = jnp.where(lane < H, t, 0.0)
        for i, (buf, r) in enumerate(((rows, 8), (rows, 9), (rows, 810), (rows, 811), (tail, 100), (tail, 101), (tail, 902), (tail, 903))):
            grows[pl.ds(i, 1), :] = buf[pl.ds(r, 1), :]
        w2[...] = rows[pl.ds(10, H), pl.ds(0, H)].astype(BF16)
        wd2[...] = tail[pl.ds(102, H), pl.ds(0, H)].astype(BF16)
        top = lax.broadcasted_iota(jnp.int32, (LP, H), 0) < L
        wd1[...] = jnp.where(top, tail[pl.ds(0, LP), pl.ds(0, H)], 0.0).astype(BF16)
        v = rows[pl.ds(812, 200), :]
        for i in range(4):
            for k, half in enumerate((whm, whl)):
                half[pl.ds(i, 200, stride=4), :] = turned(v, ((200 * i + L * k, 200 * i + L * k + L, 0),))[:, :LP]
        wh[:, pl.ds(0, LP)] = whm[...].astype(BF16)
        wh[:, pl.ds(LP, LP)] = whl[...].astype(BF16)
        b = turned(rows[pl.ds(1012, 1), :], ((0, L, 0), (L, 2 * L, LP)))[:, :2 * LP]
        bh[...] = jnp.transpose(jnp.broadcast_to(b, (LP, 2 * LP)))

    leaving = []

    def leave(src, dst):
        cp = pltpu.make_async_copy(src, dst, osem.at[len(leaving)])
        cp.start()
        leaving.append(cp)

    norm(0, lin1, act1, unpack)
    lin2[...] = mm(w2[...], act1[...], TN)
    leave(act1, act1o)
    leave(lin2, lin2o)
    norm(1, lin2, act2)
    leave(act2, act2o)
    h = (mm(wh[...], act2[...], TN) + bh[:, 0:1]).astype(BF16)
    heads[...] = h
    mu, lv = h[:LP].astype(F32), h[LP:].astype(F32)
    part = mm(hot[...], h[:LP], NT)
    hf = hot[...].astype(F32)
    lane = lax.broadcasted_iota(jnp.int32, (NC, LP), 1)
    top = jnp.where(lane == LP - 1, jnp.sum(hf, axis=1, keepdims=True), part)
    kl = jnp.sum(jnp.sum(1.0 + lv - mu * mu - jnp.exp(lv), axis=0, keepdims=True), axis=1, keepdims=True)
    low = jnp.where(lax.broadcasted_iota(jnp.int32, (4, LP), 0) == 0, kl, 0.0)

    t = sums("table", jnp.concatenate([top, low]))
    table[...] = t
    cond = t[0:NC, :]
    counts = cond[:, LP - 1:LP]
    cond = jnp.where(lane == LP - 1, 0.0, cond)
    off = cond / counts - jnp.sum(cond, axis=0, keepdims=True) / total
    square[pl.ds(0, NC), :] = off
    offc = jnp.transpose(square[...])
    chosen = sum(offc[:, i:i + 1] * hf[i:i + 1, :] for i in range(NC))
    lat = (mu + jnp.exp(0.5 * lv) * eps[...].astype(F32) - chosen).astype(BF16)
    latent[...] = lat
    lin3[...] = mm(wd1[...], latent[...], TN)
    leave(lin3, lin3o)
    norm(2, lin3, act3)
    leave(act3, act3o)
    lin4[...] = mm(wd2[...], act3[...], TN)

    norm(3, lin4, ends)
    ends[pl.ds(H, 16), :] = jnp.where(lax.broadcasted_iota(jnp.int32, (16, ends.shape[1]), 0) == 0, 1.0, 0.0).astype(BF16)
    for cp in leaving:
        cp.wait()


def greet_all(devices):
    bar = pltpu.get_barrier_semaphore()
    for d in devices:
        pl.semaphore_signal(bar, inc=1, device_id=d, device_id_type=MESH)
    pl.semaphore_wait(bar, len(devices))


def hidden_layers(total, lin1, F, hot, eps, cid=2):
    cells = lin1.shape[1]
    V = pltpu.VMEM
    vm = pl.BlockSpec(memory_space=V)
    hbm = pl.BlockSpec(memory_space=pl.ANY)
    S = jax.ShapeDtypeStruct
    return pl.pallas_call(
        functools.partial(forward_kernel, total),
        out_shape=(S((H, H), BF16), S((H, 2 * LP), BF16), S((LP, H), BF16), S((H, H), BF16), S((8, 896), F32),
                   S((H, cells), BF16), S((H, cells), BF16), S((H, cells), BF16), S((HX, cells), BF16), S((2 * LP, cells), BF16),
                   S((LP, cells), BF16), S((H, cells), F32), S((H, cells), F32), S((H, cells), F32), S((8, 896), F32),
                   S((8, LP), F32)),
        in_specs=[vm, hbm, vm, vm],
        out_specs=[vm] * 5 + [hbm] * 3 + [vm] * 3 + [hbm] * 2 + [vm] * 3,
        scratch_shapes=[V((1920, H), BF16), pltpu.SemaphoreType.DMA, V((1920, 896), F32), V((904, 896), F32), V((H, LP), F32), V((H, LP), F32),
                        V((2 * LP, LP), F32), *[V((H, cells), BF16)] * 3, *[V((H, cells), F32)] * 2, pltpu.SemaphoreType.DMA((8,)), V((2, 896, 128), F32), V((LP, LP), F32), *sums_scratch(4, 1)],
        compiler_params=pltpu.CompilerParams(collective_id=cid, has_side_effects=True, vmem_limit_bytes=58 * 2**20),
        name="hidden_layers",
    )(lin1, F, hot, eps)


def backward_kernel(total, g4, lin4, w2, wh, wd1, wd2, grows, stat, latent, heads, hot, eps, table, squares, act1i, act2i, act3i, lin1i, lin2i, lin3i,
                    d1, tail, sums2,
                    gnorm, rows, upper, lower, gwh, gwl, act1, act2, act3, lin1, lin2, lin3, isem, pbuf, dbuf, hbuf, bufs, part, square, n1, f1, n2, f2, a1, a2, a3, a4):
    cells = lin4.shape[1]
    sums = Sums({"stat": (n1, f1), "table": (n2, f2)}, (a1, a2, a3, a4))
    comes = {}
    for i, (name, src, dst) in enumerate((("lin3", lin3i, lin3), ("act3", act3i, act3), ("lin2", lin2i, lin2), ("act2", act2i, act2),
                                          ("lin1", lin1i, lin1), ("act1", act1i, act1))):
        comes[name] = pltpu.make_async_copy(src, dst, isem.at[i])
        comes[name].start()
    for i in range(2):
        part[i, pl.ds(H, 96), :] = jnp.zeros((96, 128), F32)
    square[...] = jnp.zeros_like(square)
    for buf in (upper, lower):
        buf[pl.ds(0, 8), :] = jnp.zeros((8, 896), F32)
        buf[pl.ds(904, 8), :] = jnp.zeros((8, 896), F32)
    rows[pl.ds(1904, 32), :] = jnp.zeros((32, 896), F32)
    greet_all(sums.others())

    def keep(r, v):
        upper[pl.ds(r + 4, v.shape[0]), pl.ds(0, H)] = v
        lower[pl.ds(r + 5, v.shape[0]), pl.ds(0, H)] = v

    def pack():
        keep(100, gnorm[5:6, pl.ds(0, H)])
        keep(101, gnorm[4:5, pl.ds(0, H)])
        keep(902, gnorm[7:8, pl.ds(0, H)])
        keep(903, gnorm[6:7, pl.ds(0, H)])

        def bend(r):
            lane = lax.broadcasted_iota(jnp.int32, (16, 896), 1)
            rows[pl.ds(pl.multiple_of(1000 + r.start, 8), 16), :] = jnp.where(
                lane < 200, pltpu.roll(lower[r, :], 296, 1), pltpu.roll(upper[r, :], 200, 1))
        rows_loop(912, bend, 16, 3)
        acc = 0.0
        for i in range(4):
            for j, half in enumerate((gwh, gwl)):
                acc = acc + turned(padded(half[pl.ds(i, 200, stride=4), :]), ((0, L, 200 * i + L * j),))
        rows[pl.ds(804, 200), :] = acc
        rows[pl.ds(802, 1), :] = gnorm[3:4, :]
        rows[pl.ds(803, 1), :] = gnorm[2:3, :]

    def norm(k, g, lin, out, between=None):
        centre, inverse = stat[2 * k:2 * k + 1, :], stat[2 * k + 1:2 * k + 2, :]
        gain, shift = grows[2 * k:2 * k + 1, :], grows[2 * k + 1:2 * k + 2, :]
        bufs[0] = along_rows(inverse)
        bufs[1] = along_rows(-centre * inverse)
        bufs[2] = along_rows(gain)
        bufs[3] = along_rows(shift)

        def one(r):
            n = lin[r, :] * wide(bufs[0, r, :], cells) + wide(bufs[1, r, :], cells)
            u = n * wide(bufs[2, r, :], cells) + wide(bufs[3, r, :], cells)
            s = 0.5 + 0.5 * jnp.tanh(0.5 * u)
            p = g[r, :] * s * (1.0 + u * (1.0 - s))
            pbuf[r, :] = p
            part[0, r, :] = by_lanes(p)
            part[1, r, :] = by_lanes(p * n)
        rows_loop(H, one)
        local = jnp.concatenate([over_rows(part[0]), over_rows(part[1])])
        gnorm[pl.ds(2 * k, 2), :] = local
        t = sums("stat", local, between)
        a = gain * inverse
        b = -a * t[1:2, :] / total
        bufs[0] = along_rows(a)
        bufs[1] = along_rows(b * inverse)
        bufs[2] = along_rows(-b * centre * inverse - a * t[0:1, :] / total)

        def two(r):
            out[r, :] = (pbuf[r, :] * wide(bufs[0, r, :], cells) + lin[r, :] * wide(bufs[1, r, :], cells)
                         + wide(bufs[2, r, :], cells)).astype(BF16)
        rows_loop(H, two)

    norm(3, g4, lin4, dbuf)
    pbuf[...] = mm(wd2[...], dbuf[...], NN)
    comes["lin3"].wait()
    comes["act3"].wait()

    def grads4():
        keep(102, mm(act3[...], dbuf[...], NT))
    norm(2, pbuf, lin3, hbuf, grads4)
    dl = mm(wd1[...], hbuf[...], NN).astype(BF16)
    cond = mm(hot[...], dl, NT)
    sq = jnp.sum(jnp.sum(squares[...], axis=0, keepdims=True), axis=1, keepdims=True)
    low = jnp.where(lax.broadcasted_iota(jnp.int32, (4, LP), 0) == 0, sq, 0.0)

    def grads3():
        keep(0, mm(latent[...], hbuf[...], NT)[:L])
    t = sums("table", jnp.concatenate([cond, low]), grads3)
    sums2[...] = t
    cond = t[0:NC, :]
    counts = table[0:NC, LP - 1:LP]
    square[pl.ds(0, NC), :] = jnp.sum(cond, axis=0, keepdims=True) / total - cond / counts
    take = jnp.transpose(square[...])
    hf = hot[...].astype(F32)
    change = sum(take[:, i:i + 1] * hf[i:i + 1, :] for i in range(NC))
    mu, lv = heads[pl.ds(0, LP), :].astype(F32), heads[pl.ds(LP, LP), :].astype(F32)
    dl = dl.astype(F32)
    dh = jnp.concatenate([
        dl + change + (KL_WEIGHT / total) * mu,
        0.5 * dl * jnp.exp(0.5 * lv) * eps[...].astype(F32) + (0.5 * KL_WEIGHT / total) * (jnp.exp(lv) - 1.0)]).astype(BF16)
    dbuf[pl.ds(0, 2 * LP), :] = dh
    bias = padded(mm(jnp.ones((8, cells), BF16), dh, NT))
    lower[pl.ds(4, 1), :] = turned(bias, ((0, L, 600), (LP, LP + L, 700)))[0:1]
    pbuf[...] = mm(wh[...], dh, NN)
    comes["lin2"].wait()
    comes["act2"].wait()

    def grads2():
        g = mm(act2[...], dbuf[pl.ds(0, 2 * LP), :], NT)
        gwh[...] = g[:, :LP]
        gwl[...] = g[:, LP:]
    norm(1, pbuf, lin2, hbuf, grads2)
    pbuf[...] = mm(w2[...], hbuf[...], NN)
    comes["lin1"].wait()
    comes["act1"].wait()

    def grads1():
        rows[pl.ds(2, H), pl.ds(0, H)] = mm(act1[...], hbuf[...], NT)
        pack()
    norm(0, pbuf, lin1, d1, grads1)
    rows[pl.ds(0, 1), :] = gnorm[1:2, :]
    rows[pl.ds(1, 1), :] = gnorm[0:1, :]

    def out(r):
        tail[r, :] = rows[r, pl.ds(0, H)].astype(BF16)
    rows_loop(1920, out, 16, 5)
    tail[pl.ds(1920, 16), :] = jnp.zeros((16, H), BF16)


def hidden_backward(total, g4, lin4, w2, wh, wd1, wd2, grows, stat, latent, heads, hot, eps, table, squares, acts, lins, cid=3):
    cells = lin4.shape[1]
    V = pltpu.VMEM
    vm = pl.BlockSpec(memory_space=V)
    hbm = pl.BlockSpec(memory_space=pl.ANY)
    S = jax.ShapeDtypeStruct
    return pl.pallas_call(
        functools.partial(backward_kernel, total),
        out_shape=(S((H, cells), BF16), S((1936, H), BF16), S((8, LP), F32)),
        in_specs=[vm] * 14 + [hbm] * 6,
        out_specs=[vm] * 3,
        scratch_shapes=[V((8, 896), F32), V((1936, 896), F32), V((912, 896), F32), V((912, 896), F32), V((H, LP), F32), V((H, LP), F32), *[V((H, cells), BF16)] * 3, *[V((H, cells), F32)] * 3, pltpu.SemaphoreType.DMA((6,)),
                        V((H, cells), F32), V((H, cells), BF16), V((H, cells), BF16),
                        V((4, 896, 128), F32), V((2, 896, 128), F32), V((LP, LP), F32), *sums_scratch(4, 1)],
        compiler_params=pltpu.CompilerParams(collective_id=cid, has_side_effects=True, vmem_limit_bytes=58 * 2**20),
        name="hidden_backward",
    )(g4, lin4, w2, wh, wd1, wd2, grows, stat, latent, heads, hot, eps, table, squares, *acts, *lins)


ZF, ZD = (0, 1, 2), (2, 3)

def reduce_kernel(FG, DG, fo, do, nf, pd, tF, tD, cF, cD, rF, rD, gF, gD, hF, hD, aF, aD, bF, bD, uF, uD, vF, vD, send, recv, loc, hsend, hrecv):
    z, x, y, c = place()
    XP, YP, CP = (z, 1 - x, y, c), (z, x, 1 - y, c), (z, x, y, 1 - c)
    UP, DN = (z + 1, x, y, c), (z - 1, x, y, c)
    me = index(z, x, y, c)
    numbered = lambda i: (lax.shift_right_arithmetic(i, 2), lax.bitwise_and(i, 3))
    before, after = numbered(jnp.maximum(me - 1, 0)), numbered(jnp.minimum(me + 1, 31))
    nf[...] = jnp.zeros_like(nf)
    pd[...] = jnp.zeros_like(pd)
    bar = pltpu.get_barrier_semaphore()
    sig = lambda d: pl.semaphore_signal(bar, inc=1, device_id=d, device_id_type=MESH)
    for d in (XP, YP, CP):
        sig(dev(*d))
    for cond, d in ((z > 0, dev(*DN)), (z < 3, dev(*UP)), (me > 0, before), (me < 31, after)):
        pl.when(cond)(functools.partial(sig, d))
    one = lambda cond: cond.astype(jnp.int32)
    pl.semaphore_wait(bar, 3 + one(z > 0) + one(z < 3) + one(me > 0) + one(me < 31))

    sems = {}
    def sem_index(key):
        return sems.setdefault(key, len(sems))
    started = []

    def cases(s, part):
        last = jnp.logical_and(s >= NF, four(s))
        f, d = s < NF, s >= NF
        if part == "all":
            return [(f, "F", 0, 496, 0), (d, "D", 0, 48, 0), (last, "D", 48, 16, 1)]
        if part == "a":
            return [(f, "F", 0, 240, 0), (d, "D", 0, 32, 0)]
        return [(f, "F", 240, 256, 0), (d, "D", 32, 16, 0), (last, "D", 48, 16, 1)]

    def land(pair, zz, b, col=None):
        buf = pair[0 if b == "F" else 1]
        zi = zz if b == "F" else zz - 2
        return buf.at[zi] if col is None else buf.at[col, zi]

    def grd(cond, guard, fn):
        pl.when(cond if guard is None else jnp.logical_and(cond, guard))(fn)

    def clampz(zz, b):
        return jnp.clip(zz, 0, 2) if b == "F" else jnp.clip(zz, 2, 3)

    def make(s, zz, part, key, target, src_of, dst_of):
        out = []
        for cond, b, off, rows, q in cases(s, part):
            k = sem_index((key, q))
            zc = clampz(zz, b)
            ref, base = src_of(b, zc)
            out.append((cond, pltpu.make_async_remote_copy(
                src_ref=ref.at[pl.ds(off if isinstance(base, int) else pl.multiple_of(base + off, 16), rows)],
                dst_ref=dst_of(b, zc)[0].at[pl.ds(off, rows)],
                send_sem=send.at[k], recv_sem=recv.at[k], device_id=dev(*target), device_id_type=MESH)))
        return out

    def go(guard, *a):
        for cond, cp in make(*a):
            grd(cond, guard, cp.start)
        started.append((guard, a))

    def got(guard, *a):
        for cond, cp in make(*a):
            grd(cond, guard, cp.wait_recv)

    def each(rows, off, step, fn):
        def body(i, _):
            fn(pl.ds(pl.multiple_of(off + step * i, 16), step))
            return 0
        lax.fori_loop(0, rows // step, body, 0)
        if rows % step:
            fn(pl.ds(off + rows - rows % step, rows % step))

    def total(s, guard, part, zz, dst, terms, out=None):
        for cond, b, off, rows, q in cases(s, part):
            zc = clampz(zz, b)
            def fn(b=b, off=off, rows=rows, zc=zc):
                refs = [t(b, zc)[0] for t in terms]
                def step(r):
                    v = refs[0][r, :].astype(jnp.float32)
                    for ref in refs[1:]:
                        v = v + ref[r, :].astype(jnp.float32)
                    if out is None:
                        dst(b, zc)[0][r, :] = v.astype(jnp.bfloat16)
                    else:
                        out[0 if b == "F" else 1][r, :] = v
                each(rows, off, 80 if b == "F" else 16, step)
            grd(cond, guard, fn)

    C, R, GU, GD, A, B, U, V = (cF, cD), (rF, rD), (gF, gD), (hF, hD), (aF, aD), (bF, bD), (uF, uD), (vF, vD)
    cols = ((x, y), (1 - x, y), (x, 1 - y), (1 - x, 1 - y))
    tags = [(7, z - 3, z >= 3), (6, z + 3, z <= 0), (5, z - 2, z >= 2), (4, z + 2, z <= 1),
            (3, z - 1, z >= 1), (2, z + 1, z <= 2), (0, z, None)]

    def own_rows(s):
        return lambda b, zc: (FG, FROWS * s) if b == "F" else (DG, 16 * d_unit(s))
    on = lambda pair, col=None: (lambda b, zc: (land(pair, zc, b, col), 0))

    for tag, zz, guard in tags:
        for col in (3, 1, 2, 0):
            s = index(zz, *cols[col], 1 - c)
            go(guard, s, zz, "all", ("c", tag, col), CP, own_rows(s), on(C, col))

    order = [(tg, col) for tg in tags for col in (3, 1, 2, 0)]

    def load(k, what):
        (tag, zz, guard), col = order[k]
        s = index(zz, *cols[col], c)
        e = d_unit(s)
        for cond, b, off, rows, q in cases(s, "all"):
            src = FG.at[pl.ds(pl.multiple_of(FROWS * s + off, 16), rows)] if b == "F" else DG.at[pl.ds(pl.multiple_of(16 * e + off, 16), rows)]
            dst = (tF if b == "F" else tD).at[k % 2, pl.ds(off, rows)]
            cp = pltpu.make_async_copy(src, dst, loc.at[k % 2, q])
            grd(cond, guard, cp.start if what == "start" else cp.wait)

    def join(k):
        if k + 1 < len(order):
            load(k + 1, "start")
        load(k, "wait")
        (tag, zz, guard), col = order[k]
        s = index(zz, *cols[col], c)
        got(guard, s, zz, "all", ("c", tag, col), CP, own_rows(s), on(C, col))
        mine = lambda b, zc: ((tF if b == "F" else tD).at[k % 2], 0)
        total(s, guard, "all", zz, on(C, col), [on(C, col), mine])

    distance = {7: 3, 6: 3, 5: 2, 4: 2, 3: 1, 2: 1, 0: 0}
    also = lambda guard, cond: cond if guard is None else jnp.logical_and(guard, cond)

    def by_z(s, t, zz):
        has = lambda planes: lax.bitwise_and(lax.shift_right_arithmetic(planes, jnp.clip(zz, 0, 3)), 1) == 1
        return [jnp.where(s < NF, has(f).astype(jnp.int32), has(d).astype(jnp.int32)) == 1
                for f, d in zip(Spread.VIA["F"][t], Spread.VIA["D"][t])]

    def flat(s, t, zz, guard):
        return [also(guard, jnp.logical_not(v)) for v in by_z(s, t, zz)] if t else [guard, guard]

    def first(i):
        tag, zz, guard = tags[i]
        t, down = distance[tag], tag in (7, 5, 3)
        join(4 * i)
        s = index(zz, *cols[3], c)
        sides = [(UP, GU, "hd", z < 3)] if down or t == 0 else []
        sides += [(DN, GD, "hu", z > 0)] if not down or t == 0 else []
        for frm, pair, name, more in sides if t < 3 else []:
            for part, v in zip("ab", by_z(s, t + 1, zz)):
                g = also(guard, jnp.logical_and(more, v))
                got(g, s, zz, part, (name, t + 1, part), frm, on(C, 3), on(pair))
                total(s, g, part, zz, on(C, 3), [on(C, 3), on(pair)])
        if t:
            to, pair, name = (DN, GU, "hd") if down else (UP, GD, "hu")
            for part, v in zip("ab", by_z(s, t, zz)):
                go(also(guard, v), s, zz, part, (name, t, part), to, on(C, 3), on(pair))
        near_a, near_b = flat(s, t, zz, guard)
        go(near_a, s, zz, "a", ("xa", tag), XP, on(C, 3), on(R))
        go(near_b, s, zz, "b", ("yb", tag), YP, on(C, 3), on(R))
        for k in (1, 2, 3):
            join(4 * i + k)

    def second(i):
        tag, zz, guard = tags[i]
        t = distance[tag]
        sx, sy = index(zz, *cols[1], c), index(zz, *cols[2], c)
        near = flat(sx, t, zz, guard)[1]
        got(near, sx, zz, "b", ("yb", tag), YP, on(C, 3), on(R))
        total(sx, near, "b", zz, on(C, 1), [on(C, 1), on(R)])
        go(guard, sx, zz, "all", ("X", tag), XP, on(C, 1), on(A))
        near = flat(sy, t, zz, guard)[0]
        got(near, sy, zz, "a", ("xa", tag), XP, on(C, 3), on(R))
        total(sy, near, "a", zz, on(C, 2), [on(C, 2), on(R)])
        go(guard, sy, zz, "all", ("Y", tag), YP, on(C, 2), on(B))

    def third(i):
        tag, zz, guard = tags[i]
        s = index(zz, *cols[0], c)
        got(guard, s, zz, "all", ("X", tag), XP, on(C, 1), on(A))
        got(guard, s, zz, "all", ("Y", tag), YP, on(C, 2), on(B))
        t = distance[tag]
        base = [on(C, 0), on(A), on(B)]
        if t == 0:
            for cond, frm, pair, key in ((z < 3, UP, U, ("zd", 1)), (z > 0, DN, V, ("zu", 1))):
                got(cond, s, zz, "all", key, frm, on(C, 0), on(pair))
            inner = jnp.logical_and(z > 0, z < 3)
            total(s, inner, "all", zz, None, base + [on(U), on(V)], out=(fo, do))
            total(s, z == 0, "all", zz, None, base + [on(U)], out=(fo, do))
            total(s, z == 3, "all", zz, None, base + [on(V)], out=(fo, do))
            return
        down = tag in (7, 5, 3)
        to, frm, pair, name = (DN, UP, U, "zd") if down else (UP, DN, V, "zu")
        more = (z < 3) if down else (z > 0)
        if t < 3:
            got(jnp.logical_and(guard, more), s, zz, "all", (name, t + 1), frm, on(C, 0), on(pair))
            total(s, jnp.logical_and(guard, more), "all", zz, on(C, 0), base + [on(pair)])
            total(s, jnp.logical_and(guard, jnp.logical_not(more)), "all", zz, on(C, 0), base)
        else:
            total(s, guard, "all", zz, on(C, 0), base)
        go(guard, s, zz, "all", (name, t), to, on(C, 0), on(pair))

    @pl.when(me >= NF)
    def _(): fo[...] = jnp.zeros_like(fo)
    do[pl.ds(48, 16), :] = jnp.zeros((16, 7000), jnp.float32)
    @pl.when(me < NF)
    def _(): do[pl.ds(0, 48), :] = jnp.zeros((48, 7000), jnp.float32)
    load(0, "start")
    n = len(tags)
    for i in range(n + 2):
        if i < n:
            first(i)
        if 1 <= i <= n:
            second(i - 1)
        if i >= 2:
            third(i - 2)
    edge = lambda k, src, dst, to: pltpu.make_async_remote_copy(
        src_ref=src, dst_ref=dst, send_sem=hsend.at[k], recv_sem=hrecv.at[k], device_id=to, device_id_type=MESH)
    edges = [(jnp.logical_and(me >= 1, me < NF), me < NF - 1, edge(0, fo.at[pl.ds(0, 32)], nf, before)),
             (me == NF, me == NF - 1, edge(2, do.at[pl.ds(0, 16)], pd, before))]
    inner = jnp.logical_and(me >= NF, me < 31)
    edges += [(jnp.logical_and(inner, four(me)), jnp.logical_and(me > NF, four(me - 1)), edge(1, do.at[pl.ds(48, 16)], pd, after)),
              (jnp.logical_and(inner, jnp.logical_not(four(me))), jnp.logical_and(me > NF, jnp.logical_not(four(me - 1))),
               edge(1, do.at[pl.ds(32, 16)], pd, after))]
    for out, _, cp in edges:
        pl.when(out)(cp.start)
    for guard, a in started:
        for cond, cp in make(*a):
            grd(cond, guard, cp.wait_send)
    for out, into, cp in edges:
        pl.when(out)(cp.wait_send)
        pl.when(into)(cp.wait_recv)

def reduce(FG, DG, cid=2):
    B16 = jnp.bfloat16
    V = pltpu.VMEM
    pair = lambda *lead: [V(lead + (3, FROWS, 800), B16), V(lead + (2, DROWS, 7000), B16)]
    return pl.pallas_call(
        reduce_kernel,
        out_shape=(jax.ShapeDtypeStruct((FROWS, 800), jnp.float32), jax.ShapeDtypeStruct((DROWS, 7000), jnp.float32),
                   jax.ShapeDtypeStruct((32, 800), jnp.float32), jax.ShapeDtypeStruct((16, 7000), jnp.float32)),
        in_specs=[pl.BlockSpec(memory_space=pl.ANY)] * 2,
        out_specs=[pl.BlockSpec(memory_space=V)] * 4,
        scratch_shapes=[V((2, FROWS, 800), B16), V((2, DROWS, 7000), B16), *pair(4), *[b for _ in range(7) for b in pair()],
                        pltpu.SemaphoreType.DMA((192,)), pltpu.SemaphoreType.DMA((192,)), pltpu.SemaphoreType.DMA((2, 2)),
                        pltpu.SemaphoreType.DMA((3,)), pltpu.SemaphoreType.DMA((3,))],
        compiler_params=pltpu.CompilerParams(collective_id=cid, has_side_effects=True, vmem_limit_bytes=60 * 2**20),
        name="sum_gradients",
    )(FG, DG)

def flatten(fo, do, nf, pd):
    me = lax.axis_index("wide") * 4 + lax.axis_index("narrow")
    ff, nextf, edge = fo.reshape(-1), nf.reshape(-1)[:20800], pd.reshape(-1)
    a = lax.dynamic_slice(jnp.concatenate([ff, nextf]), (1152 * jnp.minimum(me, 16),), (SHARD,))
    b = jnp.concatenate([ff[19584:381000], edge[:36536]])
    off = 112000 - (112000 * d_unit(me) + FLATF - SHARD * me)
    c = lax.dynamic_slice(jnp.concatenate([edge, do.reshape(-1)]), (jnp.clip(off, 0, 560000 - SHARD),), (SHARD,))
    return jnp.where(me < 17, a, jnp.where(me == 17, b, c))


def allsum(arrays):
    return lax.psum(arrays, ("wide", "narrow"))


def norm_forward(values, gain, shift, total):
    sums, squares = allsum([jnp.sum(values, axis=1), jnp.sum(values * values, axis=1)])
    centre = sums / total
    inverse = lax.rsqrt(squares / total - centre * centre + EPSILON_NORM)
    normed = (values - centre[:, None]) * inverse[:, None]
    affine = gain.astype(F32)[:, None] * normed + shift.astype(F32)[:, None]
    return (normed, inverse, affine), jax.nn.silu(affine).astype(BF16)


def norm_backward(g, kept, gain, total):
    normed, inverse, affine = kept
    sigma = jax.nn.sigmoid(affine)
    p = g * sigma * (1.0 + affine * (1.0 - sigma))
    shift_part = jnp.sum(p, axis=1)
    gain_part = jnp.sum(p * normed, axis=1)
    shift_all, gain_all = allsum([shift_part, gain_part])
    d = (gain.astype(F32) * inverse)[:, None] * (p - (shift_all / total)[:, None] - normed * (gain_all / total)[:, None])
    return d.astype(BF16), gain_part, shift_part


def rows_of(params):
    flat = lax.all_gather(params, ("wide", "narrow"), axis=0, tiled=True)
    F = flat[:FROWS * NF * H].reshape(FROWS * NF, H)
    D = flat[FLATF:]
    D = jnp.pad(D, (0, max(0, HX * G - D.shape[0])))[:HX * G].reshape(HX, G)
    return F, D


def scatter_rows(FG, DG, length):
    flat = jnp.concatenate([FG.astype(F32).reshape(-1)[:FLATF], DG.astype(F32).reshape(-1)])
    flat = jnp.pad(flat, (0, max(0, length - flat.shape[0])))[:length]
    return lax.psum_scatter(flat, ("wide", "narrow"), scatter_dimension=0, tiled=True)


def unpack_rows(F):
    tail = jnp.concatenate([F[8004:8908, 200:], F[8005:8909, :200]], axis=1)
    return [None, F[7000], F[7001], F[7002:7802], F[7802], F[7803], F[7804:8004].reshape(H, 2 * L), F[8004, :200],
            tail[:100], tail[100], tail[101], tail[102:902], tail[902], tail[903]]


def pack_rows(g):
    g = [a.astype(BF16) for a in g]
    row = lambda a: a.reshape(1, -1)
    tail = jnp.concatenate([g[7], row(g[8]), row(g[9]), g[10], row(g[11]), row(g[12])])
    bent = jnp.concatenate([jnp.concatenate([row(g[6]), tail[:, 600:]]), jnp.pad(tail[:, :600], ((0, 1), (0, 0)))], axis=1)
    return jnp.concatenate([row(g[0]), row(g[1]), g[2], row(g[3]), row(g[4]), g[5].reshape(200, 800), bent,
                            jnp.zeros((FROWS * NF - 8909, 800), BF16)])


def one_hot(labels):
    return (labels[None, :] == jnp.arange(NC, dtype=jnp.int32)[:, None]).astype(BF16)


def fast_step(expression, epsilon, params, panels, labels):
    total = float(expression.shape[0] * 32)
    x = expression.T
    hot = one_hot(labels)
    F, D, lin1 = spread_and_first(*slots(params), x)
    eps = jnp.pad(epsilon.T, ((0, LP - L), (0, 0)))
    w2, wh, wd1, wd2, grows, act1, act2, act3, ends, heads, latent, lin2, lin3, lin4, stat, table = hidden_layers(
        total, lin1, F, hot, eps)
    counts = table[:NC, LP - 1]
    cond_sums = table[:NC, :L]
    offset = cond_sums / counts[:, None] - jnp.sum(cond_sums, axis=0) / total
    mask_total = jnp.sum(counts * jnp.sum(panels.astype(F32), axis=1))
    rebuilt, direct, DG, g4, squares = output_layer(D, ends, x, panels.astype(BF16), hot, 2.0 / mask_total)
    d1, tail, sums2 = hidden_backward(
        total, g4, lin4, w2, wh, wd1, wd2, grows, stat, latent, heads, hot, eps, table, squares,
        (act1, act2, act3), (lin1, lin2, lin3))
    FG, grad_cells = last_layer(x, F, d1, direct, FROWS * NF)
    FG = lax.dynamic_update_slice(FG, tail[:FROWS * NF - G], (G, 0))
    grad_params = flatten(*reduce(FG, DG, 4))
    divergence = -0.5 * table[NC, 0] / total
    loss = sums2[NC, 0] / mask_total + KL_WEIGHT * divergence
    columns = L // 4
    mine = lax.dynamic_slice(offset, (0, lax.axis_index("narrow") * columns), (NC, columns))
    return rebuilt.T, mine, loss, grad_cells.T, grad_params, divergence


def general_step(expression, epsilon, params, panels, labels):
    total = expression.shape[0] * lax.axis_size("wide") * lax.axis_size("narrow")
    x = expression.T
    noise = epsilon.T.astype(F32)
    F, D = rows_of(params)
    w = unpack_rows(F)
    hot = one_hot(labels)
    panel_sizes = jnp.sum(panels.astype(F32), axis=1)
    kept1, act1 = norm_forward(first_linear(F, x), w[1], w[2], total)
    kept2, act2 = norm_forward(mm(w[3], act1, TN), w[4], w[5], total)
    heads = (mm(w[6], act2, TN) + w[7].astype(F32)[:, None]).astype(BF16)
    mu, logvar = heads[:L].astype(F32), heads[L:].astype(F32)
    deviation = jnp.exp(0.5 * logvar)
    cond_sums, counts, kl = allsum([
        mm(hot, heads[:L], NT), jnp.sum(hot.astype(F32), axis=1),
        jnp.sum(1.0 + logvar - mu * mu - jnp.exp(logvar)).reshape(1)])
    offset = cond_sums / counts[:, None] - jnp.sum(cond_sums, axis=0) / total
    hotf = hot.astype(F32)
    choose = lambda table: sum(table[i][:, None] * hotf[i][None, :] for i in range(NC))
    latent = (mu + deviation * noise - choose(offset)).astype(BF16)
    kept3, act3 = norm_forward(mm(w[8], latent, TN), w[9], w[10], total)
    kept4, act4 = norm_forward(mm(w[11], act3, TN), w[12], w[13], total)
    mask_total = jnp.sum(counts * panel_sizes)
    ends = jnp.concatenate([act4, jnp.ones((1, act4.shape[1]), BF16), jnp.zeros((HX - H - 1, act4.shape[1]), BF16)])
    rebuilt, direct, DG, g4, squares = output_layer(D, ends, x, panels.astype(BF16), hot, 2.0 / mask_total)
    squared_part = jnp.sum(squares)
    d4, gain4, shift4 = norm_backward(g4[:H], kept4, w[12], total)
    grad_wd2 = mm(act3, d4, NT)
    d3, gain3, shift3 = norm_backward(mm(w[11], d4, NN), kept3, w[9], total)
    grad_wd1 = mm(latent, d3, NT)
    d_latent = mm(w[8], d3, NN).astype(BF16)
    cond_grad, squared = allsum([mm(hot, d_latent, NT), squared_part.reshape(1)])
    dl = d_latent.astype(F32)
    total_grad = jnp.sum(cond_grad, axis=0)
    d_mu = dl - choose(cond_grad / counts[:, None]) + (total_grad / total)[:, None] + KL_WEIGHT * mu / total
    d_logvar = 0.5 * dl * deviation * noise + KL_WEIGHT * 0.5 * (jnp.exp(logvar) - 1.0) / total
    d_heads = jnp.concatenate([d_mu, d_logvar]).astype(BF16)
    grad_bh = jnp.sum(d_heads.astype(F32), axis=1)
    grad_wh = mm(act2, d_heads, NT)
    d2, gain2, shift2 = norm_backward(mm(w[6], d_heads, NN), kept2, w[4], total)
    grad_w2 = mm(act1, d2, NT)
    d1, gain1, shift1 = norm_backward(mm(w[3], d2, NN), kept1, w[1], total)
    FG, grad_cells = last_layer(x, F, d1, direct, FROWS * NF)
    tail = pack_rows([gain1, shift1, grad_w2, gain2, shift2, grad_wh, grad_bh, grad_wd1, gain3, shift3, grad_wd2, gain4, shift4])
    FG = lax.dynamic_update_slice(FG, tail, (G, 0))
    grad_params = scatter_rows(FG, DG, params.shape[0] * lax.axis_size("wide") * lax.axis_size("narrow"))
    divergence = -0.5 * kl[0] / total
    loss = squared[0] / mask_total + KL_WEIGHT * divergence
    columns = L // lax.axis_size("narrow")
    mine = lax.dynamic_slice(offset, (0, lax.axis_index("narrow") * columns), (NC, columns))
    return rebuilt.T, mine, loss, grad_cells.T, grad_params, divergence


def solution(mesh):
    cells = P(("wide", "narrow"), None)
    flat = P(("wide", "narrow"))
    step = fast_step if dict(mesh.shape) == {"wide": 8, "narrow": 4} else general_step
    return jax.shard_map(step, mesh=mesh, in_specs=(cells, cells, flat, P(), flat),
                         out_specs=(cells, P(None, "narrow"), P(), cells, flat, P()), check_vma=False)
```
